128 devices in a mesh: dp: 32 (over y_hi, x, z), tensor: 4 (over y_lo, core).
Axes of the slice: x: 4, y: 4 (y_hi: 2, y_lo: 2; y = y_hi * 2 + y_lo), z: 4, core: 2. Of those that a mesh axis runs over, the one named last changes fastest.
Arguments:
- teacher_states: bfloat16 [32768, 5120], P('dp', 'tensor'), may hold values from -6 to 6
- teacher_gain: bfloat16 [5120], replicated, may hold values from 0.5 to 1.5
- w_query: bfloat16 [5120, 4096], P('dp', 'tensor'), may hold values from -0.078125 to 0.078125
- key_weight: bfloat16 [5120, 512], P('dp', 'tensor'), may hold values from -0.078125 to 0.078125
- value_weight: bfloat16 [5120, 512], P('dp', 'tensor'), may hold values from -0.078125 to 0.078125
- query_gain: float32 [128], replicated, may hold values from 0.5 to 12
- key_gain: float32 [128], replicated, may hold values from 0.5 to 12
- segments: int32 [1024, 32], P('dp'), may hold values from 0 to 3, as said below
- passage_counts: int32 [1024], P('dp'), may hold values from 2 to 4
- swap_order: int32 [1024, 4], P('dp'), may hold values from 0 to 3, as said below
- list_owner: int32 [1024, 1], P('dp'), may hold values from 0 to 31; in each aligned block of 32 rows (0 to 31, 32 to 63, ...) at most 2 rows name the same one
- student_rows: bfloat16 [2048, 4, 2560], P('dp'), may hold values from -6 to 6
- student_gain: bfloat16 [2560], replicated, may hold values from 0.5 to 1.5
- w_gate: bfloat16 [2560, 4864], P(None, 'tensor'), may hold values from -0.125 to 0.125
- w_up: bfloat16 [2560, 4864], P(None, 'tensor'), may hold values from -0.125 to 0.125
- w_down: bfloat16 [4864, 2560], P('tensor'), may hold values from -0.078125 to 0.078125
Outputs:
- list_loss: float32 [1024], P('dp')
- grad_gate: float32 [2560, 4864], P('dp', 'tensor')
- grad_up: float32 [2560, 4864], P('dp', 'tensor')
- grad_down: float32 [4864, 2560], P('tensor', 'dp')
The draws below stay inside these ranges and needn't reach their ends.
Inputs may be any that keep to these rules, and one draw needn't show every extreme that they name: `segments`: segment ids of each list start at 0, never fall, rise by at most one from token to token and end at passage_counts minus 1. `swap_order`: in each list the first passage_counts entries are an ordering of 0 to passage_counts minus 1 and the rest are their own positions. `list_owner`: among the 32 lists of one device no owner is named more than 2 times.
All inputs are finite; a program needn't handle non-finite values.
Results may differ from the reference program's by a relative error of at most 0.033.
Values may be sent and summed in bfloat16 or wider, within the bound.
No kernel may reach another device: no remote copies, remote signals or barrier semaphores. Data moves between devices by JAX's collectives and lax.ppermute only.
A program may use at most 128 MiB of HBM per device.

```python
import math
import jax
import jax.numpy as jnp
import numpy as np
from jax import lax

TEACHER_WIDTH = 5120
HQ = 32
KEPT_KEY_HEADS = 4
HEAD_DIMENSION = 128
DS = 2560
FFS = 4864
L = 32
MAXP = 4
LISTS_DEV = 32
CAP = 2
SLOTS = 64
TOK_DEV = 1024
LISTS = 1024
TOKENS = 32768
N_DP = 32
N_TENSOR = 4


def list_counts(key):
    key = jax.random.fold_in(key, 11)
    drawn_counts = jax.random.randint(key, (LISTS,), 2, MAXP + 1, dtype=jnp.int32)
    return drawn_counts.at[0].set(MAXP)


def draw_passage_counts(key, part):
    return list_counts(key).astype(jnp.int32)


def draw_segments(key, part):
    passages = list_counts(key)
    key = jax.random.fold_in(key, 21)
    scores = jax.random.randint(key, (LISTS, L - 1), 0, 1 << 20, dtype=jnp.int32) * L + jnp.arange(L - 1, dtype=jnp.int32)[None, :]
    ranking = jnp.argsort(jnp.argsort(scores, axis=1), axis=1)
    boundary = (ranking < passages[:, None] - 1).astype(jnp.int32)
    starting = jnp.zeros((LISTS, 1), jnp.int32)
    return jnp.concatenate([starting, jnp.cumsum(boundary, axis=1)], axis=1).astype(jnp.int32)


def draw_swap_order(key, part):
    passages = list_counts(key)
    key = jax.random.fold_in(key, 31)
    places = jnp.arange(MAXP, dtype=jnp.int32)[None, :]
    scores = jax.random.randint(key, (LISTS, MAXP), 0, 1 << 16, dtype=jnp.int32) * MAXP + places
    scores = jnp.where(places < passages[:, None], scores, (1 << 24) + places)
    return jnp.argsort(scores, axis=1).astype(jnp.int32)


def draw_query_gain(key, part):
    key = jax.random.fold_in(key, 41)
    return jnp.exp(jax.random.uniform(key, (HEAD_DIMENSION,), jnp.float32, math.log(0.5), math.log(2.0)))


def draw_key_gain(key, part):
    key = jax.random.fold_in(key, 43)
    return jnp.exp(jax.random.uniform(key, (HEAD_DIMENSION,), jnp.float32, math.log(0.5), math.log(2.0)))


def raised(result, rng, source, target, shards_of, factor):
    owner, partner = [(jnp.arange(result.shape[axis_at]) // (result.shape[axis_at] // shards_of)).reshape([-1 if axis == axis_at else 1 for axis in range(result.ndim)]) for axis_at in (source, target)]
    chosen = jax.random.permutation(rng, shards_of)[partner]
    strong = (owner == chosen) | (owner == (partner + shards_of // 2) % shards_of)
    return jnp.where(strong, factor * result, result)


def levels(own_key, shape, pieces, smallest, largest):
    def one(axis_at, blocks):
        heights = jax.random.uniform(jax.random.fold_in(jax.random.fold_in(own_key, 6), axis_at), (blocks,), jnp.float32, smallest / len(pieces), largest / len(pieces))
        return jnp.repeat(jnp.exp(heights), shape[axis_at] // blocks).reshape((-1,) + (1,) * (len(shape) - axis_at - 1))

    gain = one(*pieces[0])
    for cut in pieces[1:]:
        gain = gain * one(*cut)
    return gain


def routed_block(own_key, own, number, rows, number_of, top, most, slope):
    sequence = jax.random.permutation(own_key, number_of)
    packed, common = shares(number_of, rows * top, most, slope, True), shares(number_of, rows * top, most, slope, False)
    places = jnp.arange(number_of)

    def named(tallies, offset_by):
        used = int((tallies > 0).sum())
        fixed = max(1, used // 4)
        moved = fixed + (places - fixed + offset_by * (used - fixed)) % max(1, number_of - fixed)
        return jnp.zeros((number_of,), jnp.int32).at[sequence[jnp.where(places < fixed, places, moved)]].set(jnp.asarray(tallies, jnp.int32))

    tallies = jnp.where(number % 4 == 0, named(packed, number // 4), named(common, number - number // 4 - 1))
    mixed = jax.random.permutation(jax.random.fold_in(own, 3), number_of)
    giver, taker = mixed[0:number_of // 2 * 2:2], mixed[1:number_of // 2 * 2:2]
    margin = jnp.minimum(tallies[giver] - 1, most - tallies[taker]) // 2
    margin = jnp.where((giver == sequence[0]) | (taker == sequence[0]) | (tallies[taker] == 0), 0, jnp.maximum(margin, 0))
    moved = jax.random.randint(jax.random.fold_in(own, 4), (number_of // 2,), 0, 1 << 20) % (margin + 1)
    tallies = tallies.at[giver].add(-moved).at[taker].add(moved)
    labels = jnp.searchsorted(jnp.cumsum(tallies), jnp.arange(rows * top), side="right").astype(jnp.int32)
    table = labels.reshape(top, rows).T
    table = table[jax.random.permutation(jax.random.fold_in(own, 1), rows)]
    offset_by = jax.random.randint(jax.random.fold_in(own, 2), (rows, 1), 0, top)
    return jnp.take_along_axis(table, (jnp.arange(top)[None, :] + offset_by) % top, axis=1)


def shares(number_of, total, limit, skew, full):
    portions = [(1 << 20) // math.isqrt(rank ** skew) + 1 for rank in range(1, number_of + 1)]
    largest = limit if full else min(limit, max(-(-total // number_of), total * portions[0] // sum(portions)))
    least = 1 if total - largest >= number_of - 1 else 0
    given, rest = [largest] + [least] * (number_of - 1), total - largest - least * (number_of - 1)
    while rest > 0:
        candidates = [i for i in range(1, number_of) if given[i] < largest] or [i for i in range(1, number_of) if given[i] < limit]
        mass, budget = sum([portions[i] for i in candidates]), rest
        for i in candidates:
            addition = min(limit - given[i], max(1, budget * portions[i] // mass), rest)
            given[i] = given[i] + addition
            rest = rest - addition
    return np.array(given)


def centred(stream_key, shape, spread, bound, shards=(), held_as=jnp.bfloat16):
    array = jax.random.normal(stream_key, shape, jnp.float32) * spread
    if len(shards) > 0:
        array = levels(stream_key, shape, shards, -0.22, 0.18) * array
    return jnp.clip(array, min=-bound, max=bound).astype(held_as)


def bell_draw_with(stream_key, extent, spread, limit, shards, heavy, held_as=jnp.bfloat16):
    entries = spread * jax.random.normal(stream_key, extent, jnp.float32)
    if shards:
        entries = entries * levels(stream_key, extent, shards, -0.22, 0.18)
    return jnp.clip(raised(entries, jax.random.fold_in(stream_key, 3), *heavy), -limit, limit).astype(held_as)


def setup_inputs(seed: int = 0) -> dict:
    key_list = jax.random.split(jax.random.key(seed), 17)
    teacher_states = centred(key_list[0], (TOKENS, TEACHER_WIDTH), 1.0, 6.0, ((0, 32), (1, 4)))
    teacher_gain = jnp.clip(1.0 + 0.1 * jax.random.normal(key_list[1], (TEACHER_WIDTH,), jnp.float32), 0.5, 1.5).astype(jnp.bfloat16)
    w_query = centred(key_list[2], (TEACHER_WIDTH, HQ * HEAD_DIMENSION), TEACHER_WIDTH ** -0.5, 0.078125, ((0, 32), (1, 4)))
    key_weight = centred(key_list[3], (TEACHER_WIDTH, KEPT_KEY_HEADS * HEAD_DIMENSION), TEACHER_WIDTH ** -0.5, 0.078125, ((0, 32), (1, 4)))
    value_weight = centred(key_list[4], (TEACHER_WIDTH, KEPT_KEY_HEADS * HEAD_DIMENSION), TEACHER_WIDTH ** -0.5, 0.078125, ((0, 32), (1, 4)))
    query_gain = draw_query_gain(jax.random.fold_in(key_list[16], 71), 0)
    key_gain = draw_key_gain(jax.random.fold_in(key_list[16], 71), 0)
    segments = draw_segments(jax.random.fold_in(key_list[16], 71), 0)
    passage_counts = draw_passage_counts(jax.random.fold_in(key_list[16], 71), 0)
    swap_order = draw_swap_order(jax.random.fold_in(key_list[16], 71), 0)
    list_owner_keys = jax.random.split(jax.random.fold_in(key_list[10], 1), LISTS // LISTS_DEV)
    list_owner_turns = jax.random.permutation(jax.random.fold_in(key_list[10], 3), LISTS // LISTS_DEV)
    list_owner = jax.vmap(lambda own, number: routed_block(jax.random.fold_in(key_list[10], 2), own, number, LISTS_DEV, N_DP, 1, CAP, 2))(list_owner_keys, list_owner_turns).reshape((LISTS, 1))
    student_rows = bell_draw_with(key_list[11], (N_DP * SLOTS, MAXP, DS), 1.0, 6.0, ((0, 32),), (0, 2, 32, 2.75))
    student_gain = jnp.clip(1.0 + 0.1 * jax.random.normal(key_list[12], (DS,), jnp.float32), 0.5, 1.5).astype(jnp.bfloat16)
    w_gate = centred(key_list[13], (DS, FFS), DS ** -0.5, 0.125, ((1, 4),))
    w_up = centred(key_list[14], (DS, FFS), DS ** -0.5, 0.125, ((1, 4),))
    w_down = centred(key_list[15], (FFS, DS), FFS ** -0.5, 0.078125, ((0, 4),))
    return dict(teacher_states=teacher_states, teacher_gain=teacher_gain, w_query=w_query, key_weight=key_weight, value_weight=value_weight, query_gain=query_gain, key_gain=key_gain, segments=segments, passage_counts=passage_counts, swap_order=swap_order, list_owner=list_owner, student_rows=student_rows, student_gain=student_gain, w_gate=w_gate, w_up=w_up, w_down=w_down)


EPSILON = 1e-06
ROPE_BASE = 1000000.0

def rms_scale(values, weights):
    return values * lax.rsqrt(lax.optimization_barrier(jnp.mean(values * values, axis=-1, keepdims=True)) + EPSILON) * weights

def rotate(values, positions):
    half_width = values.shape[-1] // 2
    exponent = jnp.arange(half_width, dtype=jnp.float32) * (-2.0 / values.shape[-1])
    angles = positions.astype(jnp.float32)[:, None] * jnp.power(ROPE_BASE, exponent)[None, :]
    cosines = jnp.cos(angles)[:, None, :]
    sines = jnp.sin(angles)[:, None, :]
    leading_half = values[..., :half_width]
    second_half = values[..., half_width:]
    return jnp.concatenate([leading_half * cosines - second_half * sines, second_half * cosines + leading_half * sines], axis=-1)

def attend_and_pool(query_proj, key_proj, value_proj, query_gain, key_gain, segments):
    list_total, seq_len = segments.shape
    head_size = query_gain.shape[0]
    query_heads = query_proj.shape[1] // head_size
    key_heads = key_proj.shape[1] // head_size
    positions = jnp.arange(seq_len, dtype=jnp.int32)
    queries = rotate(rms_scale(query_proj.reshape(list_total, seq_len, query_heads, head_size), query_gain), positions).astype(jnp.bfloat16)
    keyed = rotate(rms_scale(key_proj.reshape(list_total, seq_len, key_heads, head_size), key_gain), positions).astype(jnp.bfloat16)
    valued = value_proj.reshape(list_total, seq_len, key_heads, head_size).astype(jnp.bfloat16)
    grouped = queries.reshape(list_total, seq_len, key_heads, query_heads // key_heads, head_size)
    scores = jnp.einsum('bqkgd,bskd->bkgqs', grouped.astype(jnp.float32), keyed.astype(jnp.float32)) / math.sqrt(head_size)
    causal = positions[:, None] >= positions[None, :]
    scores = jnp.where(causal, scores, -1e+30)
    shifted = jnp.exp(scores - lax.optimization_barrier(jnp.max(scores, axis=-1, keepdims=True)))
    weights = (shifted / lax.optimization_barrier(jnp.sum(shifted, axis=-1, keepdims=True))).astype(jnp.bfloat16)
    mixed = jnp.einsum('bkgqs,bskd->bqkgd', weights.astype(jnp.float32), valued.astype(jnp.float32))
    mixed = mixed.astype(jnp.bfloat16).reshape(list_total, seq_len, query_heads * head_size)
    member = segments[:, None, :] == jnp.arange(MAXP, dtype=jnp.int32)[None, :, None]
    totals = jnp.einsum('bpl,blf->bpf', member.astype(jnp.float32), mixed.astype(jnp.float32))
    tokens_in = lax.optimization_barrier(jnp.sum(member.astype(jnp.float32), axis=-1))
    return (totals / jnp.maximum(tokens_in, 1.0)[:, :, None]).astype(jnp.bfloat16)

def permute_matrix(swap_order, passage_counts):
    places = jnp.arange(swap_order.shape[1], dtype=jnp.int32)
    matched = (swap_order[:, :, None] == places[None, None, :]) & (places[None, :, None] < passage_counts[:, None, None])
    return matched.astype(jnp.float32)

def cosine_table(gram, width):
    diagonal = jnp.diagonal(gram, axis1=1, axis2=2)
    scale = jnp.sqrt(diagonal / width + EPSILON)
    return gram / (width * scale[:, :, None] * scale[:, None, :])

def list_losses(hidden, target, live_mask):
    gram = jnp.einsum('bid,bjd->bij', hidden, hidden, precision=lax.Precision.HIGHEST)
    cosine = cosine_table(gram, hidden.shape[-1])
    paired = live_mask[:, :, None] * live_mask[:, None, :]
    passages = lax.optimization_barrier(jnp.sum(live_mask, axis=-1))
    differ = cosine - target
    return lax.optimization_barrier(jnp.sum(paired * differ * differ, axis=(1, 2))) / jnp.maximum(passages, 1.0) ** 2

def student_feedforward(flat_rows, student_gain, w_gate, w_up, w_down):
    normed = rms_scale(flat_rows.astype(jnp.float32), student_gain.astype(jnp.float32)).astype(jnp.bfloat16)
    gate_pre = jnp.dot(normed, w_gate, preferred_element_type=jnp.float32)
    up_pre = jnp.dot(normed, w_up, preferred_element_type=jnp.float32)
    activated = (gate_pre * jax.nn.sigmoid(gate_pre) * up_pre).astype(jnp.bfloat16)
    block_size = w_down.shape[0] // N_TENSOR
    ffn_out = jnp.zeros((flat_rows.shape[0], w_down.shape[1]), jnp.float32)
    for block in range(N_TENSOR):
        partial_out = jnp.dot(activated[:, block * block_size:(block + 1) * block_size], w_down[block * block_size:(block + 1) * block_size], preferred_element_type=jnp.float32)
        ffn_out = ffn_out + lax.optimization_barrier(partial_out.astype(jnp.bfloat16)).astype(jnp.float32)
    hidden = flat_rows.astype(jnp.float32) + ffn_out
    return (normed, gate_pre, up_pre, activated, hidden)

def hidden_gradient(hidden, target, live_mask):

    def objective(states):
        return states.shape[-1] * jnp.sum(list_losses(states, target, live_mask))
    unused, pullback = jax.vjp(objective, hidden)
    return pullback(jnp.ones((), jnp.float32))[0]

def weight_gradients(normed, gate_pre, up_pre, activated, grad_hidden, w_down):
    contract_rows = (((0,), (0,)), ((), ()))
    grad_down = lax.dot_general(activated, grad_hidden, contract_rows, preferred_element_type=jnp.float32)
    grad_act = lax.dot_general(grad_hidden, w_down, (((1,), (1,)), ((), ())), preferred_element_type=jnp.float32)
    sigma = jax.nn.sigmoid(gate_pre)
    grad_gate_in = (grad_act * up_pre * sigma * (1.0 + gate_pre * (1.0 - sigma))).astype(jnp.bfloat16)
    grad_up_in = (grad_act * gate_pre * sigma).astype(jnp.bfloat16)
    grad_gate = lax.dot_general(normed, grad_gate_in, contract_rows, preferred_element_type=jnp.float32)
    grad_up = lax.dot_general(normed, grad_up_in, contract_rows, preferred_element_type=jnp.float32)
    return (grad_gate, grad_up, grad_down)

def reference(teacher_states, teacher_gain, w_query, key_weight, value_weight, query_gain, key_gain, segments, passage_counts, swap_order, list_owner, student_rows, student_gain, w_gate, w_up, w_down):
    blocks = teacher_states.reshape(N_DP, TOK_DEV, TEACHER_WIDTH)
    block_segments = segments.reshape(N_DP, LISTS_DEV, L)

    def one_block(paired_inputs):
        block_states, block_ids = paired_inputs
        normed = rms_scale(block_states.astype(jnp.float32), teacher_gain.astype(jnp.float32)).astype(jnp.bfloat16)
        query_proj = jnp.dot(normed, w_query, preferred_element_type=jnp.float32)
        key_proj = jnp.dot(normed, key_weight, preferred_element_type=jnp.float32)
        value_proj = jnp.dot(normed, value_weight, preferred_element_type=jnp.float32)
        return attend_and_pool(query_proj, key_proj, value_proj, query_gain, key_gain, block_ids)
    pooled_rows = lax.map(one_block, (blocks, block_segments)).reshape(LISTS, MAXP, HQ * HEAD_DIMENSION)
    placement = permute_matrix(swap_order, passage_counts)
    permuted = jnp.einsum('bip,bpf->bif', placement, pooled_rows.astype(jnp.float32), precision=lax.Precision.HIGHEST)
    teacher_gram = jnp.einsum('bif,bjf->bij', permuted, permuted, precision=lax.Precision.HIGHEST)
    target = cosine_table(teacher_gram, HQ * HEAD_DIMENSION)
    live_mask = (jnp.arange(MAXP, dtype=jnp.int32)[None, :] < passage_counts[:, None]).astype(jnp.float32)
    owner = list_owner[:, 0]
    by_block = owner.reshape(N_DP, LISTS_DEV)
    inner = jnp.arange(LISTS_DEV, dtype=jnp.int32)
    before = (by_block[:, None, :] == by_block[:, :, None]) & (inner[None, None, :] < inner[None, :, None])
    earlier = lax.optimization_barrier(jnp.sum(before.astype(jnp.int32), axis=2)).reshape(LISTS)
    source = jnp.arange(LISTS, dtype=jnp.int32) // LISTS_DEV
    slot_id = (owner * SLOTS + source * CAP + earlier).astype(jnp.int32)
    slot_list = jnp.full((N_DP * SLOTS,), -1, jnp.int32).at[slot_id].set(jnp.arange(LISTS, dtype=jnp.int32))

    def visit(totals, index):
        start = (index * SLOTS).astype(jnp.int32)
        raw_pick = lax.dynamic_slice_in_dim(slot_list, start, SLOTS, 0)
        present = raw_pick >= 0
        picked = jnp.clip(raw_pick, 0, LISTS - 1)
        chosen_rows = lax.dynamic_slice_in_dim(student_rows, start, SLOTS, 0)
        chosen_target = target[picked] * present[:, None, None].astype(jnp.float32)
        chosen_mask = live_mask[picked] * present[:, None].astype(jnp.float32)
        normed, gate_pre, up_pre, activated, hidden = student_feedforward(chosen_rows.reshape(SLOTS * MAXP, DS), student_gain, w_gate, w_up, w_down)
        shaped = hidden.reshape(SLOTS, MAXP, DS)
        per_slot_losses = list_losses(shaped, chosen_target, chosen_mask)
        grad_hidden = hidden_gradient(shaped, chosen_target, chosen_mask)
        grad_hidden = grad_hidden.reshape(SLOTS * MAXP, DS).astype(jnp.bfloat16)
        partials = weight_gradients(normed, gate_pre, up_pre, activated, grad_hidden, w_down)
        summed = tuple((total + lax.optimization_barrier(term.astype(jnp.bfloat16)).astype(jnp.float32) for total, term in zip(totals, partials)))
        return (summed, per_slot_losses)
    initial = (jnp.zeros((DS, FFS), jnp.float32), jnp.zeros((DS, FFS), jnp.float32), jnp.zeros((FFS, DS), jnp.float32))
    summed, all_losses = lax.scan(visit, initial, jnp.arange(N_DP, dtype=jnp.int32))
    list_loss = all_losses.reshape(N_DP * SLOTS)[slot_id]
    return (list_loss, summed[0], summed[1], summed[2])
```

```python
import functools
import math

import jax
import jax.numpy as jnp
from jax import lax
from jax.experimental import pallas as pl
from jax.experimental.pallas import tpu as pltpu
from jax.sharding import Mesh
from jax.sharding import PartitionSpec as P

HQ = 32
HEAD = 128
MAXP = 4
EPSILON = 1e-06
ROPE_BASE = 1000000.0
DP = ("yh", "x", "z")
TP = ("yl", "core")
ALL = DP + TP
SIZES = {"yh": 2, "x": 4, "z": 4, "yl": 2, "core": 2}
PAIRS = [(i, j) for i in range(MAXP) for j in range(i, MAXP)]
FIRST = 80
CHUNK = 768
TOKENS_STEP = 512
AROUND = (0, 3, 1, 2)
bf16 = jnp.bfloat16
f32 = jnp.float32


def shift(value, axis, by):
    n = SIZES[axis]
    return lax.ppermute(value, axis, [(i, (i + by) % n) for i in range(n)])


def after(values, *deps):
    return lax.optimization_barrier((tuple(values), tuple(deps)))[0]


def ring_halves(block, axis, *deps):
    (block,) = after((block,), *deps)
    left, right = shift(block, axis, 1), shift(block, axis, -1)
    half = block.shape[0] // 2
    return block, left, right, shift(left[:half], axis, 1), shift(right[half:], axis, -1)


def ring(block, axis, *deps):
    (block,) = after((block,), *deps)
    return block, shift(block, axis, 1), shift(block, axis, -1), shift(block, axis, 2)


def two_rings(along_x, along_z, *deps):
    x0, z0 = after((along_x, along_z), *deps)
    x3, z3 = shift(x0, "x", 2), shift(z0, "z", 2)
    x2, x1 = shift(x0, "x", -1), shift(x0, "x", 1)
    z2, z1 = shift(z0, "z", -1), shift(z0, "z", 1)
    return (x0, x1, x2, x3), (z0, z1, z2, z3)


def stack_kernel(moves, cuts, *refs):
    sources, outs = refs[: -len(cuts)], refs[-len(cuts) :]
    for i, at, n, to in moves:
        for out, (low, high) in zip(outs, cuts):
            out[to : to + n, :] = sources[i][at : at + n, low:high]


def stack(arrays, moves, cuts=None):
    rows, columns = sum(m[2] for m in moves), arrays[0].shape[1]
    cuts = cuts or [(0, columns)]
    return pl.pallas_call(
        functools.partial(stack_kernel, moves, cuts),
        in_specs=[pl.BlockSpec(memory_space=pltpu.VMEM)] * len(arrays),
        out_specs=[pl.BlockSpec(memory_space=pltpu.VMEM)] * len(cuts),
        out_shape=[jax.ShapeDtypeStruct((rows, c[1] - c[0]), arrays[0].dtype) for c in cuts],
        compiler_params=pltpu.CompilerParams(vmem_limit_bytes=24 * 1024 * 1024),
        cost_estimate=pl.CostEstimate(
            flops=0, bytes_accessed=4 * rows * columns, transcendentals=0
        ),
    )(*arrays)


def stack_ring(blocks, cut):
    n, columns = blocks[0].shape
    return stack(blocks, [(k, 0, n, k * n) for k in range(4)], [(0, cut), (cut, columns)])


def stack_slots(blocks):
    n = blocks[0].shape[0] // MAXP
    whole = 4 if len(blocks) == 4 else 3
    moves = [(k, p * n, n, (p * 4 + k) * n) for k in range(whole) for p in range(MAXP)]
    if whole == 3:
        moves += [(3 + p // 2, p % 2 * n, n, (p * 4 + 3) * n) for p in range(MAXP)]
    return stack(blocks, moves)[0]


def head_tables(gain, tokens, list_len):
    half = HEAD // 2
    positions = (jnp.arange(tokens, dtype=jnp.int32) % list_len).astype(f32)
    exponent = jnp.arange(half, dtype=f32) * (-2.0 / HEAD)
    angles = positions[:, None] * jnp.power(ROPE_BASE, exponent)[None, :]
    cosines, sines = jnp.cos(angles), jnp.sin(angles)
    same = jnp.concatenate([cosines, cosines], axis=1) * gain[None, :]
    crossed = jnp.concatenate([-sines, sines], axis=1) * jnp.roll(gain, half)[None, :]
    return same, crossed


def norm_rotate(values, same, crossed):
    mean = jnp.mean(values * values, axis=-1, keepdims=True)
    scaled = values * lax.rsqrt(mean + EPSILON)
    return (scaled * same + pltpu.roll(scaled, HEAD // 2, 1) * crossed).astype(bf16)


def teacher_kernel(heads, with_keys, list_len, *refs):
    place, states, q_same, q_cross = refs[:4]
    rest = refs[4:]
    if with_keys:
        k_same, k_cross = rest[:2]
        rest = rest[2:]
    else:
        scale_in, k_in, v_in = rest[:3]
        rest = rest[3:]
    member, tally = rest[:2]
    pieces = rest[2:10]
    rest = rest[10:]
    if with_keys:
        gram, scale_out, k_out, v_out, weights, sems = rest
    else:
        gram, weights, sems = rest

    @pl.when(pl.program_id(0) == 0)
    def _():
        yh, xx, zz = place[0], place[1], place[2]
        copies = []
        for part in range(2):
            base = part * FIRST
            for far in range(4):
                for near in range(4):
                    for h in range(2):
                        source = part * 4 + far
                        row = (near * 2 + h) * FIRST
                        rel_x, rel_z = (far, near) if part == 0 else (near, far)
                        x_at = lax.rem(xx + AROUND[rel_x], 4)
                        z_at = lax.rem(zz + AROUND[rel_z], 4)
                        y_at = lax.rem(yh + h, 2)
                        to = ((y_at * 4 + x_at) * 4 + z_at) * (2 * FIRST) + base
                        copies.append(
                            pltpu.make_async_copy(
                                pieces[source].at[pl.ds(row, FIRST), :],
                                weights.at[pl.ds(pl.multiple_of(to, 16), FIRST), :],
                                sems.at[len(copies)],
                            )
                        )
        for copy in copies:
            copy.start()
        for copy in copies:
            copy.wait()

    groups, _, width = states.shape
    total, squares = None, None
    for k in range(groups):
        piece = states[k]
        term = jnp.dot(
            piece, weights[k * width : (k + 1) * width, :], preferred_element_type=f32
        )
        total = term if total is None else total + term
        if with_keys:
            wide = piece.astype(f32)
            more = jnp.sum(wide * wide, axis=1, keepdims=True)
            squares = more if squares is None else squares + more
    if with_keys:
        scale = lax.rsqrt(squares / (groups * width) + EPSILON)
        scale_out[...] = scale
    else:
        scale = scale_in[...]
    total = total * scale
    if with_keys:
        keys = norm_rotate(total[:, :HEAD], k_same[...], k_cross[...])
        values = total[:, HEAD : 2 * HEAD].astype(bf16)
        k_out[...] = keys
        v_out[...] = values
        first = 2 * HEAD
    else:
        keys, values, first = k_in[...], v_in[...], 0
    tokens = total.shape[0]
    block = 128
    row = lax.broadcasted_iota(jnp.int32, (block, block), 0)
    col = lax.broadcasted_iota(jnp.int32, (block, block), 1)
    allowed = (col <= row) & (col // list_len == row // list_len)
    hide = jnp.where(allowed, 0.0, -1e30)
    ones = jnp.ones((block, HEAD), bf16)
    queries = [
        norm_rotate(total[:, first + h * HEAD : first + (h + 1) * HEAD], q_same[...], q_cross[...])
        for h in range(heads)
    ]
    mixed = []
    for s in range(tokens // block):
        part = slice(s * block, (s + 1) * block)
        stacked = jnp.concatenate([q[part] for q in queries], axis=0)
        scores = lax.dot_general(
            stacked, keys[part], (((1,), (1,)), ((), ())), preferred_element_type=f32
        )
        scores = scores.reshape(heads, block, block) * (1.0 / math.sqrt(HEAD)) + hide[None]
        shifted = jnp.exp(scores - jnp.max(scores, axis=-1, keepdims=True)).astype(bf16)
        summed = jnp.dot(
            shifted.reshape(heads * block, block),
            jnp.concatenate([values[part], ones], axis=1),
            preferred_element_type=f32,
        )
        result = (summed[:, :HEAD] / summed[:, HEAD:]).astype(bf16)
        mixed.append(
            jnp.concatenate([result[h * block : (h + 1) * block] for h in range(heads)], axis=1)
        )
    attended = jnp.concatenate(mixed, axis=0)
    pooled = jnp.dot(member[...], attended, preferred_element_type=f32)
    pooled = (pooled / tally[...]).astype(bf16)
    gram[0] = lax.dot_general(
        pooled, pooled, (((1,), (1,)), ((), ())), preferred_element_type=f32
    )


def teacher_chunk(place, states, q_tables, extra, member, tally, parts, heads, with_keys, list_len):
    groups, tokens, width = states.shape
    step = TOKENS_STEP
    lists = step // list_len
    rows = lists * MAXP
    columns = parts[0].shape[1]
    pieces = list(parts)
    block = lambda n, m: pl.BlockSpec((n, m), lambda g: (g, 0))
    fixed = lambda n, m: pl.BlockSpec((n, m), lambda g: (0, 0))
    extra_specs = [fixed(step, HEAD)] * 2
    if not with_keys:
        extra_specs = [block(step, 1)] + [block(step, HEAD)] * 2
    outs = [jax.ShapeDtypeStruct((tokens // step, rows, rows), f32)]
    out_specs = [pl.BlockSpec((1, rows, rows), lambda g: (g, 0, 0))]
    if with_keys:
        outs += [jax.ShapeDtypeStruct((tokens, 1), f32)]
        outs += [jax.ShapeDtypeStruct((tokens, HEAD), bf16)] * 2
        out_specs += [block(step, 1)] + [block(step, HEAD)] * 2
    depth = groups * width
    return pl.pallas_call(
        functools.partial(teacher_kernel, heads, with_keys, list_len),
        grid=(tokens // step,),
        in_specs=[
            pl.BlockSpec(memory_space=pltpu.SMEM),
            pl.BlockSpec((groups, step, width), lambda g: (0, g, 0)),
        ]
        + [fixed(step, HEAD)] * 2
        + extra_specs
        + [block(rows, step), block(rows, 1)]
        + [pl.BlockSpec(memory_space=pltpu.HBM)] * len(pieces),
        out_specs=out_specs,
        out_shape=outs,
        scratch_shapes=[
            pltpu.VMEM((depth, columns), bf16),
            pltpu.SemaphoreType.DMA((64,)),
        ],
        compiler_params=pltpu.CompilerParams(
            dimension_semantics=("arbitrary",), vmem_limit_bytes=40 * 1024 * 1024
        ),
        cost_estimate=pl.CostEstimate(
            flops=2 * tokens * depth * columns,
            bytes_accessed=2 * depth * (tokens + columns),
            transcendentals=tokens * 128 * heads,
        ),
    )(place, states, *q_tables, *extra, member, tally, *pieces)


def rms_scale(values, weights):
    return values * lax.rsqrt(jnp.mean(values * values, axis=-1, keepdims=True) + EPSILON) * weights


def forward_kernel(count, *refs):
    z, rows, (gain, w_gate, w_up), rest = refs[0], refs[1 : 1 + count], refs[1 + count : 4 + count], refs[4 + count :]
    values = rows[0][...]
    if count == 2:
        early = pl.program_id(0) < pl.num_programs(0) // 2
        values = jnp.where(early, values, rows[1][...])
    values = values.astype(f32)
    active, scaled = rest[0], rest[-1]
    scaled[...] = rms_scale(values, gain[...]).T.astype(bf16)
    gate_pre = jnp.dot(w_gate[...], scaled[...], preferred_element_type=f32)
    up_pre = jnp.dot(w_up[...], scaled[...], preferred_element_type=f32)
    sigma = jax.nn.sigmoid(gate_pre)
    gated = gate_pre * sigma
    active[...] = (gated * up_pre).astype(bf16)
    if count == 2:
        gate_slope, up_slope, picked = rest[1:4]
        gate_slope[...] = (up_pre * sigma * (1.0 + gate_pre * (1.0 - sigma))).astype(bf16)
        up_slope[...] = gated.astype(bf16)
        pick_rows(picked, scaled, z[0], 8)


def pick_rows(picked, source, z, groups):
    own = picked.shape[0] // groups
    for k in range(groups):
        start = pl.multiple_of((k * 4 + z) * own, 16)
        picked[k * own : (k + 1) * own, :] = source[pl.ds(start, own), :]


def forward(z, rows, gain, w_gate, w_up):
    count = len(rows)
    size, width = rows[0].shape
    units = w_gate.shape[0]
    tile = 256
    middle = size // tile
    total = count * size
    whole = lambda a: pl.BlockSpec(a.shape, lambda g: (0, 0), pipeline_mode=pl.Buffered(1))
    across = lambda n: pl.BlockSpec((n, tile), lambda g: (0, g))
    outs = [units] if count == 1 else [units, units, units, width // 4]
    row_specs = [
        pl.BlockSpec((tile, width), lambda g: (jnp.minimum(g, middle - 1), 0)),
        pl.BlockSpec((tile, width), lambda g: (jnp.maximum(g - middle, 0), 0)),
    ]
    return pl.pallas_call(
        functools.partial(forward_kernel, count),
        grid=(count * middle,),
        in_specs=[pl.BlockSpec(memory_space=pltpu.SMEM)]
        + row_specs[:count]
        + [whole(gain), whole(w_gate), whole(w_up)],
        out_specs=[across(n) for n in outs],
        out_shape=[jax.ShapeDtypeStruct((n, total), bf16) for n in outs],
        scratch_shapes=[pltpu.VMEM((width, tile), bf16)],
        compiler_params=pltpu.CompilerParams(
            dimension_semantics=("arbitrary",), vmem_limit_bytes=44 * 1024 * 1024
        ),
        cost_estimate=pl.CostEstimate(
            flops=4 * total * width * units,
            bytes_accessed=2 * total * width + 4 * width * units + 6 * total * units,
            transcendentals=total * units,
        ),
    )(z, *rows, gain, w_gate, w_up)


def hidden_kernel(rows_a, rows_b, ffn_a, ffn_b, turned, grams):
    @pl.when(pl.program_id(0) == 0)
    def _():
        grams[...] = jnp.zeros_like(grams)

    for c, (rows, ffn) in enumerate(((rows_a, ffn_a), (rows_b, ffn_b))):
        hidden = (rows[...].astype(f32) + ffn[...].astype(f32)).T
        size = hidden.shape[1] // MAXP
        turned[:, c * MAXP * size : (c + 1) * MAXP * size] = hidden.astype(bf16)
        cut = [hidden[:, i * size : (i + 1) * size] for i in range(MAXP)]
        for k, (i, j) in enumerate(PAIRS):
            grams[k : k + 1, c * size : (c + 1) * size] += jnp.sum(
                cut[i] * cut[j], axis=0, keepdims=True
            )


def hidden_parts(rows_a, rows_b, ffn_a, ffn_b):
    rows, width = rows_a.shape
    tile = 256
    spec = pl.BlockSpec((rows, tile), lambda g: (0, g))
    return pl.pallas_call(
        hidden_kernel,
        grid=(width // tile,),
        in_specs=[spec] * 4,
        out_specs=[
            pl.BlockSpec((tile, 2 * rows), lambda g: (g, 0)),
            pl.BlockSpec((16, 2 * rows // MAXP), lambda g: (0, 0)),
        ],
        out_shape=[
            jax.ShapeDtypeStruct((width, 2 * rows), bf16),
            jax.ShapeDtypeStruct((16, 2 * rows // MAXP), f32),
        ],
        compiler_params=pltpu.CompilerParams(
            dimension_semantics=("arbitrary",), vmem_limit_bytes=24 * 1024 * 1024
        ),
        cost_estimate=pl.CostEstimate(
            flops=24 * rows * width, bytes_accessed=12 * rows * width, transcendentals=0
        ),
    )(rows_a, rows_b, ffn_a, ffn_b)


def cosines(at, size):
    scales = [jnp.sqrt(at[i, i] / size + EPSILON) for i in range(MAXP)]
    return {(i, j): at[i, j] / (size * scales[i] * scales[j]) for i, j in PAIRS}, scales


def back_kernel(width, z, target, grams, turned, back, picked, losses, factors):
    slots = target.shape[1]

    @pl.when(pl.program_id(0) == 0)
    def _():
        row = lambda ref, k: ref[k : k + 1, :]
        wanted, _ = cosines({p: row(target, k) for k, p in enumerate(PAIRS)}, HQ * HEAD)
        have, scales = cosines({p: row(grams, k) for k, p in enumerate(PAIRS)}, width)
        count = row(target, len(PAIRS))
        alive = [jnp.where(count > i + 0.5, 1.0, 0.0) for i in range(MAXP)]
        bound = jnp.maximum(count, 1.0)
        over = 1.0 / (bound * bound)
        slope = {}
        loss = None
        for i, j in PAIRS:
            both = alive[i] * alive[j]
            differ = have[i, j] - wanted[i, j]
            slope[i, j] = slope[j, i] = 2.0 * both * differ * over
            term = (1.0 if i == j else 2.0) * both * differ * differ
            loss = term if loss is None else loss + term
        losses[...] = jnp.broadcast_to(loss * over, losses.shape)
        for i in range(MAXP):
            pull = sum(slope[i, j] * have[min(i, j), max(i, j)] for j in range(MAXP))
            for j in range(MAXP):
                term = slope[i, j] / (scales[i] * scales[j])
                if i == j:
                    term = term - pull / (scales[i] * scales[i])
                factors[i * MAXP + j : i * MAXP + j + 1, :] = 2.0 * term

    half = slots // 2
    for c in range(2):
        at = lambda i: slice((c * MAXP + i) * half, (c * MAXP + i + 1) * half)
        cut = [turned[:, at(i)].astype(f32) for i in range(MAXP)]
        for i in range(MAXP):
            mixed = None
            for j in range(MAXP):
                k = i * MAXP + j
                term = factors[k : k + 1, c * half : (c + 1) * half] * cut[j]
                mixed = term if mixed is None else mixed + term
            back[:, at(i)] = mixed.astype(bf16)
    pick_rows(picked, back, z[0], 2)


def pull_back(z, target, grams, turned):
    width, rows = turned.shape
    tile = width // 4
    fixed = pl.BlockSpec(target.shape, lambda g: (0, 0))
    moving = lambda n: pl.BlockSpec((n, rows), lambda g: (g, 0))
    return pl.pallas_call(
        functools.partial(back_kernel, width),
        grid=(4,),
        in_specs=[pl.BlockSpec(memory_space=pltpu.SMEM), fixed, fixed, moving(tile)],
        out_specs=[
            moving(tile),
            moving(tile // 4),
            pl.BlockSpec((8, target.shape[1]), lambda g: (0, 0)),
        ],
        out_shape=[
            jax.ShapeDtypeStruct((width, rows), bf16),
            jax.ShapeDtypeStruct((width // 4, rows), bf16),
            jax.ShapeDtypeStruct((8, target.shape[1]), f32),
        ],
        scratch_shapes=[pltpu.VMEM(target.shape, f32)],
        compiler_params=pltpu.CompilerParams(
            dimension_semantics=("arbitrary",), vmem_limit_bytes=24 * 1024 * 1024
        ),
        cost_estimate=pl.CostEstimate(
            flops=8 * rows * width, bytes_accessed=5 * rows * width, transcendentals=0
        ),
    )(z, target, grams, turned)


def inner_kernel(w_down, back, gate_slope, up_slope, gate_in, up_in):
    total = jnp.dot(w_down[...], back[...], preferred_element_type=f32)
    gate_in[...] = (total * gate_slope[...].astype(f32)).astype(bf16)
    up_in[...] = (total * up_slope[...].astype(f32)).astype(bf16)


def inner_grads(w_down, back, gate_slope, up_slope):
    units, width = w_down.shape
    rows = back.shape[1]
    tile = 256
    across = lambda n: pl.BlockSpec((n, tile), lambda g: (0, g))
    return pl.pallas_call(
        inner_kernel,
        grid=(rows // tile,),
        in_specs=[
            pl.BlockSpec(w_down.shape, lambda g: (0, 0), pipeline_mode=pl.Buffered(1)),
            across(width),
            across(units),
            across(units),
        ],
        out_specs=[across(units)] * 2,
        out_shape=[jax.ShapeDtypeStruct((units, rows), bf16)] * 2,
        compiler_params=pltpu.CompilerParams(
            dimension_semantics=("arbitrary",), vmem_limit_bytes=32 * 1024 * 1024
        ),
        cost_estimate=pl.CostEstimate(
            flops=2 * rows * width * units,
            bytes_accessed=2 * (rows * width + units * width + 4 * rows * units),
            transcendentals=0,
        ),
    )(w_down, back, gate_slope, up_slope)


def grad_kernel(picked, inner, *refs):
    out = refs[-1]
    product = lax.dot_general(
        picked[...], inner[...], (((1,), (1,)), ((), ())), preferred_element_type=f32
    ).astype(bf16)
    own = picked.shape[0] // out.shape[0]
    for k in range(out.shape[0]):
        out[k, :own] = product[k * own : (k + 1) * own]
        if len(refs) == 2:
            out[k, own:] = refs[0][k]


def weight_grad(picked, inner, *more):
    features, rows = picked.shape
    units = inner.shape[0]
    size = features // 8 + sum(a.shape[1] for a in more)
    return pl.pallas_call(
        grad_kernel,
        in_specs=[pl.BlockSpec(memory_space=pltpu.VMEM)] * (2 + len(more)),
        out_specs=pl.BlockSpec(memory_space=pltpu.VMEM),
        out_shape=jax.ShapeDtypeStruct((8, size, units), bf16),
        compiler_params=pltpu.CompilerParams(vmem_limit_bytes=32 * 1024 * 1024),
        cost_estimate=pl.CostEstimate(
            flops=2 * features * rows * units,
            bytes_accessed=2 * (features * rows + units * rows + features * units),
            transcendentals=0,
        ),
    )(picked, inner, *more)


def scatter_x(blocks, x, *deps):
    total = lax.dynamic_index_in_dim(blocks, x, 1, keepdims=False).astype(f32)
    outs = [lax.dynamic_index_in_dim(blocks, lax.rem(x + by, 4), 1, keepdims=False) for by in range(1, 4)]
    terms = tuple(shift(out, "x", by + 1) for by, out in enumerate(outs))
    if deps:
        terms = after(terms, *deps)
    for term in terms:
        total = total + term.astype(f32)
    return total


def scatter_y(blocks, yh):
    mine = lax.dynamic_index_in_dim(blocks, yh, 0, keepdims=False)
    out = lax.dynamic_index_in_dim(blocks, 1 - yh, 0, keepdims=False)
    return mine.astype(f32) + shift(out, "yh", 1).astype(f32)


def shards(
    teacher_states,
    teacher_gain,
    w_query,
    key_weight,
    value_weight,
    query_gain,
    key_gain,
    segments,
    passage_counts,
    swap_order,
    list_owner,
    student_rows,
    student_gain,
    w_gate,
    w_up,
    w_down,
):
    yh, x, z, yl, core = (lax.axis_index(a) for a in ALL)
    dp = (yh * 4 + x) * 4 + z
    lists, list_len = segments.shape
    slots = student_rows.shape[0]
    width = student_rows.shape[2]

    halves = jnp.swapaxes(student_rows.reshape(2, slots // 2, MAXP, width), 1, 2)
    own_rows = halves.reshape(slots * MAXP, width)
    half = own_rows.shape[0] // 2
    rows_half = lax.dynamic_slice_in_dim(own_rows, core * half, half, 0)
    rows_ring = ring_halves(rows_half, "z")

    depth = w_query.shape[0]
    row_gain = lax.dynamic_slice_in_dim(teacher_gain, dp * depth, depth, 0).astype(f32)[:, None]
    weights = jnp.concatenate([key_weight, value_weight, w_query], axis=1)
    weights = (weights.astype(f32) * row_gain).astype(bf16)
    across_y = shift(weights, "yh", 1)
    states = lax.all_gather(teacher_states, TP, axis=0, tiled=False)
    one = jnp.concatenate([weights[:FIRST], across_y[:FIRST]], axis=0)
    two = jnp.concatenate([weights[FIRST:], across_y[FIRST:]], axis=0)

    gain = student_gain.astype(f32)[None, :]
    z_at = z[None].astype(jnp.int32)
    (active_own,) = forward(z_at, (own_rows,), gain, w_gate.T, w_up.T)

    two_ring, one_ring = two_rings(two, one, *rows_ring, active_own)
    rows_mine = stack_slots(rows_ring)
    rows_other = shift(rows_mine, "core", 1)
    line_z = stack_ring(one_ring, CHUNK)
    line_x = stack_ring(two_ring, CHUNK)

    def spread(k, *before):
        rings = two_rings(line_z[k], line_x[k], *before)
        return (*rings[0], *rings[1])

    partial = lax.dot_general(
        active_own, w_down, (((0,), (0,)), ((), ())), preferred_element_type=f32
    ).astype(bf16)
    kept = lax.dynamic_slice_in_dim(partial, core * half, half, 0).astype(f32)
    given = lax.dynamic_slice_in_dim(partial, (1 - core) * half, half, 0)
    pair_sum = (kept + shift(given, "core", 1).astype(f32)).astype(bf16)
    pair_other = shift(pair_sum, "yl", 1)
    parts_a = spread(0, line_x[0], line_z[0], rows_other, pair_other)
    ffn_half = (pair_sum.astype(f32) + pair_other.astype(f32)).astype(bf16)

    active, gate_slope, up_slope, normed_pick = forward(
        z_at, (rows_mine, rows_other), gain, w_gate.T, w_up.T
    )
    parts_b = spread(1, *parts_a, active)

    owner = list_owner[:, 0]
    index = jnp.arange(lists, dtype=jnp.int32)
    earlier = jnp.sum(
        ((owner[None, :] == owner[:, None]) & (index[None, :] < index[:, None])).astype(jnp.int32),
        axis=1,
    )
    slot_of = owner * 2 + earlier
    select = (jnp.arange(slots, dtype=jnp.int32)[:, None] == slot_of[None, :]).astype(f32)
    per = slots // 2

    place = jnp.stack([yh, x, z]).astype(jnp.int32)
    q_tables = head_tables(query_gain, TOKENS_STEP, list_len)
    k_tables = head_tables(key_gain, TOKENS_STEP, list_len)
    spot = jnp.arange(MAXP, dtype=jnp.int32)
    live = spot[None, :] < passage_counts[:, None]
    member = (segments[:, None, :] == swap_order[:, :, None]) & live[:, :, None]
    tally = jnp.maximum(jnp.sum(member.astype(f32), axis=2), 1.0).reshape(lists * MAXP, 1)
    group = TOKENS_STEP // list_len
    same_list = jnp.eye(group, dtype=bool)
    spread_member = (
        member.reshape(lists // group, group, MAXP, 1, list_len)
        & same_list[None, :, None, :, None]
    )
    spread_member = spread_member.reshape(lists * MAXP, TOKENS_STEP).astype(bf16)
    gram_a, scale, keys, values = teacher_chunk(
        place, states, q_tables, k_tables, spread_member, tally, parts_a, 4, True, list_len
    )
    ffn_ring = ring(ffn_half, "z", *parts_b, gram_a)
    (gram_b,) = teacher_chunk(
        place, states, q_tables, (scale, keys, values), spread_member, tally, parts_b, 4, False, list_len
    )
    gram = (gram_a + gram_b).reshape(lists // group, group, MAXP, group, MAXP)
    gram = jnp.sum(jnp.where(same_list[None, :, None, :, None], gram, 0.0), axis=3)
    gram = gram.reshape(lists, MAXP, MAXP)
    columns = [gram[:, i, j] for i, j in PAIRS] + [passage_counts.astype(f32) * 0.25]
    sent = jnp.stack(columns + [jnp.zeros_like(columns[0])] * (16 - len(columns)), axis=1)

    send = jnp.einsum("sl,lc->sc", select, sent, precision=lax.Precision.HIGHEST)
    send = send.reshape(8, 4, 2 * 16)
    send = jnp.stack([send[:, [(k + a) % 4 for a in AROUND]] for k in range(4)], axis=1)
    send = jnp.broadcast_to(send.reshape(8, 4, 1, 128), (8, 4, 4, 128)).reshape(128, 128)
    ffn_mine = stack_slots(after(ffn_ring, gram_b))
    ffn_other = shift(ffn_mine, "core", 1)
    turned, grams = hidden_parts(rows_mine, rows_other, ffn_mine, ffn_other)

    got = lax.all_to_all(send, ALL, split_axis=0, concat_axis=0, tiled=True)
    got = jnp.sum(got.reshape(32, 4, 128), axis=1)
    got = got.reshape(2, 16, 4, 2, 16).transpose(4, 0, 2, 1, 3).reshape(16, 2, 4 * per)
    got = jnp.where(core == 0, got, got[:, ::-1]).reshape(16, 8 * per)

    back, back_pick, losses = pull_back(z_at, got, grams, turned)
    cut = lambda grad: grad.reshape(2, 4, *grad.shape[1:])
    slot_losses = losses[0].reshape(2, 4, 4, 4, 2)
    slot_losses = lax.dynamic_index_in_dim(slot_losses, z, 3, keepdims=False)
    slot_losses = jnp.where(core == 0, slot_losses, slot_losses[::-1])
    slot_losses = slot_losses.transpose(0, 2, 1, 3).reshape(8, 8)
    owners = (yh * 4 + x) * 4 + (z + jnp.array(AROUND)) % 4
    lanes = (owners[:, None] * 2 + jnp.arange(2)[None, :]).reshape(8)
    lane = jnp.arange(w_gate.shape[1], dtype=jnp.int32)
    spots = (lanes[:, None] == lane[None, :]).astype(f32)
    laid = jnp.sum(slot_losses[:, :, None] * spots[None], axis=1)
    terms, left = [], laid
    for _ in range(3):
        terms.append(left.astype(bf16))
        left = left - terms[-1].astype(f32)
    zeros = jnp.zeros((8, 13, lane.shape[0]), bf16)
    loss_rows = jnp.concatenate([jnp.stack(terms, axis=1), zeros], axis=1)
    grad_down = weight_grad(back_pick, active)
    down_x = scatter_x(cut(grad_down), x).astype(bf16)
    gate_in, up_in = inner_grads(w_down, back, gate_slope, up_slope)
    gate_in, up_in = after((gate_in, up_in), down_x)
    grad_up = weight_grad(normed_pick, up_in, loss_rows)
    (gate_in,) = after((gate_in,), grad_up)
    grad_gate = weight_grad(normed_pick, gate_in)
    gate_y = scatter_y(cut(grad_gate), yh).astype(bf16)
    down_sum = scatter_y(down_x, yh)
    up_x = scatter_x(cut(grad_up), x, gate_y, down_sum).astype(bf16)
    gate_sum = scatter_x(gate_y[None], x)[0]
    up_sum = scatter_y(up_x, yh)

    returned = jnp.sum(up_sum[-16:, :slots], axis=0)
    list_loss = jnp.sum(select * returned[:, None], axis=0)
    return (list_loss, gate_sum, up_sum[:-16], down_sum.T)


def solution(mesh):
    fine = Mesh(mesh.devices.reshape(tuple(SIZES.values())), tuple(SIZES))
    placed = (
        P(DP, TP),
        P(),
        P(DP, TP),
        P(DP, TP),
        P(DP, TP),
        P(),
        P(),
        P(DP, None),
        P(DP),
        P(DP, None),
        P(DP, None),
        P(DP, None, None),
        P(),
        P(None, TP),
        P(None, TP),
        P(TP, None),
    )
    return jax.shard_map(
        shards,
        mesh=fine,
        in_specs=placed,
        out_specs=(P(DP), P(DP, TP), P(DP, TP), P(TP, DP)),
        check_vma=False,
    )
```

```python
import functools
import math

import jax
import jax.numpy as jnp
from jax import lax
from jax.experimental import pallas as pl
from jax.experimental.pallas import tpu as pltpu
from jax.sharding import Mesh
from jax.sharding import PartitionSpec as P

HQ = 32
HEAD = 128
MAXP = 4
EPSILON = 1e-06
ROPE_BASE = 1000000.0
DP = ("yh", "x", "z")
TP = ("yl", "core")
ALL = DP + TP
SIZES = {"yh": 2, "x": 4, "z": 4, "yl": 2, "core": 2}
PAIRS = [(i, j) for i in range(MAXP) for j in range(i, MAXP)]
FIRST = 80
CHUNK = 768
TOKENS_STEP = 512
AROUND = (0, 3, 1, 2)
bf16 = jnp.bfloat16
f32 = jnp.float32


def shift(value, axis, by):
    n = SIZES[axis]
    return lax.ppermute(value, axis, [(i, (i + by) % n) for i in range(n)])


def after(values, *deps):
    return lax.optimization_barrier((tuple(values), tuple(deps)))[0]


def ring_halves(block, axis, *deps):
    (block,) = after((block,), *deps)
    left, right = shift(block, axis, 1), shift(block, axis, -1)
    half = block.shape[0] // 2
    return block, left, right, shift(left[:half], axis, 1), shift(right[half:], axis, -1)


def ring(block, axis, *deps):
    (block,) = after((block,), *deps)
    return block, shift(block, axis, 1), shift(block, axis, -1), shift(block, axis, 2)


def two_rings(along_x, along_z, *deps):
    x0, z0 = after((along_x, along_z), *deps)
    x3, z3 = shift(x0, "x", 2), shift(z0, "z", 2)
    x2, x1 = shift(x0, "x", -1), shift(x0, "x", 1)
    z2, z1 = shift(z0, "z", -1), shift(z0, "z", 1)
    return (x0, x1, x2, x3), (z0, z1, z2, z3)


def stack_kernel(moves, cuts, *refs):
    sources, outs = refs[: -len(cuts)], refs[-len(cuts) :]
    for i, at, n, to in moves:
        for out, (low, high) in zip(outs, cuts):
            out[to : to + n, :] = sources[i][at : at + n, low:high]


def stack(arrays, moves, cuts=None):
    rows, columns = sum(m[2] for m in moves), arrays[0].shape[1]
    cuts = cuts or [(0, columns)]
    return pl.pallas_call(
        functools.partial(stack_kernel, moves, cuts),
        in_specs=[pl.BlockSpec(memory_space=pltpu.VMEM)] * len(arrays),
        out_specs=[pl.BlockSpec(memory_space=pltpu.VMEM)] * len(cuts),
        out_shape=[jax.ShapeDtypeStruct((rows, c[1] - c[0]), arrays[0].dtype) for c in cuts],
        compiler_params=pltpu.CompilerParams(vmem_limit_bytes=24 * 1024 * 1024),
        cost_estimate=pl.CostEstimate(
            flops=0, bytes_accessed=4 * rows * columns, transcendentals=0
        ),
    )(*arrays)


def stack_ring(blocks, cut):
    n, columns = blocks[0].shape
    return stack(blocks, [(k, 0, n, k * n) for k in range(4)], [(0, cut), (cut, columns)])


def stack_slots(blocks):
    n = blocks[0].shape[0] // MAXP
    whole = 4 if len(blocks) == 4 else 3
    moves = [(k, p * n, n, (p * 4 + k) * n) for k in range(whole) for p in range(MAXP)]
    if whole == 3:
        moves += [(3 + p // 2, p % 2 * n, n, (p * 4 + 3) * n) for p in range(MAXP)]
    return stack(blocks, moves)[0]


def head_tables(gain, tokens, list_len):
    half = HEAD // 2
    positions = (jnp.arange(tokens, dtype=jnp.int32) % list_len).astype(f32)
    exponent = jnp.arange(half, dtype=f32) * (-2.0 / HEAD)
    angles = positions[:, None] * jnp.power(ROPE_BASE, exponent)[None, :]
    cosines, sines = jnp.cos(angles), jnp.sin(angles)
    same = jnp.concatenate([cosines, cosines], axis=1) * gain[None, :]
    crossed = jnp.concatenate([-sines, sines], axis=1) * jnp.roll(gain, half)[None, :]
    return same, crossed


def norm_rotate(values, same, crossed):
    mean = jnp.mean(values * values, axis=-1, keepdims=True)
    scaled = values * lax.rsqrt(mean + EPSILON)
    return (scaled * same + pltpu.roll(scaled, HEAD // 2, 1) * crossed).astype(bf16)


def teacher_kernel(heads, with_keys, list_len, *refs):
    place, states, q_same, q_cross = refs[:4]
    rest = refs[4:]
    if with_keys:
        k_same, k_cross = rest[:2]
        rest = rest[2:]
    else:
        scale_in, k_in, v_in = rest[:3]
        rest = rest[3:]
    member, tally = rest[:2]
    pieces = rest[2:10]
    rest = rest[10:]
    if with_keys:
        gram, scale_out, k_out, v_out, weights, sems = rest
    else:
        gram, weights, sems = rest

    @pl.when(pl.program_id(0) == 0)
    def _():
        yh, xx, zz = place[0], place[1], place[2]
        copies = []
        for part in range(2):
            base = part * FIRST
            for far in range(4):
                for near in range(4):
                    for h in range(2):
                        source = part * 4 + far
                        row = (near * 2 + h) * FIRST
                        rel_x, rel_z = (far, near) if part == 0 else (near, far)
                        x_at = lax.rem(xx + AROUND[rel_x], 4)
                        z_at = lax.rem(zz + AROUND[rel_z], 4)
                        y_at = lax.rem(yh + h, 2)
                        to = ((y_at * 4 + x_at) * 4 + z_at) * (2 * FIRST) + base
                        copies.append(
                            pltpu.make_async_copy(
                                pieces[source].at[pl.ds(row, FIRST), :],
                                weights.at[pl.ds(pl.multiple_of(to, 16), FIRST), :],
                                sems.at[len(copies)],
                            )
                        )
        for copy in copies:
            copy.start()
        for copy in copies:
            copy.wait()

    groups, _, width = states.shape
    total, squares = None, None
    for k in range(groups):
        piece = states[k]
        term = jnp.dot(
            piece, weights[k * width : (k + 1) * width, :], preferred_element_type=f32
        )
        total = term if total is None else total + term
        if with_keys:
            wide = piece.astype(f32)
            more = jnp.sum(wide * wide, axis=1, keepdims=True)
            squares = more if squares is None else squares + more
    if with_keys:
        scale = lax.rsqrt(squares / (groups * width) + EPSILON)
        scale_out[...] = scale
    else:
        scale = scale_in[...]
    total = total * scale
    if with_keys:
        keys = norm_rotate(total[:, :HEAD], k_same[...], k_cross[...])
        values = total[:, HEAD : 2 * HEAD].astype(bf16)
        k_out[...] = keys
        v_out[...] = values
        first = 2 * HEAD
    else:
        keys, values, first = k_in[...], v_in[...], 0
    tokens = total.shape[0]
    block = 128
    row = lax.broadcasted_iota(jnp.int32, (block, block), 0)
    col = lax.broadcasted_iota(jnp.int32, (block, block), 1)
    allowed = (col <= row) & (col // list_len == row // list_len)
    hide = jnp.where(allowed, 0.0, -1e30)
    ones = jnp.ones((block, HEAD), bf16)
    queries = [
        norm_rotate(total[:, first + h * HEAD : first + (h + 1) * HEAD], q_same[...], q_cross[...])
        for h in range(heads)
    ]
    mixed = []
    for s in range(tokens // block):
        part = slice(s * block, (s + 1) * block)
        stacked = jnp.concatenate([q[part] for q in queries], axis=0)
        scores = lax.dot_general(
            stacked, keys[part], (((1,), (1,)), ((), ())), preferred_element_type=f32
        )
        scores = scores.reshape(heads, block, block) * (1.0 / math.sqrt(HEAD)) + hide[None]
        shifted = jnp.exp(scores - jnp.max(scores, axis=-1, keepdims=True)).astype(bf16)
        summed = jnp.dot(
            shifted.reshape(heads * block, block),
            jnp.concatenate([values[part], ones], axis=1),
            preferred_element_type=f32,
        )
        result = (summed[:, :HEAD] / summed[:, HEAD:]).astype(bf16)
        mixed.append(
            jnp.concatenate([result[h * block : (h + 1) * block] for h in range(heads)], axis=1)
        )
    attended = jnp.concatenate(mixed, axis=0)
    pooled = jnp.dot(member[...], attended, preferred_element_type=f32)
    pooled = (pooled / tally[...]).astype(bf16)
    gram[0] = lax.dot_general(
        pooled, pooled, (((1,), (1,)), ((), ())), preferred_element_type=f32
    )


def teacher_chunk(place, states, q_tables, extra, member, tally, parts, heads, with_keys, list_len):
    groups, tokens, width = states.shape
    step = TOKENS_STEP
    lists = step // list_len
    rows = lists * MAXP
    columns = parts[0].shape[1]
    pieces = list(parts)
    block = lambda n, m: pl.BlockSpec((n, m), lambda g: (g, 0))
    fixed = lambda n, m: pl.BlockSpec((n, m), lambda g: (0, 0))
    extra_specs = [fixed(step, HEAD)] * 2
    if not with_keys:
        extra_specs = [block(step, 1)] + [block(step, HEAD)] * 2
    outs = [jax.ShapeDtypeStruct((tokens // step, rows, rows), f32)]
    out_specs = [pl.BlockSpec((1, rows, rows), lambda g: (g, 0, 0))]
    if with_keys:
        outs += [jax.ShapeDtypeStruct((tokens, 1), f32)]
        outs += [jax.ShapeDtypeStruct((tokens, HEAD), bf16)] * 2
        out_specs += [block(step, 1)] + [block(step, HEAD)] * 2
    depth = groups * width
    return pl.pallas_call(
        functools.partial(teacher_kernel, heads, with_keys, list_len),
        grid=(tokens // step,),
        in_specs=[
            pl.BlockSpec(memory_space=pltpu.SMEM),
            pl.BlockSpec((groups, step, width), lambda g: (0, g, 0)),
        ]
        + [fixed(step, HEAD)] * 2
        + extra_specs
        + [block(rows, step), block(rows, 1)]
        + [pl.BlockSpec(memory_space=pltpu.HBM)] * len(pieces),
        out_specs=out_specs,
        out_shape=outs,
        scratch_shapes=[
            pltpu.VMEM((depth, columns), bf16),
            pltpu.SemaphoreType.DMA((64,)),
        ],
        compiler_params=pltpu.CompilerParams(
            dimension_semantics=("arbitrary",), vmem_limit_bytes=58 * 1024 * 1024
        ),
        cost_estimate=pl.CostEstimate(
            flops=2 * tokens * depth * columns,
            bytes_accessed=2 * depth * (tokens + columns),
            transcendentals=tokens * 128 * heads,
        ),
    )(place, states, *q_tables, *extra, member, tally, *pieces)


def rms_scale(values, weights):
    return values * lax.rsqrt(jnp.mean(values * values, axis=-1, keepdims=True) + EPSILON) * weights


def forward_kernel(count, *refs):
    z, rows, (gain, w_gate, w_up), rest = refs[0], refs[1 : 1 + count], refs[1 + count : 4 + count], refs[4 + count :]
    values = rows[0][...]
    if count == 2:
        early = pl.program_id(0) < pl.num_programs(0) // 2
        values = jnp.where(early, values, rows[1][...])
    values = values.astype(f32)
    active, scaled = rest[0], rest[-1]
    scaled[...] = rms_scale(values, gain[...]).T.astype(bf16)
    gate_pre = jnp.dot(w_gate[...], scaled[...], preferred_element_type=f32)
    up_pre = jnp.dot(w_up[...], scaled[...], preferred_element_type=f32)
    sigma = jax.nn.sigmoid(gate_pre)
    gated = gate_pre * sigma
    active[...] = (gated * up_pre).astype(bf16)
    if count == 2:
        gate_slope, up_slope, picked = rest[1:4]
        gate_slope[...] = (up_pre * sigma * (1.0 + gate_pre * (1.0 - sigma))).astype(bf16)
        up_slope[...] = gated.astype(bf16)
        pick_rows(picked, scaled, z[0], 8)


def pick_rows(picked, source, z, groups):
    own = picked.shape[0] // groups
    for k in range(groups):
        start = pl.multiple_of((k * 4 + z) * own, 16)
        picked[k * own : (k + 1) * own, :] = source[pl.ds(start, own), :]


def forward(z, rows, gain, w_gate, w_up):
    count = len(rows)
    size, width = rows[0].shape
    units = w_gate.shape[0]
    tile = 256
    middle = size // tile
    total = count * size
    whole = lambda a: pl.BlockSpec(a.shape, lambda g: (0, 0), pipeline_mode=pl.Buffered(1))
    across = lambda n: pl.BlockSpec((n, tile), lambda g: (0, g))
    outs = [units] if count == 1 else [units, units, units, width // 4]
    row_specs = [
        pl.BlockSpec((tile, width), lambda g: (jnp.minimum(g, middle - 1), 0)),
        pl.BlockSpec((tile, width), lambda g: (jnp.maximum(g - middle, 0), 0)),
    ]
    return pl.pallas_call(
        functools.partial(forward_kernel, count),
        grid=(count * middle,),
        in_specs=[pl.BlockSpec(memory_space=pltpu.SMEM)]
        + row_specs[:count]
        + [whole(gain), whole(w_gate), whole(w_up)],
        out_specs=[across(n) for n in outs],
        out_shape=[jax.ShapeDtypeStruct((n, total), bf16) for n in outs],
        scratch_shapes=[pltpu.VMEM((width, tile), bf16)],
        compiler_params=pltpu.CompilerParams(
            dimension_semantics=("arbitrary",), vmem_limit_bytes=58 * 1024 * 1024
        ),
        cost_estimate=pl.CostEstimate(
            flops=4 * total * width * units,
            bytes_accessed=2 * total * width + 4 * width * units + 6 * total * units,
            transcendentals=total * units,
        ),
    )(z, *rows, gain, w_gate, w_up)


def hidden_kernel(rows_a, rows_b, ffn_a, ffn_b, turned, grams):
    @pl.when(pl.program_id(0) == 0)
    def _():
        grams[...] = jnp.zeros_like(grams)

    for c, (rows, ffn) in enumerate(((rows_a, ffn_a), (rows_b, ffn_b))):
        hidden = (rows[...].astype(f32) + ffn[...].astype(f32)).T
        size = hidden.shape[1] // MAXP
        turned[:, c * MAXP * size : (c + 1) * MAXP * size] = hidden.astype(bf16)
        cut = [hidden[:, i * size : (i + 1) * size] for i in range(MAXP)]
        for k, (i, j) in enumerate(PAIRS):
            grams[k : k + 1, c * size : (c + 1) * size] += jnp.sum(
                cut[i] * cut[j], axis=0, keepdims=True
            )


def hidden_parts(rows_a, rows_b, ffn_a, ffn_b):
    rows, width = rows_a.shape
    tile = 256
    spec = pl.BlockSpec((rows, tile), lambda g: (0, g))
    return pl.pallas_call(
        hidden_kernel,
        grid=(width // tile,),
        in_specs=[spec] * 4,
        out_specs=[
            pl.BlockSpec((tile, 2 * rows), lambda g: (g, 0)),
            pl.BlockSpec((16, 2 * rows // MAXP), lambda g: (0, 0)),
        ],
        out_shape=[
            jax.ShapeDtypeStruct((width, 2 * rows), bf16),
            jax.ShapeDtypeStruct((16, 2 * rows // MAXP), f32),
        ],
        compiler_params=pltpu.CompilerParams(
            dimension_semantics=("arbitrary",), vmem_limit_bytes=24 * 1024 * 1024
        ),
        cost_estimate=pl.CostEstimate(
            flops=24 * rows * width, bytes_accessed=12 * rows * width, transcendentals=0
        ),
    )(rows_a, rows_b, ffn_a, ffn_b)


def cosines(at, size):
    scales = [jnp.sqrt(at[i, i] / size + EPSILON) for i in range(MAXP)]
    return {(i, j): at[i, j] / (size * scales[i] * scales[j]) for i, j in PAIRS}, scales


def back_kernel(width, z, target, grams, turned, active, back, down, losses, factors, picked, held, sem):
    slots = target.shape[1]
    fetch = pltpu.make_async_copy(active, held, sem)

    @pl.when(pl.program_id(0) == 0)
    def _():
        fetch.start()

    @pl.when(pl.program_id(0) == 0)
    def _():
        row = lambda ref, k: ref[k : k + 1, :]
        wanted, _ = cosines({p: row(target, k) for k, p in enumerate(PAIRS)}, HQ * HEAD)
        have, scales = cosines({p: row(grams, k) for k, p in enumerate(PAIRS)}, width)
        count = row(target, len(PAIRS))
        alive = [jnp.where(count > i + 0.5, 1.0, 0.0) for i in range(MAXP)]
        bound = jnp.maximum(count, 1.0)
        over = 1.0 / (bound * bound)
        slope = {}
        loss = None
        for i, j in PAIRS:
            both = alive[i] * alive[j]
            differ = have[i, j] - wanted[i, j]
            slope[i, j] = slope[j, i] = 2.0 * both * differ * over
            term = (1.0 if i == j else 2.0) * both * differ * differ
            loss = term if loss is None else loss + term
        losses[...] = jnp.broadcast_to(loss * over, losses.shape)
        for i in range(MAXP):
            pull = sum(slope[i, j] * have[min(i, j), max(i, j)] for j in range(MAXP))
            for j in range(MAXP):
                term = slope[i, j] / (scales[i] * scales[j])
                if i == j:
                    term = term - pull / (scales[i] * scales[i])
                factors[i * MAXP + j : i * MAXP + j + 1, :] = 2.0 * term

    half = slots // 2
    for c in range(2):
        at = lambda i: slice((c * MAXP + i) * half, (c * MAXP + i + 1) * half)
        cut = [turned[:, at(i)].astype(f32) for i in range(MAXP)]
        for i in range(MAXP):
            mixed = None
            for j in range(MAXP):
                k = i * MAXP + j
                term = factors[k : k + 1, c * half : (c + 1) * half] * cut[j]
                mixed = term if mixed is None else mixed + term
            back[:, at(i)] = mixed.astype(bf16)
    step = pl.program_id(0)
    own = down.shape[1]
    group = back.shape[0] // 2
    for k in range(2):
        start = pl.multiple_of(k * group + z[0] * own, 16)
        to = pl.multiple_of((step * 2 + k) * own, 16)
        picked[pl.ds(to, own), :] = back[pl.ds(start, own), :]

    @pl.when(step == pl.num_programs(0) - 1)
    def _():
        fetch.wait()
        product = lax.dot_general(
            picked[...], held[...], (((1,), (1,)), ((), ())), preferred_element_type=f32
        ).astype(bf16)
        for k in range(down.shape[0]):
            down[k] = product[k * own : (k + 1) * own]


def pull_back(z, target, grams, turned, active):
    width, rows = turned.shape
    units = active.shape[0]
    own = width // 32
    tile = width // 4
    fixed = pl.BlockSpec(target.shape, lambda g: (0, 0))
    moving = lambda n: pl.BlockSpec((n, rows), lambda g: (g, 0))
    return pl.pallas_call(
        functools.partial(back_kernel, width),
        grid=(4,),
        in_specs=[
            pl.BlockSpec(memory_space=pltpu.SMEM),
            fixed,
            fixed,
            moving(tile),
            pl.BlockSpec(memory_space=pltpu.HBM),
        ],
        out_specs=[
            moving(tile),
            pl.BlockSpec((8, own, units), lambda g: (0, 0, 0)),
            pl.BlockSpec((8, target.shape[1]), lambda g: (0, 0)),
        ],
        out_shape=[
            jax.ShapeDtypeStruct((width, rows), bf16),
            jax.ShapeDtypeStruct((8, own, units), bf16),
            jax.ShapeDtypeStruct((8, target.shape[1]), f32),
        ],
        scratch_shapes=[
            pltpu.VMEM(target.shape, f32),
            pltpu.VMEM((8 * own, rows), bf16),
            pltpu.VMEM((units, rows), bf16),
            pltpu.SemaphoreType.DMA,
        ],
        compiler_params=pltpu.CompilerParams(
            dimension_semantics=("arbitrary",), vmem_limit_bytes=32 * 1024 * 1024
        ),
        cost_estimate=pl.CostEstimate(
            flops=8 * rows * width + 16 * own * rows * units, bytes_accessed=5 * rows * width, transcendentals=0
        ),
    )(z, target, grams, turned, active)


def inner_kernel(w_down, back, gate_slope, up_slope, gate_in, up_in):
    total = jnp.dot(w_down[...], back[...], preferred_element_type=f32)
    gate_in[...] = (total * gate_slope[...].astype(f32)).astype(bf16)
    up_in[...] = (total * up_slope[...].astype(f32)).astype(bf16)


def inner_grads(w_down, back, gate_slope, up_slope):
    units, width = w_down.shape
    rows = back.shape[1]
    tile = 256
    across = lambda n: pl.BlockSpec((n, tile), lambda g: (0, g))
    return pl.pallas_call(
        inner_kernel,
        grid=(rows // tile,),
        in_specs=[
            pl.BlockSpec(w_down.shape, lambda g: (0, 0), pipeline_mode=pl.Buffered(1)),
            across(width),
            across(units),
            across(units),
        ],
        out_specs=[across(units)] * 2,
        out_shape=[jax.ShapeDtypeStruct((units, rows), bf16)] * 2,
        compiler_params=pltpu.CompilerParams(
            dimension_semantics=("arbitrary",), vmem_limit_bytes=32 * 1024 * 1024
        ),
        cost_estimate=pl.CostEstimate(
            flops=2 * rows * width * units,
            bytes_accessed=2 * (rows * width + units * width + 4 * rows * units),
            transcendentals=0,
        ),
    )(w_down, back, gate_slope, up_slope)


def grad_kernel(picked, inner, *refs):
    out = refs[-1]
    product = lax.dot_general(
        picked[...], inner[...], (((1,), (1,)), ((), ())), preferred_element_type=f32
    ).astype(bf16)
    own = picked.shape[0] // out.shape[0]
    for k in range(out.shape[0]):
        out[k, :own] = product[k * own : (k + 1) * own]
        if len(refs) == 2:
            out[k, own:] = refs[0][k]


def weight_grad(picked, inner, *more):
    features, rows = picked.shape
    units = inner.shape[0]
    size = features // 8 + sum(a.shape[1] for a in more)
    return pl.pallas_call(
        grad_kernel,
        in_specs=[pl.BlockSpec(memory_space=pltpu.VMEM)] * (2 + len(more)),
        out_specs=pl.BlockSpec(memory_space=pltpu.VMEM),
        out_shape=jax.ShapeDtypeStruct((8, size, units), bf16),
        compiler_params=pltpu.CompilerParams(vmem_limit_bytes=32 * 1024 * 1024),
        cost_estimate=pl.CostEstimate(
            flops=2 * features * rows * units,
            bytes_accessed=2 * (features * rows + units * rows + features * units),
            transcendentals=0,
        ),
    )(picked, inner, *more)


def scatter_x(blocks, x, *deps):
    total = lax.dynamic_index_in_dim(blocks, x, 1, keepdims=False).astype(f32)
    outs = [lax.dynamic_index_in_dim(blocks, lax.rem(x + by, 4), 1, keepdims=False) for by in range(1, 4)]
    terms = tuple(shift(out, "x", by + 1) for by, out in enumerate(outs))
    if deps:
        terms = after(terms, *deps)
    for term in terms:
        total = total + term.astype(f32)
    return total


def scatter_y(blocks, yh):
    mine = lax.dynamic_index_in_dim(blocks, yh, 0, keepdims=False)
    out = lax.dynamic_index_in_dim(blocks, 1 - yh, 0, keepdims=False)
    return mine.astype(f32) + shift(out, "yh", 1).astype(f32)


def shards(
    teacher_states,
    teacher_gain,
    w_query,
    key_weight,
    value_weight,
    query_gain,
    key_gain,
    segments,
    passage_counts,
    swap_order,
    list_owner,
    student_rows,
    student_gain,
    w_gate,
    w_up,
    w_down,
):
    yh, x, z, yl, core = (lax.axis_index(a) for a in ALL)
    dp = (yh * 4 + x) * 4 + z
    lists, list_len = segments.shape
    slots = student_rows.shape[0]
    width = student_rows.shape[2]

    halves = jnp.swapaxes(student_rows.reshape(2, slots // 2, MAXP, width), 1, 2)
    own_rows = halves.reshape(slots * MAXP, width)
    half = own_rows.shape[0] // 2
    rows_half = lax.dynamic_slice_in_dim(own_rows, core * half, half, 0)
    rows_ring = ring_halves(rows_half, "z")

    depth = w_query.shape[0]
    row_gain = lax.dynamic_slice_in_dim(teacher_gain, dp * depth, depth, 0).astype(f32)[:, None]
    weights = jnp.concatenate([key_weight, value_weight, w_query], axis=1)
    weights = (weights.astype(f32) * row_gain).astype(bf16)
    across_y = shift(weights, "yh", 1)
    states = lax.all_gather(teacher_states, TP, axis=0, tiled=False)
    one = jnp.concatenate([weights[:FIRST], across_y[:FIRST]], axis=0)
    two = jnp.concatenate([weights[FIRST:], across_y[FIRST:]], axis=0)

    gain = student_gain.astype(f32)[None, :]
    z_at = z[None].astype(jnp.int32)
    (rows_now,) = after((own_rows,), rows_ring[1], rows_ring[2])
    (active_own,) = forward(z_at, (rows_now,), gain, w_gate.T, w_up.T)

    two_ring, one_ring = two_rings(two, one, *rows_ring, active_own)
    rows_mine = stack_slots(after(rows_ring, *one_ring[1:], *two_ring[1:]))
    rows_other = shift(rows_mine, "core", 1)
    line_z = stack_ring(one_ring, CHUNK)
    line_x = stack_ring(two_ring, CHUNK)

    def spread(k, *before):
        rings = two_rings(line_z[k], line_x[k], *before)
        return (*rings[0], *rings[1])

    partial = lax.dot_general(
        active_own, w_down, (((0,), (0,)), ((), ())), preferred_element_type=f32
    ).astype(bf16)
    kept = lax.dynamic_slice_in_dim(partial, core * half, half, 0).astype(f32)
    given = lax.dynamic_slice_in_dim(partial, (1 - core) * half, half, 0)
    pair_sum = (kept + shift(given, "core", 1).astype(f32)).astype(bf16)
    pair_other = shift(pair_sum, "yl", 1)
    ffn_half = (pair_sum.astype(f32) + pair_other.astype(f32)).astype(bf16)
    parts_a = spread(0, line_x[0], line_z[0])

    active, gate_slope, up_slope, normed_pick = forward(
        z_at, (rows_mine, rows_other), gain, w_gate.T, w_up.T
    )
    parts_b = spread(1, *parts_a, active, ffn_half)

    owner = list_owner[:, 0]
    index = jnp.arange(lists, dtype=jnp.int32)
    earlier = jnp.sum(
        ((owner[None, :] == owner[:, None]) & (index[None, :] < index[:, None])).astype(jnp.int32),
        axis=1,
    )
    slot_of = owner * 2 + earlier
    select = (jnp.arange(slots, dtype=jnp.int32)[:, None] == slot_of[None, :]).astype(f32)
    per = slots // 2

    place = jnp.stack([yh, x, z]).astype(jnp.int32)
    q_tables = head_tables(query_gain, TOKENS_STEP, list_len)
    k_tables = head_tables(key_gain, TOKENS_STEP, list_len)
    spot = jnp.arange(MAXP, dtype=jnp.int32)
    live = spot[None, :] < passage_counts[:, None]
    member = (segments[:, None, :] == swap_order[:, :, None]) & live[:, :, None]
    tally = jnp.maximum(jnp.sum(member.astype(f32), axis=2), 1.0).reshape(lists * MAXP, 1)
    group = TOKENS_STEP // list_len
    same_list = jnp.eye(group, dtype=bool)
    spread_member = (
        member.reshape(lists // group, group, MAXP, 1, list_len)
        & same_list[None, :, None, :, None]
    )
    spread_member = spread_member.reshape(lists * MAXP, TOKENS_STEP).astype(bf16)
    gram_a, scale, keys, values = teacher_chunk(
        place, states, q_tables, k_tables, spread_member, tally, parts_a, 4, True, list_len
    )
    ffn_ring = ring(ffn_half, "z", *parts_b, gram_a)
    (gram_b,) = teacher_chunk(
        place, states, q_tables, (scale, keys, values), spread_member, tally, parts_b, 4, False, list_len
    )
    gram = (gram_a + gram_b).reshape(lists // group, group, MAXP, group, MAXP)
    gram = jnp.sum(jnp.where(same_list[None, :, None, :, None], gram, 0.0), axis=3)
    gram = gram.reshape(lists, MAXP, MAXP)
    columns = [gram[:, i, j] for i, j in PAIRS] + [passage_counts.astype(f32) * 0.25]
    sent = jnp.stack(columns + [jnp.zeros_like(columns[0])] * (16 - len(columns)), axis=1)

    send = jnp.einsum("sl,lc->sc", select, sent, precision=lax.Precision.HIGHEST)
    send = send.reshape(8, 4, 2 * 16)
    send = jnp.stack([send[:, [(k + a) % 4 for a in AROUND]] for k in range(4)], axis=1)
    send = jnp.broadcast_to(send.reshape(8, 4, 1, 128), (8, 4, 4, 128)).reshape(128, 128)
    ffn_mine = stack_slots(after(ffn_ring, gram_b))
    ffn_other = shift(ffn_mine, "core", 1)
    turned, grams = hidden_parts(rows_mine, rows_other, ffn_mine, ffn_other)

    got = lax.all_to_all(send, ALL, split_axis=0, concat_axis=0, tiled=True)
    got = jnp.sum(got.reshape(32, 4, 128), axis=1)
    got = got.reshape(2, 16, 4, 2, 16).transpose(4, 0, 2, 1, 3).reshape(16, 2, 4 * per)
    got = jnp.where(core == 0, got, got[:, ::-1]).reshape(16, 8 * per)

    back, grad_down, losses = pull_back(z_at, got, grams, turned, active)
    cut = lambda grad: grad.reshape(2, 4, *grad.shape[1:])
    slot_losses = losses[0].reshape(2, 4, 4, 4, 2)
    slot_losses = lax.dynamic_index_in_dim(slot_losses, z, 3, keepdims=False)
    slot_losses = jnp.where(core == 0, slot_losses, slot_losses[::-1])
    slot_losses = slot_losses.transpose(0, 2, 1, 3).reshape(8, 8)
    owners = (yh * 4 + x) * 4 + (z + jnp.array(AROUND)) % 4
    lanes = (owners[:, None] * 2 + jnp.arange(2)[None, :]).reshape(8)
    lane = jnp.arange(w_gate.shape[1], dtype=jnp.int32)
    spots = (lanes[:, None] == lane[None, :]).astype(f32)
    laid = jnp.sum(slot_losses[:, :, None] * spots[None], axis=1)
    terms, left = [], laid
    for _ in range(3):
        terms.append(left.astype(bf16))
        left = left - terms[-1].astype(f32)
    zeros = jnp.zeros((8, 13, lane.shape[0]), bf16)
    loss_rows = jnp.concatenate([jnp.stack(terms, axis=1), zeros], axis=1)
    down_x = scatter_x(cut(grad_down), x).astype(bf16)
    gate_in, up_in = inner_grads(w_down, back, gate_slope, up_slope)
    gate_in, up_in = after((gate_in, up_in), down_x)
    grad_gate = weight_grad(normed_pick, gate_in)
    gate_y = scatter_y(cut(grad_gate), yh).astype(bf16)
    (up_in,) = after((up_in,), grad_gate)
    grad_up = weight_grad(normed_pick, up_in, loss_rows)
    down_sum = scatter_y(down_x, yh)
    up_x = scatter_x(cut(grad_up), x, gate_y, down_sum).astype(bf16)
    gate_sum = scatter_x(gate_y[None], x)[0]
    up_sum = scatter_y(up_x, yh)

    returned = jnp.sum(up_sum[-16:, :slots], axis=0)
    list_loss = jnp.sum(select * returned[:, None], axis=0)
    return (list_loss, gate_sum, up_sum[:-16], down_sum.T)


def solution(mesh):
    fine = Mesh(mesh.devices.reshape(tuple(SIZES.values())), tuple(SIZES))
    placed = (
        P(DP, TP),
        P(),
        P(DP, TP),
        P(DP, TP),
        P(DP, TP),
        P(),
        P(),
        P(DP, None),
        P(DP),
        P(DP, None),
        P(DP, None),
        P(DP, None, None),
        P(),
        P(None, TP),
        P(None, TP),
        P(TP, None),
    )
    return jax.shard_map(
        shards,
        mesh=fine,
        in_specs=placed,
        out_specs=(P(DP), P(DP, TP), P(DP, TP), P(TP, DP)),
        check_vma=False,
    )
```

```python
import functools
import math

import jax
import jax.numpy as jnp
from jax import lax
from jax.experimental import pallas as pl
from jax.experimental.pallas import tpu as pltpu
from jax.sharding import Mesh
from jax.sharding import PartitionSpec as P

HQ = 32
HEAD = 128
MAXP = 4
EPSILON = 1e-06
ROPE_BASE = 1000000.0
DP = ("yh", "x", "z")
TP = ("yl", "core")
ALL = DP + TP
SIZES = {"yh": 2, "x": 4, "z": 4, "yl": 2, "core": 2}
PAIRS = [(i, j) for i in range(MAXP) for j in range(i, MAXP)]
FIRST = 80
CHUNK = 768
TOKENS_STEP = 512
AROUND = (0, 3, 1, 2)
bf16 = jnp.bfloat16
f32 = jnp.float32


def shift(value, axis, by):
    n = SIZES[axis]
    return lax.ppermute(value, axis, [(i, (i + by) % n) for i in range(n)])


def after(values, *deps):
    return lax.optimization_barrier((tuple(values), tuple(deps)))[0]


def ring_halves(block, axis, *deps):
    (block,) = after((block,), *deps)
    left, right = shift(block, axis, 1), shift(block, axis, -1)
    half = block.shape[0] // 2
    return block, left, right, shift(left[:half], axis, 1), shift(right[half:], axis, -1)


def ring(block, axis, *deps):
    (block,) = after((block,), *deps)
    return block, shift(block, axis, 1), shift(block, axis, -1), shift(block, axis, 2)


def two_rings(along_x, along_z, *deps):
    x0, z0 = after((along_x, along_z), *deps)
    x3, z3 = shift(x0, "x", 2), shift(z0, "z", 2)
    x2, x1 = shift(x0, "x", -1), shift(x0, "x", 1)
    z2, z1 = shift(z0, "z", -1), shift(z0, "z", 1)
    return (x0, x1, x2, x3), (z0, z1, z2, z3)


def stack_kernel(moves, cuts, *refs):
    sems = refs[-1]
    sources, outs = refs[: -len(cuts) - 1], refs[-len(cuts) - 1 : -1]
    copies = []
    for i, at, n, to in moves:
        for out, (low, high) in zip(outs, cuts):
            copies.append(
                pltpu.make_async_copy(
                    sources[i].at[pl.ds(at, n), pl.ds(low, high - low)],
                    out.at[pl.ds(to, n), :],
                    sems.at[len(copies)],
                )
            )
    for copy in copies:
        copy.start()
    for copy in copies:
        copy.wait()


def stack(arrays, moves, cuts=None):
    rows, columns = sum(m[2] for m in moves), arrays[0].shape[1]
    cuts = cuts or [(0, columns)]
    return pl.pallas_call(
        functools.partial(stack_kernel, moves, cuts),
        in_specs=[pl.BlockSpec(memory_space=pl.ANY)] * len(arrays),
        out_specs=[pl.BlockSpec(memory_space=pltpu.VMEM)] * len(cuts),
        out_shape=[jax.ShapeDtypeStruct((rows, c[1] - c[0]), arrays[0].dtype) for c in cuts],
        scratch_shapes=[pltpu.SemaphoreType.DMA((len(moves) * len(cuts),))],
        compiler_params=pltpu.CompilerParams(vmem_limit_bytes=24 * 1024 * 1024),
        cost_estimate=pl.CostEstimate(
            flops=0, bytes_accessed=4 * rows * columns, transcendentals=0
        ),
    )(*arrays)


def stack_ring(blocks, cut):
    n, columns = blocks[0].shape
    return stack(blocks, [(k, 0, n, k * n) for k in range(4)], [(0, cut), (cut, columns)])


def stack_slots(blocks):
    n = blocks[0].shape[0] // MAXP
    whole = 4 if len(blocks) == 4 else 3
    moves = [(k, p * n, n, (p * 4 + k) * n) for k in range(whole) for p in range(MAXP)]
    if whole == 3:
        moves += [(3 + p // 2, p % 2 * n, n, (p * 4 + 3) * n) for p in range(MAXP)]
    return stack(blocks, moves)[0]


def head_tables(gain, tokens, list_len):
    half = HEAD // 2
    positions = (jnp.arange(tokens, dtype=jnp.int32) % list_len).astype(f32)
    exponent = jnp.arange(half, dtype=f32) * (-2.0 / HEAD)
    angles = positions[:, None] * jnp.power(ROPE_BASE, exponent)[None, :]
    cosines, sines = jnp.cos(angles), jnp.sin(angles)
    same = jnp.concatenate([cosines, cosines], axis=1) * gain[None, :]
    crossed = jnp.concatenate([-sines, sines], axis=1) * jnp.roll(gain, half)[None, :]
    return same, crossed


def norm_rotate(values, same, crossed):
    mean = jnp.mean(values * values, axis=-1, keepdims=True)
    scaled = values * lax.rsqrt(mean + EPSILON)
    return (scaled * same + pltpu.roll(scaled, HEAD // 2, 1) * crossed).astype(bf16)


def teacher_kernel(heads, with_keys, list_len, *refs):
    place, states, q_same, q_cross = refs[:4]
    rest = refs[4:]
    if with_keys:
        k_same, k_cross = rest[:2]
        rest = rest[2:]
    else:
        scale_in, k_in, v_in = rest[:3]
        rest = rest[3:]
    member, tally = rest[:2]
    pieces = rest[2:10]
    rest = rest[10:]
    if with_keys:
        gram, scale_out, k_out, v_out, weights, sems = rest
    else:
        gram, weights, sems = rest

    @pl.when(pl.program_id(0) == 0)
    def _():
        yh, xx, zz = place[0], place[1], place[2]
        copies = []
        for part in range(2):
            base = part * FIRST
            for far in range(4):
                for near in range(4):
                    for h in range(2):
                        source = part * 4 + far
                        row = (near * 2 + h) * FIRST
                        rel_x, rel_z = (far, near) if part == 0 else (near, far)
                        x_at = lax.rem(xx + AROUND[rel_x], 4)
                        z_at = lax.rem(zz + AROUND[rel_z], 4)
                        y_at = lax.rem(yh + h, 2)
                        to = ((y_at * 4 + x_at) * 4 + z_at) * (2 * FIRST) + base
                        copies.append(
                            pltpu.make_async_copy(
                                pieces[source].at[pl.ds(row, FIRST), :],
                                weights.at[pl.ds(pl.multiple_of(to, 16), FIRST), :],
                                sems.at[len(copies)],
                            )
                        )
        for copy in copies:
            copy.start()
        for copy in copies:
            copy.wait()

    groups, _, width = states.shape
    total, squares = None, None
    for k in range(groups):
        piece = states[k]
        term = jnp.dot(
            piece, weights[k * width : (k + 1) * width, :], preferred_element_type=f32
        )
        total = term if total is None else total + term
        if with_keys:
            wide = piece.astype(f32)
            more = jnp.sum(wide * wide, axis=1, keepdims=True)
            squares = more if squares is None else squares + more
    if with_keys:
        scale = lax.rsqrt(squares / (groups * width) + EPSILON)
        scale_out[...] = scale
    else:
        scale = scale_in[...]
    total = total * scale
    if with_keys:
        keys = norm_rotate(total[:, :HEAD], k_same[...], k_cross[...])
        values = total[:, HEAD : 2 * HEAD].astype(bf16)
        k_out[...] = keys
        v_out[...] = values
        first = 2 * HEAD
    else:
        keys, values, first = k_in[...], v_in[...], 0
    tokens = total.shape[0]
    block = 128
    row = lax.broadcasted_iota(jnp.int32, (block, block), 0)
    col = lax.broadcasted_iota(jnp.int32, (block, block), 1)
    allowed = (col <= row) & (col // list_len == row // list_len)
    hide = jnp.where(allowed, 0.0, -1e30)
    ones = jnp.ones((block, HEAD), bf16)
    queries = [
        norm_rotate(total[:, first + h * HEAD : first + (h + 1) * HEAD], q_same[...], q_cross[...])
        for h in range(heads)
    ]
    mixed = []
    for s in range(tokens // block):
        part = slice(s * block, (s + 1) * block)
        stacked = jnp.concatenate([q[part] for q in queries], axis=0)
        scores = lax.dot_general(
            stacked, keys[part], (((1,), (1,)), ((), ())), preferred_element_type=f32
        )
        scores = scores.reshape(heads, block, block) * (1.0 / math.sqrt(HEAD)) + hide[None]
        shifted = jnp.exp(scores - jnp.max(scores, axis=-1, keepdims=True)).astype(bf16)
        summed = jnp.dot(
            shifted.reshape(heads * block, block),
            jnp.concatenate([values[part], ones], axis=1),
            preferred_element_type=f32,
        )
        result = (summed[:, :HEAD] / summed[:, HEAD:]).astype(bf16)
        mixed.append(
            jnp.concatenate([result[h * block : (h + 1) * block] for h in range(heads)], axis=1)
        )
    attended = jnp.concatenate(mixed, axis=0)
    pooled = jnp.dot(member[...], attended, preferred_element_type=f32)
    pooled = (pooled / tally[...]).astype(bf16)
    gram[0] = lax.dot_general(
        pooled, pooled, (((1,), (1,)), ((), ())), preferred_element_type=f32
    )


def teacher_chunk(place, states, q_tables, extra, member, tally, parts, heads, with_keys, list_len):
    groups, tokens, width = states.shape
    step = TOKENS_STEP
    lists = step // list_len
    rows = lists * MAXP
    columns = parts[0].shape[1]
    pieces = list(parts)
    block = lambda n, m: pl.BlockSpec((n, m), lambda g: (g, 0))
    fixed = lambda n, m: pl.BlockSpec((n, m), lambda g: (0, 0))
    extra_specs = [fixed(step, HEAD)] * 2
    if not with_keys:
        extra_specs = [block(step, 1)] + [block(step, HEAD)] * 2
    outs = [jax.ShapeDtypeStruct((tokens // step, rows, rows), f32)]
    out_specs = [pl.BlockSpec((1, rows, rows), lambda g: (g, 0, 0))]
    if with_keys:
        outs += [jax.ShapeDtypeStruct((tokens, 1), f32)]
        outs += [jax.ShapeDtypeStruct((tokens, HEAD), bf16)] * 2
        out_specs += [block(step, 1)] + [block(step, HEAD)] * 2
    depth = groups * width
    return pl.pallas_call(
        functools.partial(teacher_kernel, heads, with_keys, list_len),
        grid=(tokens // step,),
        in_specs=[
            pl.BlockSpec(memory_space=pltpu.SMEM),
            pl.BlockSpec((groups, step, width), lambda g: (0, g, 0)),
        ]
        + [fixed(step, HEAD)] * 2
        + extra_specs
        + [block(rows, step), block(rows, 1)]
        + [pl.BlockSpec(memory_space=pltpu.HBM)] * len(pieces),
        out_specs=out_specs,
        out_shape=outs,
        scratch_shapes=[
            pltpu.VMEM((depth, columns), bf16),
            pltpu.SemaphoreType.DMA((64,)),
        ],
        compiler_params=pltpu.CompilerParams(
            dimension_semantics=("arbitrary",), vmem_limit_bytes=58 * 1024 * 1024
        ),
        cost_estimate=pl.CostEstimate(
            flops=2 * tokens * depth * columns,
            bytes_accessed=2 * depth * (tokens + columns),
            transcendentals=tokens * 128 * heads,
        ),
    )(place, states, *q_tables, *extra, member, tally, *pieces)


def rms_scale(values, weights):
    return values * lax.rsqrt(jnp.mean(values * values, axis=-1, keepdims=True) + EPSILON) * weights


def forward_kernel(count, *refs):
    z, rows, (gain, w_gate, w_up), rest = refs[0], refs[1 : 1 + count], refs[1 + count : 4 + count], refs[4 + count :]
    values = rows[0][...]
    if count == 2:
        early = pl.program_id(0) < pl.num_programs(0) // 2
        values = jnp.where(early, values, rows[1][...])
    values = values.astype(f32)
    active, scaled = rest[0], rest[-1]
    scaled[...] = rms_scale(values, gain[...]).T.astype(bf16)
    gate_pre = jnp.dot(w_gate[...], scaled[...], preferred_element_type=f32)
    up_pre = jnp.dot(w_up[...], scaled[...], preferred_element_type=f32)
    sigma = jax.nn.sigmoid(gate_pre)
    gated = gate_pre * sigma
    active[...] = (gated * up_pre).astype(bf16)
    if count == 2:
        gate_slope, up_slope, picked = rest[1:4]
        gate_slope[...] = (up_pre * sigma * (1.0 + gate_pre * (1.0 - sigma))).astype(bf16)
        up_slope[...] = gated.astype(bf16)
        pick_rows(picked, scaled, z[0], 8)


def pick_rows(picked, source, z, groups):
    own = picked.shape[0] // groups
    for k in range(groups):
        start = pl.multiple_of((k * 4 + z) * own, 16)
        picked[k * own : (k + 1) * own, :] = source[pl.ds(start, own), :]


def forward(z, rows, gain, w_gate, w_up):
    count = len(rows)
    size, width = rows[0].shape
    units = w_gate.shape[0]
    tile = 256
    middle = size // tile
    total = count * size
    whole = lambda a: pl.BlockSpec(a.shape, lambda g: (0, 0), pipeline_mode=pl.Buffered(1))
    across = lambda n: pl.BlockSpec((n, tile), lambda g: (0, g))
    outs = [units] if count == 1 else [units, units, units, width // 4]
    row_specs = [
        pl.BlockSpec((tile, width), lambda g: (jnp.minimum(g, middle - 1), 0)),
        pl.BlockSpec((tile, width), lambda g: (jnp.maximum(g - middle, 0), 0)),
    ]
    return pl.pallas_call(
        functools.partial(forward_kernel, count),
        grid=(count * middle,),
        in_specs=[pl.BlockSpec(memory_space=pltpu.SMEM)]
        + row_specs[:count]
        + [whole(gain), whole(w_gate), whole(w_up)],
        out_specs=[across(n) for n in outs],
        out_shape=[jax.ShapeDtypeStruct((n, total), bf16) for n in outs],
        scratch_shapes=[pltpu.VMEM((width, tile), bf16)],
        compiler_params=pltpu.CompilerParams(
            dimension_semantics=("arbitrary",), vmem_limit_bytes=58 * 1024 * 1024
        ),
        cost_estimate=pl.CostEstimate(
            flops=4 * total * width * units,
            bytes_accessed=2 * total * width + 4 * width * units + 6 * total * units,
            transcendentals=total * units,
        ),
    )(z, *rows, gain, w_gate, w_up)


def pack_kernel(gram_a, gram_b, base, dispatch, out):
    steps, rows, _ = gram_a.shape
    row = lax.broadcasted_iota(jnp.int32, (rows, rows), 0)
    col = lax.broadcasted_iota(jnp.int32, (rows, rows), 1)
    lane = lax.broadcasted_iota(jnp.int32, (rows, 128), 1)
    same = row // MAXP == col // MAXP
    blocks = []
    for s in range(steps):
        gram = gram_a[s] + gram_b[s]
        block = base[s * rows : (s + 1) * rows, :]
        for k, (i, j) in enumerate(PAIRS):
            wanted = same & (row % MAXP == i) & (col % MAXP == j)
            value = jnp.sum(jnp.where(wanted, gram, 0.0), axis=1, keepdims=True)
            block = block + jnp.where(lane == k, value, 0.0)
        blocks.append(block)
    sent = jnp.dot(
        dispatch[...],
        jnp.concatenate(blocks, axis=0),
        precision=lax.Precision.HIGHEST,
        preferred_element_type=f32,
    )
    total = sent[:128]
    for q in range(1, 8):
        total = total + pltpu.roll(sent[q * 128 : (q + 1) * 128], 16 * q, 1)
    out[...] = total


def pack(gram_a, gram_b, base, dispatch):
    return pl.pallas_call(
        pack_kernel,
        in_specs=[pl.BlockSpec(memory_space=pltpu.VMEM)] * 4,
        out_specs=pl.BlockSpec(memory_space=pltpu.VMEM),
        out_shape=jax.ShapeDtypeStruct((128, 128), f32),
        compiler_params=pltpu.CompilerParams(vmem_limit_bytes=16 * 1024 * 1024),
        cost_estimate=pl.CostEstimate(
            flops=2 * 6 * 1024 * 128 * 128, bytes_accessed=1 << 20, transcendentals=0
        ),
    )(gram_a, gram_b, base, dispatch)


def hidden_kernel(rows_a, rows_b, ffn_a, ffn_b, turned, grams):
    @pl.when(pl.program_id(0) == 0)
    def _():
        grams[...] = jnp.zeros_like(grams)

    for c, (rows, ffn) in enumerate(((rows_a, ffn_a), (rows_b, ffn_b))):
        hidden = (rows[...].astype(f32) + ffn[...].astype(f32)).T
        size = hidden.shape[1] // MAXP
        turned[:, c * MAXP * size : (c + 1) * MAXP * size] = hidden.astype(bf16)
        cut = [hidden[:, i * size : (i + 1) * size] for i in range(MAXP)]
        for k, (i, j) in enumerate(PAIRS):
            grams[k : k + 1, c * size : (c + 1) * size] += jnp.sum(
                cut[i] * cut[j], axis=0, keepdims=True
            )


def hidden_parts(rows_a, rows_b, ffn_a, ffn_b):
    rows, width = rows_a.shape
    tile = 256
    spec = pl.BlockSpec((rows, tile), lambda g: (0, g))
    return pl.pallas_call(
        hidden_kernel,
        grid=(width // tile,),
        in_specs=[spec] * 4,
        out_specs=[
            pl.BlockSpec((tile, 2 * rows), lambda g: (g, 0)),
            pl.BlockSpec((16, 2 * rows // MAXP), lambda g: (0, 0)),
        ],
        out_shape=[
            jax.ShapeDtypeStruct((width, 2 * rows), bf16),
            jax.ShapeDtypeStruct((16, 2 * rows // MAXP), f32),
        ],
        compiler_params=pltpu.CompilerParams(
            dimension_semantics=("arbitrary",), vmem_limit_bytes=24 * 1024 * 1024
        ),
        cost_estimate=pl.CostEstimate(
            flops=24 * rows * width, bytes_accessed=12 * rows * width, transcendentals=0
        ),
    )(rows_a, rows_b, ffn_a, ffn_b)


def cosines(at, size):
    scales = [jnp.sqrt(at[i, i] / size + EPSILON) for i in range(MAXP)]
    return {(i, j): at[i, j] / (size * scales[i] * scales[j]) for i, j in PAIRS}, scales


def back_kernel(width, z, target, grams, turned, active, back, down, losses, factors, picked, held, sem):
    slots = target.shape[1]
    fetch = pltpu.make_async_copy(active, held, sem)

    @pl.when(pl.program_id(0) == 0)
    def _():
        fetch.start()

    @pl.when(pl.program_id(0) == 0)
    def _():
        row = lambda ref, k: ref[k : k + 1, :]
        wanted, _ = cosines({p: row(target, k) for k, p in enumerate(PAIRS)}, HQ * HEAD)
        have, scales = cosines({p: row(grams, k) for k, p in enumerate(PAIRS)}, width)
        count = row(target, len(PAIRS))
        alive = [jnp.where(count > i + 0.5, 1.0, 0.0) for i in range(MAXP)]
        bound = jnp.maximum(count, 1.0)
        over = 1.0 / (bound * bound)
        slope = {}
        loss = None
        for i, j in PAIRS:
            both = alive[i] * alive[j]
            differ = have[i, j] - wanted[i, j]
            slope[i, j] = slope[j, i] = 2.0 * both * differ * over
            term = (1.0 if i == j else 2.0) * both * differ * differ
            loss = term if loss is None else loss + term
        losses[...] = jnp.broadcast_to(loss * over, losses.shape)
        for i in range(MAXP):
            pull = sum(slope[i, j] * have[min(i, j), max(i, j)] for j in range(MAXP))
            for j in range(MAXP):
                term = slope[i, j] / (scales[i] * scales[j])
                if i == j:
                    term = term - pull / (scales[i] * scales[i])
                factors[i * MAXP + j : i * MAXP + j + 1, :] = 2.0 * term

    half = slots // 2
    for c in range(2):
        at = lambda i: slice((c * MAXP + i) * half, (c * MAXP + i + 1) * half)
        cut = [turned[:, at(i)].astype(f32) for i in range(MAXP)]
        for i in range(MAXP):
            mixed = None
            for j in range(MAXP):
                k = i * MAXP + j
                term = factors[k : k + 1, c * half : (c + 1) * half] * cut[j]
                mixed = term if mixed is None else mixed + term
            back[:, at(i)] = mixed.astype(bf16)
    step = pl.program_id(0)
    own = down.shape[1]
    group = back.shape[0] // 2
    for k in range(2):
        start = pl.multiple_of(k * group + z[0] * own, 16)
        to = pl.multiple_of((step * 2 + k) * own, 16)
        picked[pl.ds(to, own), :] = back[pl.ds(start, own), :]

    @pl.when(step == pl.num_programs(0) - 1)
    def _():
        fetch.wait()
        product = lax.dot_general(
            picked[...], held[...], (((1,), (1,)), ((), ())), preferred_element_type=f32
        ).astype(bf16)
        for k in range(down.shape[0]):
            down[k] = product[k * own : (k + 1) * own]


def pull_back(z, target, grams, turned, active):
    width, rows = turned.shape
    units = active.shape[0]
    own = width // 32
    tile = width // 4
    fixed = pl.BlockSpec(target.shape, lambda g: (0, 0))
    moving = lambda n: pl.BlockSpec((n, rows), lambda g: (g, 0))
    return pl.pallas_call(
        functools.partial(back_kernel, width),
        grid=(4,),
        in_specs=[
            pl.BlockSpec(memory_space=pltpu.SMEM),
            fixed,
            fixed,
            moving(tile),
            pl.BlockSpec(memory_space=pltpu.HBM),
        ],
        out_specs=[
            moving(tile),
            pl.BlockSpec((8, own, units), lambda g: (0, 0, 0)),
            pl.BlockSpec((8, target.shape[1]), lambda g: (0, 0)),
        ],
        out_shape=[
            jax.ShapeDtypeStruct((width, rows), bf16),
            jax.ShapeDtypeStruct((8, own, units), bf16),
            jax.ShapeDtypeStruct((8, target.shape[1]), f32),
        ],
        scratch_shapes=[
            pltpu.VMEM(target.shape, f32),
            pltpu.VMEM((8 * own, rows), bf16),
            pltpu.VMEM((units, rows), bf16),
            pltpu.SemaphoreType.DMA,
        ],
        compiler_params=pltpu.CompilerParams(
            dimension_semantics=("arbitrary",), vmem_limit_bytes=58 * 1024 * 1024
        ),
        cost_estimate=pl.CostEstimate(
            flops=8 * rows * width + 16 * own * rows * units, bytes_accessed=5 * rows * width, transcendentals=0
        ),
    )(z, target, grams, turned, active)


def inner_kernel(w_down, back, gate_slope, up_slope, gate_in, up_in):
    total = jnp.dot(w_down[...], back[...], preferred_element_type=f32)
    gate_in[...] = (total * gate_slope[...].astype(f32)).astype(bf16)
    up_in[...] = (total * up_slope[...].astype(f32)).astype(bf16)


def inner_grads(w_down, back, gate_slope, up_slope):
    units, width = w_down.shape
    rows = back.shape[1]
    tile = 256
    across = lambda n: pl.BlockSpec((n, tile), lambda g: (0, g))
    return pl.pallas_call(
        inner_kernel,
        grid=(rows // tile,),
        in_specs=[
            pl.BlockSpec(w_down.shape, lambda g: (0, 0), pipeline_mode=pl.Buffered(1)),
            across(width),
            across(units),
            across(units),
        ],
        out_specs=[across(units)] * 2,
        out_shape=[jax.ShapeDtypeStruct((units, rows), bf16)] * 2,
        compiler_params=pltpu.CompilerParams(
            dimension_semantics=("arbitrary",), vmem_limit_bytes=58 * 1024 * 1024
        ),
        cost_estimate=pl.CostEstimate(
            flops=2 * rows * width * units,
            bytes_accessed=2 * (rows * width + units * width + 4 * rows * units),
            transcendentals=0,
        ),
    )(w_down, back, gate_slope, up_slope)


def grad_kernel(picked, inner, *refs):
    out = refs[-1]
    product = lax.dot_general(
        picked[...], inner[...], (((1,), (1,)), ((), ())), preferred_element_type=f32
    ).astype(bf16)
    own = picked.shape[0] // out.shape[0]
    for k in range(out.shape[0]):
        out[k, :own] = product[k * own : (k + 1) * own]
        if len(refs) == 2:
            out[k, own:] = refs[0][k]


def weight_grad(picked, inner, *more):
    features, rows = picked.shape
    units = inner.shape[0]
    size = features // 8 + sum(a.shape[1] for a in more)
    return pl.pallas_call(
        grad_kernel,
        in_specs=[pl.BlockSpec(memory_space=pltpu.VMEM)] * (2 + len(more)),
        out_specs=pl.BlockSpec(memory_space=pltpu.VMEM),
        out_shape=jax.ShapeDtypeStruct((8, size, units), bf16),
        compiler_params=pltpu.CompilerParams(vmem_limit_bytes=32 * 1024 * 1024),
        cost_estimate=pl.CostEstimate(
            flops=2 * features * rows * units,
            bytes_accessed=2 * (features * rows + units * rows + features * units),
            transcendentals=0,
        ),
    )(picked, inner, *more)


def scatter_x(blocks, x, *deps):
    total = lax.dynamic_index_in_dim(blocks, x, 1, keepdims=False).astype(f32)
    outs = [lax.dynamic_index_in_dim(blocks, lax.rem(x + by, 4), 1, keepdims=False) for by in range(1, 4)]
    terms = tuple(shift(out, "x", by + 1) for by, out in enumerate(outs))
    if deps:
        terms = after(terms, *deps)
    for term in terms:
        total = total + term.astype(f32)
    return total


def scatter_y(blocks, yh):
    mine = lax.dynamic_index_in_dim(blocks, yh, 0, keepdims=False)
    out = lax.dynamic_index_in_dim(blocks, 1 - yh, 0, keepdims=False)
    return mine.astype(f32) + shift(out, "yh", 1).astype(f32)


def shards(
    teacher_states,
    teacher_gain,
    w_query,
    key_weight,
    value_weight,
    query_gain,
    key_gain,
    segments,
    passage_counts,
    swap_order,
    list_owner,
    student_rows,
    student_gain,
    w_gate,
    w_up,
    w_down,
):
    yh, x, z, yl, core = (lax.axis_index(a) for a in ALL)
    dp = (yh * 4 + x) * 4 + z
    lists, list_len = segments.shape
    slots = student_rows.shape[0]
    width = student_rows.shape[2]

    halves = jnp.swapaxes(student_rows.reshape(2, slots // 2, MAXP, width), 1, 2)
    own_rows = halves.reshape(slots * MAXP, width)
    half = own_rows.shape[0] // 2
    rows_half = lax.dynamic_slice_in_dim(own_rows, core * half, half, 0)
    rows_ring = ring_halves(rows_half, "z")

    depth = w_query.shape[0]
    row_gain = lax.dynamic_slice_in_dim(teacher_gain, dp * depth, depth, 0).astype(f32)[:, None]
    weights = jnp.concatenate([key_weight, value_weight, w_query], axis=1)
    weights = (weights.astype(f32) * row_gain).astype(bf16)
    across_y = shift(weights, "yh", 1)
    states = lax.all_gather(teacher_states, TP, axis=0, tiled=False)
    one = jnp.concatenate([weights[:FIRST], across_y[:FIRST]], axis=0)
    two = jnp.concatenate([weights[FIRST:], across_y[FIRST:]], axis=0)

    gain = student_gain.astype(f32)[None, :]
    z_at = z[None].astype(jnp.int32)
    (rows_now,) = after((own_rows,), rows_ring[1], rows_ring[2])
    (active_own,) = forward(z_at, (rows_now,), gain, w_gate.T, w_up.T)

    two_ring, one_ring = two_rings(two, one, *rows_ring, active_own)
    rows_mine = stack_slots(after(rows_ring, *one_ring[1:], *two_ring[1:]))
    rows_other = shift(rows_mine, "core", 1)
    line_z = stack_ring(one_ring, CHUNK)
    line_x = stack_ring(two_ring, CHUNK)

    def spread(k, *before):
        rings = two_rings(line_z[k], line_x[k], *before)
        return (*rings[0], *rings[1])

    partial = lax.dot_general(
        active_own, w_down, (((0,), (0,)), ((), ())), preferred_element_type=f32
    ).astype(bf16)
    kept = lax.dynamic_slice_in_dim(partial, core * half, half, 0).astype(f32)
    given = lax.dynamic_slice_in_dim(partial, (1 - core) * half, half, 0)
    pair_sum = (kept + shift(given, "core", 1).astype(f32)).astype(bf16)
    ffn_half = lax.psum(pair_sum, "yl")
    parts_a = spread(0, line_x[0], line_z[0], rows_other, pair_sum)

    active, gate_slope, up_slope, normed_pick = forward(
        z_at, (rows_mine, rows_other), gain, w_gate.T, w_up.T
    )
    parts_b = spread(1, *parts_a, active)

    owner = list_owner[:, 0]
    index = jnp.arange(lists, dtype=jnp.int32)
    earlier = jnp.sum(
        ((owner[None, :] == owner[:, None]) & (index[None, :] < index[:, None])).astype(jnp.int32),
        axis=1,
    )
    slot_of = owner * 2 + earlier
    select = (jnp.arange(slots, dtype=jnp.int32)[:, None] == slot_of[None, :]).astype(f32)
    per = slots // 2

    place = jnp.stack([yh, x, z]).astype(jnp.int32)
    q_tables = head_tables(query_gain, TOKENS_STEP, list_len)
    k_tables = head_tables(key_gain, TOKENS_STEP, list_len)
    spot = jnp.arange(MAXP, dtype=jnp.int32)
    live = spot[None, :] < passage_counts[:, None]
    member = (segments[:, None, :] == swap_order[:, :, None]) & live[:, :, None]
    tally = jnp.maximum(jnp.sum(member.astype(f32), axis=2), 1.0).reshape(lists * MAXP, 1)
    group = TOKENS_STEP // list_len
    same_list = jnp.eye(group, dtype=bool)
    spread_member = (
        member.reshape(lists // group, group, MAXP, 1, list_len)
        & same_list[None, :, None, :, None]
    )
    spread_member = spread_member.reshape(lists * MAXP, TOKENS_STEP).astype(bf16)
    gram_a, scale, keys, values = teacher_chunk(
        place, states, q_tables, k_tables, spread_member, tally, parts_a, 4, True, list_len
    )
    ffn_ring = ring(ffn_half, "z", *parts_b, gram_a)
    (gram_b,) = teacher_chunk(
        place, states, q_tables, (scale, keys, values), spread_member, tally, parts_b, 4, False, list_len
    )
    line = jnp.arange(1024, dtype=jnp.int32)
    rel, e, d8, z_to = line // 256, line // 128 % 2, line // 16 % 8, line // 4 % 4
    order = jnp.where(rel == 0, 0, jnp.where(rel == 1, 3, rel - 1))
    slot_to = (d8 * 4 + (z_to + order) % 4) * 2 + e
    dispatch = (slot_to[:, None] == jnp.repeat(slot_of, MAXP)[None, :]).astype(f32)
    counted = (jnp.arange(128)[None, None, :] == len(PAIRS)) & (spot[None, :, None] == 0)
    base = jnp.where(counted, 0.25 * passage_counts.astype(f32)[:, None, None], 0.0)
    send = pack(gram_a, gram_b, base.reshape(lists * MAXP, 128), dispatch)
    ffn_mine = stack_slots(after(ffn_ring, send))
    ffn_other = shift(ffn_mine, "core", 1)
    turned, grams = hidden_parts(rows_mine, rows_other, ffn_mine, ffn_other)

    got = lax.all_to_all(send, ALL, split_axis=0, concat_axis=0, tiled=True)
    got = jnp.sum(got.reshape(32, 4, 128), axis=1)
    got = got.reshape(2, 16, 4, 2, 16).transpose(4, 0, 2, 1, 3).reshape(16, 2, 4 * per)
    got = jnp.where(core == 0, got, got[:, ::-1]).reshape(16, 8 * per)

    back, grad_down, losses = pull_back(z_at, got, grams, turned, active)
    cut = lambda grad: grad.reshape(2, 4, *grad.shape[1:])
    slot_losses = losses[0].reshape(2, 4, 4, 4, 2)
    slot_losses = lax.dynamic_index_in_dim(slot_losses, z, 3, keepdims=False)
    slot_losses = jnp.where(core == 0, slot_losses, slot_losses[::-1])
    slot_losses = slot_losses.transpose(0, 2, 1, 3).reshape(8, 8)
    owners = (yh * 4 + x) * 4 + (z + jnp.array(AROUND)) % 4
    lanes = (owners[:, None] * 2 + jnp.arange(2)[None, :]).reshape(8)
    lane = jnp.arange(w_gate.shape[1], dtype=jnp.int32)
    spots = (lanes[:, None] == lane[None, :]).astype(f32)
    laid = jnp.sum(slot_losses[:, :, None] * spots[None], axis=1)
    terms, left = [], laid
    for _ in range(3):
        terms.append(left.astype(bf16))
        left = left - terms[-1].astype(f32)
    zeros = jnp.zeros((8, 13, lane.shape[0]), bf16)
    loss_rows = jnp.concatenate([jnp.stack(terms, axis=1), zeros], axis=1)
    down_x = scatter_x(cut(grad_down), x).astype(bf16)
    gate_in, up_in = inner_grads(w_down, back, gate_slope, up_slope)
    gate_in, up_in = after((gate_in, up_in), down_x)
    grad_gate = weight_grad(normed_pick, gate_in)
    gate_y = scatter_y(cut(grad_gate), yh).astype(bf16)
    (up_in,) = after((up_in,), grad_gate)
    grad_up = weight_grad(normed_pick, up_in, loss_rows)
    down_sum = scatter_y(down_x, yh)
    up_x = scatter_x(cut(grad_up), x, gate_y, down_sum).astype(bf16)
    gate_sum = scatter_x(gate_y[None], x)[0]
    up_sum = scatter_y(up_x, yh)

    returned = jnp.sum(up_sum[-16:, :slots], axis=0)
    list_loss = jnp.sum(select * returned[:, None], axis=0)
    return (list_loss, gate_sum, up_sum[:-16], down_sum.T)


def solution(mesh):
    fine = Mesh(mesh.devices.reshape(tuple(SIZES.values())), tuple(SIZES))
    placed = (
        P(DP, TP),
        P(),
        P(DP, TP),
        P(DP, TP),
        P(DP, TP),
        P(),
        P(),
        P(DP, None),
        P(DP),
        P(DP, None),
        P(DP, None),
        P(DP, None, None),
        P(),
        P(None, TP),
        P(None, TP),
        P(TP, None),
    )
    return jax.shard_map(
        shards,
        mesh=fine,
        in_specs=placed,
        out_specs=(P(DP), P(DP, TP), P(DP, TP), P(TP, DP)),
        check_vma=False,
    )
```

```python
import functools
import math

import jax
import jax.numpy as jnp
from jax import lax
from jax.experimental import pallas as pl
from jax.experimental.pallas import tpu as pltpu
from jax.sharding import Mesh
from jax.sharding import PartitionSpec as P

HQ = 32
HEAD = 128
MAXP = 4
EPSILON = 1e-06
ROPE_BASE = 1000000.0
DP = ("yh", "x", "z")
TP = ("yl", "core")
ALL = DP + TP
SIZES = {"yh": 2, "x": 4, "z": 4, "yl": 2, "core": 2}
PAIRS = [(i, j) for i in range(MAXP) for j in range(i, MAXP)]
FIRST = 80
CHUNK = 768
TOKENS_STEP = 512
AROUND = (0, 3, 1, 2)
bf16 = jnp.bfloat16
f32 = jnp.float32


def shift(value, axis, by):
    n = SIZES[axis]
    return lax.ppermute(value, axis, [(i, (i + by) % n) for i in range(n)])


def after(values, *deps):
    return lax.optimization_barrier((tuple(values), tuple(deps)))[0]


def ring_halves(block, axis, *deps):
    (block,) = after((block,), *deps)
    left, right = shift(block, axis, 1), shift(block, axis, -1)
    half = block.shape[0] // 2
    return block, left, right, shift(left[:half], axis, 1), shift(right[half:], axis, -1)


def ring(block, axis, *deps):
    (block,) = after((block,), *deps)
    return block, shift(block, axis, 1), shift(block, axis, -1), shift(block, axis, 2)


def two_rings(along_x, along_z, *deps, last=()):
    x0, z0 = after((along_x, along_z), *deps)
    (z_last,) = after((z0,), *last) if last else (z0,)
    x3, z3 = shift(x0, "x", 2), shift(z_last, "z", 2)
    x2, x1 = shift(x0, "x", -1), shift(x0, "x", 1)
    z2, z1 = shift(z0, "z", -1), shift(z0, "z", 1)
    return (x0, x1, x2, x3), (z0, z1, z2, z3)


def stack_kernel(moves, cuts, *refs):
    sources, outs = refs[: -len(cuts)], refs[-len(cuts) :]
    for i, at, n, to in moves:
        for out, (low, high) in zip(outs, cuts):
            out[to : to + n, :] = sources[i][at : at + n, low:high]


def stack(arrays, moves, cuts=None):
    rows, columns = sum(m[2] for m in moves), arrays[0].shape[1]
    cuts = cuts or [(0, columns)]
    return pl.pallas_call(
        functools.partial(stack_kernel, moves, cuts),
        in_specs=[pl.BlockSpec(memory_space=pltpu.VMEM)] * len(arrays),
        out_specs=[pl.BlockSpec(memory_space=pltpu.VMEM)] * len(cuts),
        out_shape=[jax.ShapeDtypeStruct((rows, c[1] - c[0]), arrays[0].dtype) for c in cuts],
        compiler_params=pltpu.CompilerParams(vmem_limit_bytes=24 * 1024 * 1024),
        cost_estimate=pl.CostEstimate(
            flops=0, bytes_accessed=4 * rows * columns, transcendentals=0
        ),
    )(*arrays)


def stack_ring(blocks, cut):
    n, columns = blocks[0].shape
    return stack(blocks, [(k, 0, n, k * n) for k in range(4)], [(0, cut), (cut, columns)])


def stack_slots(blocks):
    n = blocks[0].shape[0] // MAXP
    whole = 4 if len(blocks) == 4 else 3
    moves = [(k, p * n, n, (p * 4 + k) * n) for k in range(whole) for p in range(MAXP)]
    if whole == 3:
        moves += [(3 + p // 2, p % 2 * n, n, (p * 4 + 3) * n) for p in range(MAXP)]
    return stack(blocks, moves)[0]


def head_tables(gain, tokens, list_len):
    half = HEAD // 2
    positions = (jnp.arange(tokens, dtype=jnp.int32) % list_len).astype(f32)
    exponent = jnp.arange(half, dtype=f32) * (-2.0 / HEAD)
    angles = positions[:, None] * jnp.power(ROPE_BASE, exponent)[None, :]
    cosines, sines = jnp.cos(angles), jnp.sin(angles)
    same = jnp.concatenate([cosines, cosines], axis=1) * gain[None, :]
    crossed = jnp.concatenate([-sines, sines], axis=1) * jnp.roll(gain, half)[None, :]
    return same, crossed


def norm_rotate(values, same, crossed):
    mean = jnp.mean(values * values, axis=-1, keepdims=True)
    scaled = values * lax.rsqrt(mean + EPSILON)
    return (scaled * same + pltpu.roll(scaled, HEAD // 2, 1) * crossed).astype(bf16)


def teacher_kernel(heads, with_keys, list_len, *refs):
    place, states, q_same, q_cross = refs[:4]
    rest = refs[4:]
    if with_keys:
        k_same, k_cross = rest[:2]
        rest = rest[2:]
    else:
        scale_in, k_in, v_in = rest[:3]
        rest = rest[3:]
    member, tally = rest[:2]
    pieces = rest[2:10]
    rest = rest[10:]
    if with_keys:
        gram, scale_out, k_out, v_out, weights, sems = rest
    else:
        gram, weights, sems = rest

    @pl.when(pl.program_id(0) == 0)
    def _():
        yh, xx, zz = place[0], place[1], place[2]
        copies = []
        for part in range(2):
            base = part * FIRST
            for far in range(4):
                for near in range(4):
                    for h in range(2):
                        source = part * 4 + far
                        row = (near * 2 + h) * FIRST
                        rel_x, rel_z = (far, near) if part == 0 else (near, far)
                        x_at = lax.rem(xx + AROUND[rel_x], 4)
                        z_at = lax.rem(zz + AROUND[rel_z], 4)
                        y_at = lax.rem(yh + h, 2)
                        to = ((y_at * 4 + x_at) * 4 + z_at) * (2 * FIRST) + base
                        copies.append(
                            pltpu.make_async_copy(
                                pieces[source].at[pl.ds(row, FIRST), :],
                                weights.at[pl.ds(pl.multiple_of(to, 16), FIRST), :],
                                sems.at[len(copies)],
                            )
                        )
        for copy in copies:
            copy.start()
        for copy in copies:
            copy.wait()

    groups, _, width = states.shape
    total, squares = None, None
    for k in range(groups):
        piece = states[k]
        term = jnp.dot(
            piece, weights[k * width : (k + 1) * width, :], preferred_element_type=f32
        )
        total = term if total is None else total + term
        if with_keys:
            wide = piece.astype(f32)
            more = jnp.sum(wide * wide, axis=1, keepdims=True)
            squares = more if squares is None else squares + more
    if with_keys:
        scale = lax.rsqrt(squares / (groups * width) + EPSILON)
        scale_out[...] = scale
    else:
        scale = scale_in[...]
    total = total * scale
    if with_keys:
        keys = norm_rotate(total[:, :HEAD], k_same[...], k_cross[...])
        values = total[:, HEAD : 2 * HEAD].astype(bf16)
        k_out[...] = keys
        v_out[...] = values
        first = 2 * HEAD
    else:
        keys, values, first = k_in[...], v_in[...], 0
    tokens = total.shape[0]
    block = 128
    row = lax.broadcasted_iota(jnp.int32, (block, block), 0)
    col = lax.broadcasted_iota(jnp.int32, (block, block), 1)
    allowed = (col <= row) & (col // list_len == row // list_len)
    hide = jnp.where(allowed, 0.0, -1e30)
    ones = jnp.ones((block, HEAD), bf16)
    queries = [
        norm_rotate(total[:, first + h * HEAD : first + (h + 1) * HEAD], q_same[...], q_cross[...])
        for h in range(heads)
    ]
    mixed = []
    for s in range(tokens // block):
        part = slice(s * block, (s + 1) * block)
        stacked = jnp.concatenate([q[part] for q in queries], axis=0)
        scores = lax.dot_general(
            stacked, keys[part], (((1,), (1,)), ((), ())), preferred_element_type=f32
        )
        scores = scores.reshape(heads, block, block) * (1.0 / math.sqrt(HEAD)) + hide[None]
        shifted = jnp.exp(scores - jnp.max(scores, axis=-1, keepdims=True)).astype(bf16)
        summed = jnp.dot(
            shifted.reshape(heads * block, block),
            jnp.concatenate([values[part], ones], axis=1),
            preferred_element_type=f32,
        )
        result = (summed[:, :HEAD] / summed[:, HEAD:]).astype(bf16)
        mixed.append(
            jnp.concatenate([result[h * block : (h + 1) * block] for h in range(heads)], axis=1)
        )
    attended = jnp.concatenate(mixed, axis=0)
    pooled = jnp.dot(member[...], attended, preferred_element_type=f32)
    pooled = (pooled / tally[...]).astype(bf16)
    gram[0] = lax.dot_general(
        pooled, pooled, (((1,), (1,)), ((), ())), preferred_element_type=f32
    )


def teacher_chunk(place, states, q_tables, extra, member, tally, parts, heads, with_keys, list_len, span=None):
    groups, tokens, width = states.shape
    step = TOKENS_STEP
    first, steps = span or (0, tokens // step)
    tokens = steps * step
    lists = step // list_len
    rows = lists * MAXP
    columns = parts[0].shape[1]
    pieces = list(parts)
    block = lambda n, m: pl.BlockSpec((n, m), lambda g: (g, 0))
    later = lambda n, m: pl.BlockSpec((n, m), lambda g: (g + first, 0))
    fixed = lambda n, m: pl.BlockSpec((n, m), lambda g: (0, 0))
    extra_specs = [fixed(step, HEAD)] * 2
    if not with_keys:
        extra_specs = [block(step, 1)] + [block(step, HEAD)] * 2
    outs = [jax.ShapeDtypeStruct((tokens // step, rows, rows), f32)]
    out_specs = [pl.BlockSpec((1, rows, rows), lambda g: (g, 0, 0))]
    if with_keys:
        outs += [jax.ShapeDtypeStruct((tokens, 1), f32)]
        outs += [jax.ShapeDtypeStruct((tokens, HEAD), bf16)] * 2
        out_specs += [block(step, 1)] + [block(step, HEAD)] * 2
    depth = groups * width
    return pl.pallas_call(
        functools.partial(teacher_kernel, heads, with_keys, list_len),
        grid=(tokens // step,),
        in_specs=[
            pl.BlockSpec(memory_space=pltpu.SMEM),
            pl.BlockSpec((groups, step, width), lambda g: (0, g + first, 0)),
        ]
        + [fixed(step, HEAD)] * 2
        + extra_specs
        + [later(rows, step), later(rows, 1)]
        + [pl.BlockSpec(memory_space=pltpu.HBM)] * len(pieces),
        out_specs=out_specs,
        out_shape=outs,
        scratch_shapes=[
            pltpu.VMEM((depth, columns), bf16),
            pltpu.SemaphoreType.DMA((64,)),
        ],
        compiler_params=pltpu.CompilerParams(
            dimension_semantics=("arbitrary",), vmem_limit_bytes=58 * 1024 * 1024
        ),
        cost_estimate=pl.CostEstimate(
            flops=2 * tokens * depth * columns,
            bytes_accessed=2 * depth * (tokens + columns),
            transcendentals=tokens * 128 * heads,
        ),
    )(place, states, *q_tables, *extra, member, tally, *pieces)


def rms_scale(values, weights):
    return values * lax.rsqrt(jnp.mean(values * values, axis=-1, keepdims=True) + EPSILON) * weights


def forward_kernel(count, *refs):
    z, rows, (gain, w_gate, w_up), rest = refs[0], refs[1 : 1 + count], refs[1 + count : 4 + count], refs[4 + count :]
    values = rows[0][...]
    if count == 2:
        early = pl.program_id(0) < pl.num_programs(0) // 2
        values = jnp.where(early, values, rows[1][...])
    values = values.astype(f32)
    active, scaled = rest[0], rest[-1]
    scaled[...] = rms_scale(values, gain[...]).T.astype(bf16)
    gate_pre = jnp.dot(w_gate[...], scaled[...], preferred_element_type=f32)
    up_pre = jnp.dot(w_up[...], scaled[...], preferred_element_type=f32)
    sigma = jax.nn.sigmoid(gate_pre)
    gated = gate_pre * sigma
    active[...] = (gated * up_pre).astype(bf16)
    if count == 2:
        gate_slope, up_slope, picked = rest[1:4]
        gate_slope[...] = (up_pre * sigma * (1.0 + gate_pre * (1.0 - sigma))).astype(bf16)
        up_slope[...] = gated.astype(bf16)
        pick_rows(picked, scaled, z[0], 8)


def pick_rows(picked, source, z, groups):
    own = picked.shape[0] // groups
    for k in range(groups):
        start = pl.multiple_of((k * 4 + z) * own, 16)
        picked[k * own : (k + 1) * own, :] = source[pl.ds(start, own), :]


def forward(z, rows, gain, w_gate, w_up):
    count = len(rows)
    size, width = rows[0].shape
    units = w_gate.shape[0]
    tile = 256
    middle = size // tile
    total = count * size
    whole = lambda a: pl.BlockSpec(a.shape, lambda g: (0, 0), pipeline_mode=pl.Buffered(1))
    across = lambda n: pl.BlockSpec((n, tile), lambda g: (0, g))
    outs = [units] if count == 1 else [units, units, units, width // 4]
    row_specs = [
        pl.BlockSpec((tile, width), lambda g: (jnp.minimum(g, middle - 1), 0)),
        pl.BlockSpec((tile, width), lambda g: (jnp.maximum(g - middle, 0), 0)),
    ]
    return pl.pallas_call(
        functools.partial(forward_kernel, count),
        grid=(count * middle,),
        in_specs=[pl.BlockSpec(memory_space=pltpu.SMEM)]
        + row_specs[:count]
        + [whole(gain), whole(w_gate), whole(w_up)],
        out_specs=[across(n) for n in outs],
        out_shape=[jax.ShapeDtypeStruct((n, total), bf16) for n in outs],
        scratch_shapes=[pltpu.VMEM((width, tile), bf16)],
        compiler_params=pltpu.CompilerParams(
            dimension_semantics=("arbitrary",), vmem_limit_bytes=58 * 1024 * 1024
        ),
        cost_estimate=pl.CostEstimate(
            flops=4 * total * width * units,
            bytes_accessed=2 * total * width + 4 * width * units + 6 * total * units,
            transcendentals=total * units,
        ),
    )(z, *rows, gain, w_gate, w_up)


def pack_kernel(gram_a, gram_b, base, dispatch, out):
    steps, rows, _ = gram_a.shape
    row = lax.broadcasted_iota(jnp.int32, (rows, rows), 0)
    col = lax.broadcasted_iota(jnp.int32, (rows, rows), 1)
    lane = lax.broadcasted_iota(jnp.int32, (rows, 128), 1)
    same = row // MAXP == col // MAXP
    blocks = []
    for s in range(steps):
        gram = gram_a[s] + gram_b[s]
        block = base[s * rows : (s + 1) * rows, :]
        for k, (i, j) in enumerate(PAIRS):
            wanted = same & (row % MAXP == i) & (col % MAXP == j)
            value = jnp.sum(jnp.where(wanted, gram, 0.0), axis=1, keepdims=True)
            block = block + jnp.where(lane == k, value, 0.0)
        blocks.append(block)
    sent = jnp.dot(
        dispatch[...],
        jnp.concatenate(blocks, axis=0),
        precision=lax.Precision.HIGHEST,
        preferred_element_type=f32,
    )
    total = sent[:128]
    for q in range(1, 8):
        total = total + pltpu.roll(sent[q * 128 : (q + 1) * 128], 16 * q, 1)
    out[...] = total


def pack(gram_a, gram_b, base, dispatch):
    return pl.pallas_call(
        pack_kernel,
        in_specs=[pl.BlockSpec(memory_space=pltpu.VMEM)] * 4,
        out_specs=pl.BlockSpec(memory_space=pltpu.VMEM),
        out_shape=jax.ShapeDtypeStruct((128, 128), f32),
        compiler_params=pltpu.CompilerParams(vmem_limit_bytes=16 * 1024 * 1024),
        cost_estimate=pl.CostEstimate(
            flops=2 * 6 * 1024 * 128 * 128, bytes_accessed=1 << 20, transcendentals=0
        ),
    )(gram_a, gram_b, base, dispatch)


def hidden_kernel(rows_a, rows_b, ffn_a, ffn_b, turned, grams):
    @pl.when(pl.program_id(0) == 0)
    def _():
        grams[...] = jnp.zeros_like(grams)

    for c, (rows, ffn) in enumerate(((rows_a, ffn_a), (rows_b, ffn_b))):
        hidden = (rows[...].astype(f32) + ffn[...].astype(f32)).T
        size = hidden.shape[1] // MAXP
        turned[:, c * MAXP * size : (c + 1) * MAXP * size] = hidden.astype(bf16)
        cut = [hidden[:, i * size : (i + 1) * size] for i in range(MAXP)]
        for k, (i, j) in enumerate(PAIRS):
            grams[k : k + 1, c * size : (c + 1) * size] += jnp.sum(
                cut[i] * cut[j], axis=0, keepdims=True
            )


def hidden_parts(rows_a, rows_b, ffn_a, ffn_b):
    rows, width = rows_a.shape
    tile = 256
    spec = pl.BlockSpec((rows, tile), lambda g: (0, g))
    return pl.pallas_call(
        hidden_kernel,
        grid=(width // tile,),
        in_specs=[spec] * 4,
        out_specs=[
            pl.BlockSpec((tile, 2 * rows), lambda g: (g, 0)),
            pl.BlockSpec((16, 2 * rows // MAXP), lambda g: (0, 0)),
        ],
        out_shape=[
            jax.ShapeDtypeStruct((width, 2 * rows), bf16),
            jax.ShapeDtypeStruct((16, 2 * rows // MAXP), f32),
        ],
        compiler_params=pltpu.CompilerParams(
            dimension_semantics=("arbitrary",), vmem_limit_bytes=24 * 1024 * 1024
        ),
        cost_estimate=pl.CostEstimate(
            flops=24 * rows * width, bytes_accessed=12 * rows * width, transcendentals=0
        ),
    )(rows_a, rows_b, ffn_a, ffn_b)


def cosines(at, size):
    scales = [jnp.sqrt(at[i, i] / size + EPSILON) for i in range(MAXP)]
    return {(i, j): at[i, j] / (size * scales[i] * scales[j]) for i, j in PAIRS}, scales


def back_kernel(width, z, target, grams, turned, active, back, down, losses, factors, picked, held, sem):
    slots = target.shape[1]
    fetch = pltpu.make_async_copy(active, held, sem)

    @pl.when(pl.program_id(0) == 0)
    def _():
        fetch.start()

    @pl.when(pl.program_id(0) == 0)
    def _():
        row = lambda ref, k: ref[k : k + 1, :]
        wanted, _ = cosines({p: row(target, k) for k, p in enumerate(PAIRS)}, HQ * HEAD)
        have, scales = cosines({p: row(grams, k) for k, p in enumerate(PAIRS)}, width)
        count = row(target, len(PAIRS))
        alive = [jnp.where(count > i + 0.5, 1.0, 0.0) for i in range(MAXP)]
        bound = jnp.maximum(count, 1.0)
        over = 1.0 / (bound * bound)
        slope = {}
        loss = None
        for i, j in PAIRS:
            both = alive[i] * alive[j]
            differ = have[i, j] - wanted[i, j]
            slope[i, j] = slope[j, i] = 2.0 * both * differ * over
            term = (1.0 if i == j else 2.0) * both * differ * differ
            loss = term if loss is None else loss + term
        losses[...] = jnp.broadcast_to(loss * over, losses.shape)
        for i in range(MAXP):
            pull = sum(slope[i, j] * have[min(i, j), max(i, j)] for j in range(MAXP))
            for j in range(MAXP):
                term = slope[i, j] / (scales[i] * scales[j])
                if i == j:
                    term = term - pull / (scales[i] * scales[i])
                factors[i * MAXP + j : i * MAXP + j + 1, :] = 2.0 * term

    half = slots // 2
    for c in range(2):
        at = lambda i: slice((c * MAXP + i) * half, (c * MAXP + i + 1) * half)
        cut = [turned[:, at(i)].astype(f32) for i in range(MAXP)]
        for i in range(MAXP):
            mixed = None
            for j in range(MAXP):
                k = i * MAXP + j
                term = factors[k : k + 1, c * half : (c + 1) * half] * cut[j]
                mixed = term if mixed is None else mixed + term
            back[:, at(i)] = mixed.astype(bf16)
    step = pl.program_id(0)
    own = down.shape[1]
    group = back.shape[0] // 2
    for k in range(2):
        start = pl.multiple_of(k * group + z[0] * own, 16)
        to = pl.multiple_of((step * 2 + k) * own, 16)
        picked[pl.ds(to, own), :] = back[pl.ds(start, own), :]

    @pl.when(step == pl.num_programs(0) - 1)
    def _():
        fetch.wait()
        product = lax.dot_general(
            picked[...], held[...], (((1,), (1,)), ((), ())), preferred_element_type=f32
        ).astype(bf16)
        for k in range(down.shape[0]):
            down[k] = product[k * own : (k + 1) * own]


def pull_back(z, target, grams, turned, active):
    width, rows = turned.shape
    units = active.shape[0]
    own = width // 32
    tile = width // 4
    fixed = pl.BlockSpec(target.shape, lambda g: (0, 0))
    moving = lambda n: pl.BlockSpec((n, rows), lambda g: (g, 0))
    return pl.pallas_call(
        functools.partial(back_kernel, width),
        grid=(4,),
        in_specs=[
            pl.BlockSpec(memory_space=pltpu.SMEM),
            fixed,
            fixed,
            moving(tile),
            pl.BlockSpec(memory_space=pltpu.HBM),
        ],
        out_specs=[
            moving(tile),
            pl.BlockSpec((8, own, units), lambda g: (0, 0, 0)),
            pl.BlockSpec((8, target.shape[1]), lambda g: (0, 0)),
        ],
        out_shape=[
            jax.ShapeDtypeStruct((width, rows), bf16),
            jax.ShapeDtypeStruct((8, own, units), bf16),
            jax.ShapeDtypeStruct((8, target.shape[1]), f32),
        ],
        scratch_shapes=[
            pltpu.VMEM(target.shape, f32),
            pltpu.VMEM((8 * own, rows), bf16),
            pltpu.VMEM((units, rows), bf16),
            pltpu.SemaphoreType.DMA,
        ],
        compiler_params=pltpu.CompilerParams(
            dimension_semantics=("arbitrary",), vmem_limit_bytes=32 * 1024 * 1024
        ),
        cost_estimate=pl.CostEstimate(
            flops=8 * rows * width + 16 * own * rows * units, bytes_accessed=5 * rows * width, transcendentals=0
        ),
    )(z, target, grams, turned, active)


def inner_kernel(w_down, back, gate_slope, up_slope, gate_in, up_in):
    total = jnp.dot(w_down[...], back[...], preferred_element_type=f32)
    gate_in[...] = (total * gate_slope[...].astype(f32)).astype(bf16)
    up_in[...] = (total * up_slope[...].astype(f32)).astype(bf16)


def inner_grads(w_down, back, gate_slope, up_slope):
    units, width = w_down.shape
    rows = back.shape[1]
    tile = 256
    across = lambda n: pl.BlockSpec((n, tile), lambda g: (0, g))
    return pl.pallas_call(
        inner_kernel,
        grid=(rows // tile,),
        in_specs=[
            pl.BlockSpec(w_down.shape, lambda g: (0, 0), pipeline_mode=pl.Buffered(1)),
            across(width),
            across(units),
            across(units),
        ],
        out_specs=[across(units)] * 2,
        out_shape=[jax.ShapeDtypeStruct((units, rows), bf16)] * 2,
        compiler_params=pltpu.CompilerParams(
            dimension_semantics=("arbitrary",), vmem_limit_bytes=58 * 1024 * 1024
        ),
        cost_estimate=pl.CostEstimate(
            flops=2 * rows * width * units,
            bytes_accessed=2 * (rows * width + units * width + 4 * rows * units),
            transcendentals=0,
        ),
    )(w_down, back, gate_slope, up_slope)


def grad_kernel(picked, inner, *refs):
    out = refs[-1]
    product = lax.dot_general(
        picked[...], inner[...], (((1,), (1,)), ((), ())), preferred_element_type=f32
    ).astype(bf16)
    own = picked.shape[0] // out.shape[0]
    for k in range(out.shape[0]):
        out[k, :own] = product[k * own : (k + 1) * own]
        if len(refs) == 2:
            out[k, own:] = refs[0][k]


def weight_grad(picked, inner, *more):
    features, rows = picked.shape
    units = inner.shape[0]
    size = features // 8 + sum(a.shape[1] for a in more)
    return pl.pallas_call(
        grad_kernel,
        in_specs=[pl.BlockSpec(memory_space=pltpu.VMEM)] * (2 + len(more)),
        out_specs=pl.BlockSpec(memory_space=pltpu.VMEM),
        out_shape=jax.ShapeDtypeStruct((8, size, units), bf16),
        compiler_params=pltpu.CompilerParams(vmem_limit_bytes=32 * 1024 * 1024),
        cost_estimate=pl.CostEstimate(
            flops=2 * features * rows * units,
            bytes_accessed=2 * (features * rows + units * rows + features * units),
            transcendentals=0,
        ),
    )(picked, inner, *more)


def send_x(blocks, x):
    own = lax.dynamic_index_in_dim(blocks, x, 1, keepdims=False)
    outs = [lax.dynamic_index_in_dim(blocks, lax.rem(x + by, 4), 1, keepdims=False) for by in range(1, 4)]
    return (own, *(shift(out, "x", by + 1) for by, out in enumerate(outs)))


def add_up(terms):
    total = terms[0].astype(f32)
    for term in terms[1:]:
        total = total + term.astype(f32)
    return total


def scatter_y(blocks, yh, *deps):
    mine = lax.dynamic_index_in_dim(blocks, yh, 0, keepdims=False)
    out = lax.dynamic_index_in_dim(blocks, 1 - yh, 0, keepdims=False)
    came = shift(out, "yh", 1)
    if deps:
        (came,) = after((came,), *deps)
    return mine.astype(f32) + came.astype(f32)


def shards(
    teacher_states,
    teacher_gain,
    w_query,
    key_weight,
    value_weight,
    query_gain,
    key_gain,
    segments,
    passage_counts,
    swap_order,
    list_owner,
    student_rows,
    student_gain,
    w_gate,
    w_up,
    w_down,
):
    yh, x, z, yl, core = (lax.axis_index(a) for a in ALL)
    dp = (yh * 4 + x) * 4 + z
    lists, list_len = segments.shape
    slots = student_rows.shape[0]
    width = student_rows.shape[2]

    halves = jnp.swapaxes(student_rows.reshape(2, slots // 2, MAXP, width), 1, 2)
    own_rows = halves.reshape(slots * MAXP, width)
    half = own_rows.shape[0] // 2
    rows_half = lax.dynamic_slice_in_dim(own_rows, core * half, half, 0)
    rows_ring = ring_halves(rows_half, "z")

    depth = w_query.shape[0]
    row_gain = lax.dynamic_slice_in_dim(teacher_gain, dp * depth, depth, 0).astype(f32)[:, None]
    weights = jnp.concatenate([key_weight, value_weight, w_query], axis=1)
    weights = (weights.astype(f32) * row_gain).astype(bf16)
    across_y = shift(weights, "yh", 1)
    states = lax.all_gather(teacher_states, TP, axis=0, tiled=False)
    one = jnp.concatenate([weights[:FIRST], across_y[:FIRST]], axis=0)
    two = jnp.concatenate([weights[FIRST:], across_y[FIRST:]], axis=0)

    gain = student_gain.astype(f32)[None, :]
    z_at = z[None].astype(jnp.int32)
    (active_own,) = forward(z_at, (own_rows,), gain, w_gate.T, w_up.T)

    partial = lax.dot_general(
        active_own, w_down, (((0,), (0,)), ((), ())), preferred_element_type=f32
    ).astype(bf16)
    kept = lax.dynamic_slice_in_dim(partial, core * half, half, 0).astype(f32)
    given = lax.dynamic_slice_in_dim(partial, (1 - core) * half, half, 0)
    pair_sum = (kept + shift(given, "core", 1).astype(f32)).astype(bf16)
    two_ring, one_ring = two_rings(two, one, *rows_ring, pair_sum)
    rows_mine = stack_slots(after(rows_ring, *one_ring[1:], *two_ring[1:]))
    rows_other = shift(rows_mine, "core", 1)
    line_z = stack_ring(one_ring, CHUNK)
    line_x = stack_ring(two_ring, CHUNK)

    def spread(k, *before, last=()):
        rings = two_rings(line_z[k], line_x[k], *before, last=last)
        return (*rings[0], *rings[1])

    ffn_half = lax.psum(pair_sum, "yl")
    parts_a = spread(0, line_x[0], line_z[0], rows_other)

    active, gate_slope, up_slope, normed_pick = forward(
        z_at, (rows_mine, rows_other), gain, w_gate.T, w_up.T
    )

    owner = list_owner[:, 0]
    index = jnp.arange(lists, dtype=jnp.int32)
    earlier = jnp.sum(
        ((owner[None, :] == owner[:, None]) & (index[None, :] < index[:, None])).astype(jnp.int32),
        axis=1,
    )
    slot_of = owner * 2 + earlier
    select = (jnp.arange(slots, dtype=jnp.int32)[:, None] == slot_of[None, :]).astype(f32)
    per = slots // 2

    place = jnp.stack([yh, x, z]).astype(jnp.int32)
    q_tables = head_tables(query_gain, TOKENS_STEP, list_len)
    k_tables = head_tables(key_gain, TOKENS_STEP, list_len)
    spot = jnp.arange(MAXP, dtype=jnp.int32)
    live = spot[None, :] < passage_counts[:, None]
    member = (segments[:, None, :] == swap_order[:, :, None]) & live[:, :, None]
    tally = jnp.maximum(jnp.sum(member.astype(f32), axis=2), 1.0).reshape(lists * MAXP, 1)
    group = TOKENS_STEP // list_len
    same_list = jnp.eye(group, dtype=bool)
    spread_member = (
        member.reshape(lists // group, group, MAXP, 1, list_len)
        & same_list[None, :, None, :, None]
    )
    spread_member = spread_member.reshape(lists * MAXP, TOKENS_STEP).astype(bf16)
    halves_a = [
        teacher_chunk(
            place, states, q_tables, k_tables, spread_member, tally, parts_a, 4, True, list_len, (k, 1)
        )
        for k in range(2)
    ]
    gram_a, scale, keys, values = (jnp.concatenate(pair, axis=0) for pair in zip(*halves_a))
    parts_b = spread(1, *parts_a, active, last=(halves_a[0][0],))
    ffn_ring = ring(ffn_half, "z", *parts_b, halves_a[1][0])
    (gram_b,) = teacher_chunk(
        place, states, q_tables, (scale, keys, values), spread_member, tally, parts_b, 4, False, list_len
    )
    line = jnp.arange(1024, dtype=jnp.int32)
    rel, e, d8, z_to = line // 256, line // 128 % 2, line // 16 % 8, line // 4 % 4
    order = jnp.where(rel == 0, 0, jnp.where(rel == 1, 3, rel - 1))
    slot_to = (d8 * 4 + (z_to + order) % 4) * 2 + e
    dispatch = (slot_to[:, None] == jnp.repeat(slot_of, MAXP)[None, :]).astype(f32)
    counted = (jnp.arange(128)[None, None, :] == len(PAIRS)) & (spot[None, :, None] == 0)
    base = jnp.where(counted, 0.25 * passage_counts.astype(f32)[:, None, None], 0.0)
    send = pack(gram_a, gram_b, base.reshape(lists * MAXP, 128), dispatch)
    ffn_mine = stack_slots(after(ffn_ring, send))
    ffn_other = shift(ffn_mine, "core", 1)
    turned, grams = hidden_parts(rows_mine, rows_other, ffn_mine, ffn_other)

    got = lax.all_to_all(send, ALL, split_axis=0, concat_axis=0, tiled=True)
    got = jnp.sum(got.reshape(32, 4, 128), axis=1)
    got = got.reshape(2, 16, 4, 2, 16).transpose(4, 0, 2, 1, 3).reshape(16, 2, 4 * per)
    got = jnp.where(core == 0, got, got[:, ::-1]).reshape(16, 8 * per)

    back, grad_down, losses = pull_back(z_at, got, grams, turned, active)
    cut = lambda grad: grad.reshape(2, 4, *grad.shape[1:])
    slot_losses = losses[0].reshape(2, 4, 4, 4, 2)
    slot_losses = lax.dynamic_index_in_dim(slot_losses, z, 3, keepdims=False)
    slot_losses = jnp.where(core == 0, slot_losses, slot_losses[::-1])
    slot_losses = slot_losses.transpose(0, 2, 1, 3).reshape(8, 8)
    owners = (yh * 4 + x) * 4 + (z + jnp.array(AROUND)) % 4
    lanes = (owners[:, None] * 2 + jnp.arange(2)[None, :]).reshape(8)
    lane = jnp.arange(w_gate.shape[1], dtype=jnp.int32)
    spots = (lanes[:, None] == lane[None, :]).astype(f32)
    laid = jnp.sum(slot_losses[:, :, None] * spots[None], axis=1)
    terms, left = [], laid
    for _ in range(3):
        terms.append(left.astype(bf16))
        left = left - terms[-1].astype(f32)
    zeros = jnp.zeros((8, 13, lane.shape[0]), bf16)
    loss_rows = jnp.concatenate([jnp.stack(terms, axis=1), zeros], axis=1)
    down_terms = send_x(cut(grad_down), x)
    gate_in, up_in = inner_grads(w_down, back, gate_slope, up_slope)
    (up_in,) = after((up_in,), down_terms[3])
    grad_up = weight_grad(normed_pick, up_in, loss_rows)
    up_terms = send_x(cut(grad_up), x)
    (gate_in,) = after((gate_in,), grad_up)
    grad_gate = weight_grad(normed_pick, gate_in)
    gate_y = scatter_y(cut(grad_gate), yh).astype(bf16)
    down_sum = scatter_y(add_up(down_terms).astype(bf16), yh, gate_y)
    up_sum = scatter_y(add_up(up_terms).astype(bf16), yh, gate_y)
    gate_sum = add_up(send_x(gate_y[None], x))[0]

    returned = jnp.sum(up_sum[-16:, :slots], axis=0)
    list_loss = jnp.sum(select * returned[:, None], axis=0)
    return (list_loss, gate_sum, up_sum[:-16], down_sum.T)


def solution(mesh):
    fine = Mesh(mesh.devices.reshape(tuple(SIZES.values())), tuple(SIZES))
    placed = (
        P(DP, TP),
        P(),
        P(DP, TP),
        P(DP, TP),
        P(DP, TP),
        P(),
        P(),
        P(DP, None),
        P(DP),
        P(DP, None),
        P(DP, None),
        P(DP, None, None),
        P(),
        P(None, TP),
        P(None, TP),
        P(TP, None),
    )
    return jax.shard_map(
        shards,
        mesh=fine,
        in_specs=placed,
        out_specs=(P(DP), P(DP, TP), P(DP, TP), P(TP, DP)),
        check_vma=False,
    )
```

```python
import functools
import math

import jax
import jax.numpy as jnp
from jax import lax
from jax.experimental import pallas as pl
from jax.experimental.pallas import tpu as pltpu
from jax.sharding import Mesh
from jax.sharding import PartitionSpec as P

HQ = 32
HEAD = 128
MAXP = 4
EPSILON = 1e-06
ROPE_BASE = 1000000.0
DP = ("yh", "x", "z")
TP = ("yl", "core")
ALL = DP + TP
SIZES = {"yh": 2, "x": 4, "z": 4, "yl": 2, "core": 2}
PAIRS = [(i, j) for i in range(MAXP) for j in range(i, MAXP)]
FIRST = 80
CHUNK = 768
TOKENS_STEP = 512
AROUND = (0, 3, 1, 2)
bf16 = jnp.bfloat16
f32 = jnp.float32


def shift(value, axis, by):
    n = SIZES[axis]
    return lax.ppermute(value, axis, [(i, (i + by) % n) for i in range(n)])


def after(values, *deps):
    return lax.optimization_barrier((tuple(values), tuple(deps)))[0]


def ring_halves(block, axis, *deps):
    (block,) = after((block,), *deps)
    left, right = shift(block, axis, 1), shift(block, axis, -1)
    half = block.shape[0] // 2
    return block, left, right, shift(left[:half], axis, 1), shift(right[half:], axis, -1)


def ring(block, axis, *deps):
    (block,) = after((block,), *deps)
    return block, shift(block, axis, 1), shift(block, axis, -1), shift(block, axis, 2)


def two_rings(along_x, along_z, *deps, last=()):
    x0, z0 = after((along_x, along_z), *deps)
    (z_last,) = after((z0,), *last) if last else (z0,)
    x3, z3 = shift(x0, "x", 2), shift(z_last, "z", 2)
    x2, x1 = shift(x0, "x", -1), shift(x0, "x", 1)
    z2, z1 = shift(z0, "z", -1), shift(z0, "z", 1)
    return (x0, x1, x2, x3), (z0, z1, z2, z3)


def stack_kernel(moves, cuts, *refs):
    sources, outs = refs[: -len(cuts)], refs[-len(cuts) :]
    for i, at, n, to in moves:
        for out, (low, high) in zip(outs, cuts):
            out[to : to + n, :] = sources[i][at : at + n, low:high]


def stack(arrays, moves, cuts=None):
    rows, columns = sum(m[2] for m in moves), arrays[0].shape[1]
    cuts = cuts or [(0, columns)]
    return pl.pallas_call(
        functools.partial(stack_kernel, moves, cuts),
        in_specs=[pl.BlockSpec(memory_space=pltpu.VMEM)] * len(arrays),
        out_specs=[pl.BlockSpec(memory_space=pltpu.VMEM)] * len(cuts),
        out_shape=[jax.ShapeDtypeStruct((rows, c[1] - c[0]), arrays[0].dtype) for c in cuts],
        compiler_params=pltpu.CompilerParams(vmem_limit_bytes=24 * 1024 * 1024),
        cost_estimate=pl.CostEstimate(
            flops=0, bytes_accessed=4 * rows * columns, transcendentals=0
        ),
    )(*arrays)


def stack_ring(blocks, cut):
    n, columns = blocks[0].shape
    return stack(blocks, [(k, 0, n, k * n) for k in range(4)], [(0, cut), (cut, columns)])


def stack_slots(blocks):
    n = blocks[0].shape[0] // MAXP
    whole = 4 if len(blocks) == 4 else 3
    moves = [(k, p * n, n, (p * 4 + k) * n) for k in range(whole) for p in range(MAXP)]
    if whole == 3:
        moves += [(3 + p // 2, p % 2 * n, n, (p * 4 + 3) * n) for p in range(MAXP)]
    return stack(blocks, moves)[0]


def head_tables(gain, tokens, list_len):
    half = HEAD // 2
    positions = (jnp.arange(tokens, dtype=jnp.int32) % list_len).astype(f32)
    exponent = jnp.arange(half, dtype=f32) * (-2.0 / HEAD)
    angles = positions[:, None] * jnp.power(ROPE_BASE, exponent)[None, :]
    cosines, sines = jnp.cos(angles), jnp.sin(angles)
    same = jnp.concatenate([cosines, cosines], axis=1) * gain[None, :]
    crossed = jnp.concatenate([-sines, sines], axis=1) * jnp.roll(gain, half)[None, :]
    return same, crossed


def norm_rotate(values, same, crossed):
    mean = jnp.mean(values * values, axis=-1, keepdims=True)
    scaled = values * lax.rsqrt(mean + EPSILON)
    return (scaled * same + pltpu.roll(scaled, HEAD // 2, 1) * crossed).astype(bf16)


def teacher_kernel(heads, with_keys, list_len, *refs):
    place, states, q_same, q_cross = refs[:4]
    rest = refs[4:]
    if with_keys:
        k_same, k_cross = rest[:2]
        rest = rest[2:]
    else:
        scale_in, k_in, v_in = rest[:3]
        rest = rest[3:]
    member, tally = rest[:2]
    pieces = rest[2:10]
    rest = rest[10:]
    if with_keys:
        gram, scale_out, k_out, v_out, weights, sems = rest
    else:
        gram, weights, sems = rest

    @pl.when(pl.program_id(0) == 0)
    def _():
        yh, xx, zz = place[0], place[1], place[2]
        copies = []
        for part in range(2):
            base = part * FIRST
            for far in range(4):
                for near in range(4):
                    for h in range(2):
                        source = part * 4 + far
                        row = (near * 2 + h) * FIRST
                        rel_x, rel_z = (far, near) if part == 0 else (near, far)
                        x_at = lax.rem(xx + AROUND[rel_x], 4)
                        z_at = lax.rem(zz + AROUND[rel_z], 4)
                        y_at = lax.rem(yh + h, 2)
                        to = ((y_at * 4 + x_at) * 4 + z_at) * (2 * FIRST) + base
                        copies.append(
                            pltpu.make_async_copy(
                                pieces[source].at[pl.ds(row, FIRST), :],
                                weights.at[pl.ds(pl.multiple_of(to, 16), FIRST), :],
                                sems.at[len(copies)],
                            )
                        )
        for copy in copies:
            copy.start()
        for copy in copies:
            copy.wait()

    groups, _, width = states.shape
    total, squares = None, None
    for k in range(groups):
        piece = states[k]
        term = jnp.dot(
            piece, weights[k * width : (k + 1) * width, :], preferred_element_type=f32
        )
        total = term if total is None else total + term
        if with_keys:
            wide = piece.astype(f32)
            more = jnp.sum(wide * wide, axis=1, keepdims=True)
            squares = more if squares is None else squares + more
    if with_keys:
        scale = lax.rsqrt(squares / (groups * width) + EPSILON)
        scale_out[...] = scale
    else:
        scale = scale_in[...]
    total = total * scale
    if with_keys:
        keys = norm_rotate(total[:, :HEAD], k_same[...], k_cross[...])
        values = total[:, HEAD : 2 * HEAD].astype(bf16)
        k_out[...] = keys
        v_out[...] = values
        first = 2 * HEAD
    else:
        keys, values, first = k_in[...], v_in[...], 0
    tokens = total.shape[0]
    block = 128
    row = lax.broadcasted_iota(jnp.int32, (block, block), 0)
    col = lax.broadcasted_iota(jnp.int32, (block, block), 1)
    allowed = (col <= row) & (col // list_len == row // list_len)
    hide = jnp.where(allowed, 0.0, -1e30)
    ones = jnp.ones((block, HEAD), bf16)
    queries = [
        norm_rotate(total[:, first + h * HEAD : first + (h + 1) * HEAD], q_same[...], q_cross[...])
        for h in range(heads)
    ]
    mixed = []
    for s in range(tokens // block):
        part = slice(s * block, (s + 1) * block)
        stacked = jnp.concatenate([q[part] for q in queries], axis=0)
        scores = lax.dot_general(
            stacked, keys[part], (((1,), (1,)), ((), ())), preferred_element_type=f32
        )
        scores = scores.reshape(heads, block, block) * (1.0 / math.sqrt(HEAD)) + hide[None]
        shifted = jnp.exp(scores - jnp.max(scores, axis=-1, keepdims=True)).astype(bf16)
        summed = jnp.dot(
            shifted.reshape(heads * block, block),
            jnp.concatenate([values[part], ones], axis=1),
            preferred_element_type=f32,
        )
        result = (summed[:, :HEAD] / summed[:, HEAD:]).astype(bf16)
        mixed.append(
            jnp.concatenate([result[h * block : (h + 1) * block] for h in range(heads)], axis=1)
        )
    attended = jnp.concatenate(mixed, axis=0)
    pooled = jnp.dot(member[...], attended, preferred_element_type=f32)
    pooled = (pooled / tally[...]).astype(bf16)
    gram[0] = lax.dot_general(
        pooled, pooled, (((1,), (1,)), ((), ())), preferred_element_type=f32
    )


def teacher_chunk(place, states, q_tables, extra, member, tally, parts, heads, with_keys, list_len, span=None):
    groups, tokens, width = states.shape
    step = TOKENS_STEP
    first, steps = span or (0, tokens // step)
    tokens = steps * step
    lists = step // list_len
    rows = lists * MAXP
    columns = parts[0].shape[1]
    pieces = list(parts)
    block = lambda n, m: pl.BlockSpec((n, m), lambda g: (g, 0))
    later = lambda n, m: pl.BlockSpec((n, m), lambda g: (g + first, 0))
    fixed = lambda n, m: pl.BlockSpec((n, m), lambda g: (0, 0))
    extra_specs = [fixed(step, HEAD)] * 2
    if not with_keys:
        extra_specs = [block(step, 1)] + [block(step, HEAD)] * 2
    outs = [jax.ShapeDtypeStruct((tokens // step, rows, rows), f32)]
    out_specs = [pl.BlockSpec((1, rows, rows), lambda g: (g, 0, 0))]
    if with_keys:
        outs += [jax.ShapeDtypeStruct((tokens, 1), f32)]
        outs += [jax.ShapeDtypeStruct((tokens, HEAD), bf16)] * 2
        out_specs += [block(step, 1)] + [block(step, HEAD)] * 2
    depth = groups * width
    return pl.pallas_call(
        functools.partial(teacher_kernel, heads, with_keys, list_len),
        grid=(tokens // step,),
        in_specs=[
            pl.BlockSpec(memory_space=pltpu.SMEM),
            pl.BlockSpec((groups, step, width), lambda g: (0, g + first, 0)),
        ]
        + [fixed(step, HEAD)] * 2
        + extra_specs
        + [later(rows, step), later(rows, 1)]
        + [pl.BlockSpec(memory_space=pltpu.HBM)] * len(pieces),
        out_specs=out_specs,
        out_shape=outs,
        scratch_shapes=[
            pltpu.VMEM((depth, columns), bf16),
            pltpu.SemaphoreType.DMA((64,)),
        ],
        compiler_params=pltpu.CompilerParams(
            dimension_semantics=("arbitrary",), vmem_limit_bytes=58 * 1024 * 1024
        ),
        cost_estimate=pl.CostEstimate(
            flops=2 * tokens * depth * columns,
            bytes_accessed=2 * depth * (tokens + columns),
            transcendentals=tokens * 128 * heads,
        ),
    )(place, states, *q_tables, *extra, member, tally, *pieces)


def rms_scale(values, weights):
    return values * lax.rsqrt(jnp.mean(values * values, axis=-1, keepdims=True) + EPSILON) * weights


def forward_kernel(count, *refs):
    z, rows, (gain, w_gate, w_up), rest = refs[0], refs[1 : 1 + count], refs[1 + count : 4 + count], refs[4 + count :]
    values = rows[0][...]
    if count == 2:
        early = pl.program_id(0) < pl.num_programs(0) // 2
        values = jnp.where(early, values, rows[1][...])
    values = values.astype(f32)
    active, scaled = rest[0], rest[-1]
    scaled[...] = rms_scale(values, gain[...]).T.astype(bf16)
    gate_pre = jnp.dot(w_gate[...], scaled[...], preferred_element_type=f32)
    up_pre = jnp.dot(w_up[...], scaled[...], preferred_element_type=f32)
    sigma = jax.nn.sigmoid(gate_pre)
    gated = gate_pre * sigma
    active[...] = (gated * up_pre).astype(bf16)
    if count == 2:
        gate_slope, up_slope, picked = rest[1:4]
        gate_slope[...] = (up_pre * sigma * (1.0 + gate_pre * (1.0 - sigma))).astype(bf16)
        up_slope[...] = gated.astype(bf16)
        pick_rows(picked, scaled, z[0], 8)


def pick_rows(picked, source, z, groups):
    own = picked.shape[0] // groups
    for k in range(groups):
        start = pl.multiple_of((k * 4 + z) * own, 16)
        picked[k * own : (k + 1) * own, :] = source[pl.ds(start, own), :]


def forward(z, rows, gain, w_gate, w_up):
    count = len(rows)
    size, width = rows[0].shape
    units = w_gate.shape[0]
    tile = 256
    middle = size // tile
    total = count * size
    whole = lambda a: pl.BlockSpec(a.shape, lambda g: (0, 0), pipeline_mode=pl.Buffered(1))
    across = lambda n: pl.BlockSpec((n, tile), lambda g: (0, g))
    outs = [units] if count == 1 else [units, units, units, width // 4]
    row_specs = [
        pl.BlockSpec((tile, width), lambda g: (jnp.minimum(g, middle - 1), 0)),
        pl.BlockSpec((tile, width), lambda g: (jnp.maximum(g - middle, 0), 0)),
    ]
    return pl.pallas_call(
        functools.partial(forward_kernel, count),
        grid=(count * middle,),
        in_specs=[pl.BlockSpec(memory_space=pltpu.SMEM)]
        + row_specs[:count]
        + [whole(gain), whole(w_gate), whole(w_up)],
        out_specs=[across(n) for n in outs],
        out_shape=[jax.ShapeDtypeStruct((n, total), bf16) for n in outs],
        scratch_shapes=[pltpu.VMEM((width, tile), bf16)],
        compiler_params=pltpu.CompilerParams(
            dimension_semantics=("arbitrary",), vmem_limit_bytes=(58 if count == 2 else 36) * 1024 * 1024
        ),
        cost_estimate=pl.CostEstimate(
            flops=4 * total * width * units,
            bytes_accessed=2 * total * width + 4 * width * units + 6 * total * units,
            transcendentals=total * units,
        ),
    )(z, *rows, gain, w_gate, w_up)


def pack_kernel(gram_a, gram_b, base, dispatch, out):
    steps, rows, _ = gram_a.shape
    row = lax.broadcasted_iota(jnp.int32, (rows, rows), 0)
    col = lax.broadcasted_iota(jnp.int32, (rows, rows), 1)
    lane = lax.broadcasted_iota(jnp.int32, (rows, 128), 1)
    same = row // MAXP == col // MAXP
    blocks = []
    for s in range(steps):
        gram = gram_a[s] + gram_b[s]
        block = base[s * rows : (s + 1) * rows, :]
        for k, (i, j) in enumerate(PAIRS):
            wanted = same & (row % MAXP == i) & (col % MAXP == j)
            value = jnp.sum(jnp.where(wanted, gram, 0.0), axis=1, keepdims=True)
            block = block + jnp.where(lane == k, value, 0.0)
        blocks.append(block)
    sent = jnp.dot(
        dispatch[...],
        jnp.concatenate(blocks, axis=0),
        precision=lax.Precision.HIGHEST,
        preferred_element_type=f32,
    )
    total = sent[:128]
    for q in range(1, 8):
        total = total + pltpu.roll(sent[q * 128 : (q + 1) * 128], 16 * q, 1)
    out[...] = total


def pack(gram_a, gram_b, base, dispatch):
    return pl.pallas_call(
        pack_kernel,
        in_specs=[pl.BlockSpec(memory_space=pltpu.VMEM)] * 4,
        out_specs=pl.BlockSpec(memory_space=pltpu.VMEM),
        out_shape=jax.ShapeDtypeStruct((128, 128), f32),
        compiler_params=pltpu.CompilerParams(vmem_limit_bytes=16 * 1024 * 1024),
        cost_estimate=pl.CostEstimate(
            flops=2 * 6 * 1024 * 128 * 128, bytes_accessed=1 << 20, transcendentals=0
        ),
    )(gram_a, gram_b, base, dispatch)


def hidden_kernel(rows_a, rows_b, ffn_a, ffn_b, turned, grams):
    @pl.when(pl.program_id(0) == 0)
    def _():
        grams[...] = jnp.zeros_like(grams)

    for c, (rows, ffn) in enumerate(((rows_a, ffn_a), (rows_b, ffn_b))):
        hidden = (rows[...].astype(f32) + ffn[...].astype(f32)).T
        size = hidden.shape[1] // MAXP
        turned[:, c * MAXP * size : (c + 1) * MAXP * size] = hidden.astype(bf16)
        cut = [hidden[:, i * size : (i + 1) * size] for i in range(MAXP)]
        for k, (i, j) in enumerate(PAIRS):
            grams[k : k + 1, c * size : (c + 1) * size] += jnp.sum(
                cut[i] * cut[j], axis=0, keepdims=True
            )


def hidden_parts(rows_a, rows_b, ffn_a, ffn_b):
    rows, width = rows_a.shape
    tile = 256
    spec = pl.BlockSpec((rows, tile), lambda g: (0, g))
    return pl.pallas_call(
        hidden_kernel,
        grid=(width // tile,),
        in_specs=[spec] * 4,
        out_specs=[
            pl.BlockSpec((tile, 2 * rows), lambda g: (g, 0)),
            pl.BlockSpec((16, 2 * rows // MAXP), lambda g: (0, 0)),
        ],
        out_shape=[
            jax.ShapeDtypeStruct((width, 2 * rows), bf16),
            jax.ShapeDtypeStruct((16, 2 * rows // MAXP), f32),
        ],
        compiler_params=pltpu.CompilerParams(
            dimension_semantics=("arbitrary",), vmem_limit_bytes=24 * 1024 * 1024
        ),
        cost_estimate=pl.CostEstimate(
            flops=24 * rows * width, bytes_accessed=12 * rows * width, transcendentals=0
        ),
    )(rows_a, rows_b, ffn_a, ffn_b)


def cosines(at, size):
    scales = [jnp.sqrt(at[i, i] / size + EPSILON) for i in range(MAXP)]
    return {(i, j): at[i, j] / (size * scales[i] * scales[j]) for i, j in PAIRS}, scales


def back_kernel(width, z, target, grams, turned, active, back, down, losses, factors, picked, held, sem):
    slots = target.shape[1]
    fetch = pltpu.make_async_copy(active, held, sem)

    @pl.when(pl.program_id(0) == 0)
    def _():
        fetch.start()

    @pl.when(pl.program_id(0) == 0)
    def _():
        row = lambda ref, k: ref[k : k + 1, :]
        wanted, _ = cosines({p: row(target, k) for k, p in enumerate(PAIRS)}, HQ * HEAD)
        have, scales = cosines({p: row(grams, k) for k, p in enumerate(PAIRS)}, width)
        count = row(target, len(PAIRS))
        alive = [jnp.where(count > i + 0.5, 1.0, 0.0) for i in range(MAXP)]
        bound = jnp.maximum(count, 1.0)
        over = 1.0 / (bound * bound)
        slope = {}
        loss = None
        for i, j in PAIRS:
            both = alive[i] * alive[j]
            differ = have[i, j] - wanted[i, j]
            slope[i, j] = slope[j, i] = 2.0 * both * differ * over
            term = (1.0 if i == j else 2.0) * both * differ * differ
            loss = term if loss is None else loss + term
        losses[...] = jnp.broadcast_to(loss * over, losses.shape)
        for i in range(MAXP):
            pull = sum(slope[i, j] * have[min(i, j), max(i, j)] for j in range(MAXP))
            for j in range(MAXP):
                term = slope[i, j] / (scales[i] * scales[j])
                if i == j:
                    term = term - pull / (scales[i] * scales[i])
                factors[i * MAXP + j : i * MAXP + j + 1, :] = 2.0 * term

    half = slots // 2
    for c in range(2):
        at = lambda i: slice((c * MAXP + i) * half, (c * MAXP + i + 1) * half)
        cut = [turned[:, at(i)].astype(f32) for i in range(MAXP)]
        for i in range(MAXP):
            mixed = None
            for j in range(MAXP):
                k = i * MAXP + j
                term = factors[k : k + 1, c * half : (c + 1) * half] * cut[j]
                mixed = term if mixed is None else mixed + term
            back[:, at(i)] = mixed.astype(bf16)
    step = pl.program_id(0)
    own = down.shape[1]
    group = back.shape[0] // 2
    for k in range(2):
        start = pl.multiple_of(k * group + z[0] * own, 16)
        to = pl.multiple_of((step * 2 + k) * own, 16)
        picked[pl.ds(to, own), :] = back[pl.ds(start, own), :]

    @pl.when(step == pl.num_programs(0) - 1)
    def _():
        fetch.wait()
        product = lax.dot_general(
            picked[...], held[...], (((1,), (1,)), ((), ())), preferred_element_type=f32
        ).astype(bf16)
        for k in range(down.shape[0]):
            down[k] = product[k * own : (k + 1) * own]


def pull_back(z, target, grams, turned, active):
    width, rows = turned.shape
    units = active.shape[0]
    own = width // 32
    tile = width // 4
    fixed = pl.BlockSpec(target.shape, lambda g: (0, 0))
    moving = lambda n: pl.BlockSpec((n, rows), lambda g: (g, 0))
    return pl.pallas_call(
        functools.partial(back_kernel, width),
        grid=(4,),
        in_specs=[
            pl.BlockSpec(memory_space=pltpu.SMEM),
            fixed,
            fixed,
            moving(tile),
            pl.BlockSpec(memory_space=pltpu.HBM),
        ],
        out_specs=[
            moving(tile),
            pl.BlockSpec((8, own, units), lambda g: (0, 0, 0)),
            pl.BlockSpec((8, target.shape[1]), lambda g: (0, 0)),
        ],
        out_shape=[
            jax.ShapeDtypeStruct((width, rows), bf16),
            jax.ShapeDtypeStruct((8, own, units), bf16),
            jax.ShapeDtypeStruct((8, target.shape[1]), f32),
        ],
        scratch_shapes=[
            pltpu.VMEM(target.shape, f32),
            pltpu.VMEM((8 * own, rows), bf16),
            pltpu.VMEM((units, rows), bf16),
            pltpu.SemaphoreType.DMA,
        ],
        compiler_params=pltpu.CompilerParams(
            dimension_semantics=("arbitrary",), vmem_limit_bytes=32 * 1024 * 1024
        ),
        cost_estimate=pl.CostEstimate(
            flops=8 * rows * width + 16 * own * rows * units, bytes_accessed=5 * rows * width, transcendentals=0
        ),
    )(z, target, grams, turned, active)


def inner_kernel(w_down, back, gate_slope, up_slope, gate_in, up_in):
    total = jnp.dot(w_down[...], back[...], preferred_element_type=f32)
    gate_in[...] = (total * gate_slope[...].astype(f32)).astype(bf16)
    up_in[...] = (total * up_slope[...].astype(f32)).astype(bf16)


def inner_grads(w_down, back, gate_slope, up_slope):
    units, width = w_down.shape
    rows = back.shape[1]
    tile = 256
    across = lambda n: pl.BlockSpec((n, tile), lambda g: (0, g))
    return pl.pallas_call(
        inner_kernel,
        grid=(rows // tile,),
        in_specs=[
            pl.BlockSpec(w_down.shape, lambda g: (0, 0), pipeline_mode=pl.Buffered(1)),
            across(width),
            across(units),
            across(units),
        ],
        out_specs=[across(units)] * 2,
        out_shape=[jax.ShapeDtypeStruct((units, rows), bf16)] * 2,
        compiler_params=pltpu.CompilerParams(
            dimension_semantics=("arbitrary",), vmem_limit_bytes=58 * 1024 * 1024
        ),
        cost_estimate=pl.CostEstimate(
            flops=2 * rows * width * units,
            bytes_accessed=2 * (rows * width + units * width + 4 * rows * units),
            transcendentals=0,
        ),
    )(w_down, back, gate_slope, up_slope)


def grad_kernel(picked, inner, *refs):
    out = refs[-1]
    product = lax.dot_general(
        picked[...], inner[...], (((1,), (1,)), ((), ())), preferred_element_type=f32
    ).astype(bf16)
    own = picked.shape[0] // out.shape[0]
    for k in range(out.shape[0]):
        out[k, :own] = product[k * own : (k + 1) * own]
        if len(refs) == 2:
            out[k, own:] = refs[0][k]


def weight_grad(picked, inner, *more):
    features, rows = picked.shape
    units = inner.shape[0]
    size = features // 8 + sum(a.shape[1] for a in more)
    return pl.pallas_call(
        grad_kernel,
        in_specs=[pl.BlockSpec(memory_space=pltpu.VMEM)] * (2 + len(more)),
        out_specs=pl.BlockSpec(memory_space=pltpu.VMEM),
        out_shape=jax.ShapeDtypeStruct((8, size, units), bf16),
        compiler_params=pltpu.CompilerParams(vmem_limit_bytes=32 * 1024 * 1024),
        cost_estimate=pl.CostEstimate(
            flops=2 * features * rows * units,
            bytes_accessed=2 * (features * rows + units * rows + features * units),
            transcendentals=0,
        ),
    )(picked, inner, *more)


def send_x(blocks, x):
    own = lax.dynamic_index_in_dim(blocks, x, 1, keepdims=False)
    outs = [lax.dynamic_index_in_dim(blocks, lax.rem(x + by, 4), 1, keepdims=False) for by in range(1, 4)]
    return (own, *(shift(out, "x", by + 1) for by, out in enumerate(outs)))


def add_up(terms):
    total = terms[0].astype(f32)
    for term in terms[1:]:
        total = total + term.astype(f32)
    return total


def scatter_y(blocks, yh, *deps):
    mine = lax.dynamic_index_in_dim(blocks, yh, 0, keepdims=False)
    out = lax.dynamic_index_in_dim(blocks, 1 - yh, 0, keepdims=False)
    came = shift(out, "yh", 1)
    if deps:
        (came,) = after((came,), *deps)
    return mine.astype(f32) + came.astype(f32)


def shards(
    teacher_states,
    teacher_gain,
    w_query,
    key_weight,
    value_weight,
    query_gain,
    key_gain,
    segments,
    passage_counts,
    swap_order,
    list_owner,
    student_rows,
    student_gain,
    w_gate,
    w_up,
    w_down,
):
    yh, x, z, yl, core = (lax.axis_index(a) for a in ALL)
    dp = (yh * 4 + x) * 4 + z
    lists, list_len = segments.shape
    slots = student_rows.shape[0]
    width = student_rows.shape[2]

    halves = jnp.swapaxes(student_rows.reshape(2, slots // 2, MAXP, width), 1, 2)
    own_rows = halves.reshape(slots * MAXP, width)
    half = own_rows.shape[0] // 2
    rows_half = lax.dynamic_slice_in_dim(own_rows, core * half, half, 0)
    rows_ring = ring_halves(rows_half, "z")

    depth = w_query.shape[0]
    row_gain = lax.dynamic_slice_in_dim(teacher_gain, dp * depth, depth, 0).astype(f32)[:, None]
    weights = jnp.concatenate([key_weight, value_weight, w_query], axis=1)
    weights = (weights.astype(f32) * row_gain).astype(bf16)
    across_y = shift(weights, "yh", 1)
    states = lax.all_gather(teacher_states, TP, axis=0, tiled=False)
    one = jnp.concatenate([weights[:FIRST], across_y[:FIRST]], axis=0)
    two = jnp.concatenate([weights[FIRST:], across_y[FIRST:]], axis=0)

    gain = student_gain.astype(f32)[None, :]
    z_at = z[None].astype(jnp.int32)
    (active_own,) = forward(z_at, (own_rows,), gain, w_gate.T, w_up.T)

    partial = lax.dot_general(
        active_own, w_down, (((0,), (0,)), ((), ())), preferred_element_type=f32
    ).astype(bf16)
    kept = lax.dynamic_slice_in_dim(partial, core * half, half, 0).astype(f32)
    given = lax.dynamic_slice_in_dim(partial, (1 - core) * half, half, 0)
    pair_sum = (kept + shift(given, "core", 1).astype(f32)).astype(bf16)
    two_ring, one_ring = two_rings(two, one, *rows_ring, pair_sum)
    rows_mine = stack_slots(after(rows_ring, *one_ring[1:], *two_ring[1:]))
    rows_other = shift(rows_mine, "core", 1)
    line_z = stack_ring(one_ring, CHUNK)
    line_x = stack_ring(two_ring, CHUNK)

    def spread(k, *before, last=()):
        rings = two_rings(line_z[k], line_x[k], *before, last=last)
        return (*rings[0], *rings[1])

    ffn_half = lax.psum(pair_sum, "yl")
    parts_a = spread(0, line_x[0], line_z[0], rows_other)

    active, gate_slope, up_slope, normed_pick = forward(
        z_at, (rows_mine, rows_other), gain, w_gate.T, w_up.T
    )

    owner = list_owner[:, 0]
    index = jnp.arange(lists, dtype=jnp.int32)
    earlier = jnp.sum(
        ((owner[None, :] == owner[:, None]) & (index[None, :] < index[:, None])).astype(jnp.int32),
        axis=1,
    )
    slot_of = owner * 2 + earlier
    select = (jnp.arange(slots, dtype=jnp.int32)[:, None] == slot_of[None, :]).astype(f32)
    per = slots // 2

    place = jnp.stack([yh, x, z]).astype(jnp.int32)
    q_tables = head_tables(query_gain, TOKENS_STEP, list_len)
    k_tables = head_tables(key_gain, TOKENS_STEP, list_len)
    spot = jnp.arange(MAXP, dtype=jnp.int32)
    live = spot[None, :] < passage_counts[:, None]
    member = (segments[:, None, :] == swap_order[:, :, None]) & live[:, :, None]
    tally = jnp.maximum(jnp.sum(member.astype(f32), axis=2), 1.0).reshape(lists * MAXP, 1)
    group = TOKENS_STEP // list_len
    same_list = jnp.eye(group, dtype=bool)
    spread_member = (
        member.reshape(lists // group, group, MAXP, 1, list_len)
        & same_list[None, :, None, :, None]
    )
    spread_member = spread_member.reshape(lists * MAXP, TOKENS_STEP).astype(bf16)
    gram_a, scale, keys, values = teacher_chunk(
        place, states, q_tables, k_tables, spread_member, tally, parts_a, 4, True, list_len
    )
    parts_b = spread(1, *parts_a, active, last=(gram_a,))
    ffn_ring = ring(ffn_half, "z", *parts_b, gram_a)
    (gram_b,) = teacher_chunk(
        place, states, q_tables, (scale, keys, values), spread_member, tally, parts_b, 4, False, list_len
    )
    line = jnp.arange(1024, dtype=jnp.int32)
    rel, e, d8, z_to = line // 256, line // 128 % 2, line // 16 % 8, line // 4 % 4
    order = jnp.where(rel == 0, 0, jnp.where(rel == 1, 3, rel - 1))
    slot_to = (d8 * 4 + (z_to + order) % 4) * 2 + e
    dispatch = (slot_to[:, None] == jnp.repeat(slot_of, MAXP)[None, :]).astype(f32)
    counted = (jnp.arange(128)[None, None, :] == len(PAIRS)) & (spot[None, :, None] == 0)
    base = jnp.where(counted, 0.25 * passage_counts.astype(f32)[:, None, None], 0.0)
    send = pack(gram_a, gram_b, base.reshape(lists * MAXP, 128), dispatch)
    ffn_mine = stack_slots(after(ffn_ring, send))
    ffn_other = shift(ffn_mine, "core", 1)
    turned, grams = hidden_parts(rows_mine, rows_other, ffn_mine, ffn_other)

    got = lax.all_to_all(send, ALL, split_axis=0, concat_axis=0, tiled=True)
    got = jnp.sum(got.reshape(32, 4, 128), axis=1)
    got = got.reshape(2, 16, 4, 2, 16).transpose(4, 0, 2, 1, 3).reshape(16, 2, 4 * per)
    got = jnp.where(core == 0, got, got[:, ::-1]).reshape(16, 8 * per)

    back, grad_down, losses = pull_back(z_at, got, grams, turned, active)
    cut = lambda grad: grad.reshape(2, 4, *grad.shape[1:])
    slot_losses = losses[0].reshape(2, 4, 4, 4, 2)
    slot_losses = lax.dynamic_index_in_dim(slot_losses, z, 3, keepdims=False)
    slot_losses = jnp.where(core == 0, slot_losses, slot_losses[::-1])
    slot_losses = slot_losses.transpose(0, 2, 1, 3).reshape(8, 8)
    owners = (yh * 4 + x) * 4 + (z + jnp.array(AROUND)) % 4
    lanes = (owners[:, None] * 2 + jnp.arange(2)[None, :]).reshape(8)
    lane = jnp.arange(w_gate.shape[1], dtype=jnp.int32)
    spots = (lanes[:, None] == lane[None, :]).astype(f32)
    laid = jnp.sum(slot_losses[:, :, None] * spots[None], axis=1)
    terms, left = [], laid
    for _ in range(3):
        terms.append(left.astype(bf16))
        left = left - terms[-1].astype(f32)
    zeros = jnp.zeros((8, 13, lane.shape[0]), bf16)
    loss_rows = jnp.concatenate([jnp.stack(terms, axis=1), zeros], axis=1)
    down_terms = send_x(cut(grad_down), x)
    gate_in, up_in = inner_grads(w_down, back, gate_slope, up_slope)
    (up_in,) = after((up_in,), down_terms[3])
    grad_up = weight_grad(normed_pick, up_in, loss_rows)
    up_terms = send_x(cut(grad_up), x)
    (gate_in,) = after((gate_in,), grad_up)
    grad_gate = weight_grad(normed_pick, gate_in)
    gate_y = scatter_y(cut(grad_gate), yh).astype(bf16)
    down_sum = scatter_y(add_up(down_terms).astype(bf16), yh, gate_y)
    up_sum = scatter_y(add_up(up_terms).astype(bf16), yh, gate_y)
    gate_sum = add_up(send_x(gate_y[None], x))[0]

    returned = jnp.sum(up_sum[-16:, :slots], axis=0)
    list_loss = jnp.sum(select * returned[:, None], axis=0)
    return (list_loss, gate_sum, up_sum[:-16], down_sum.T)


def solution(mesh):
    fine = Mesh(mesh.devices.reshape(tuple(SIZES.values())), tuple(SIZES))
    placed = (
        P(DP, TP),
        P(),
        P(DP, TP),
        P(DP, TP),
        P(DP, TP),
        P(),
        P(),
        P(DP, None),
        P(DP),
        P(DP, None),
        P(DP, None),
        P(DP, None, None),
        P(),
        P(None, TP),
        P(None, TP),
        P(TP, None),
    )
    return jax.shard_map(
        shards,
        mesh=fine,
        in_specs=placed,
        out_specs=(P(DP), P(DP, TP), P(DP, TP), P(TP, DP)),
        check_vma=False,
    )
```

```python
import functools
import math

import jax
import jax.numpy as jnp
from jax import lax
from jax.experimental import pallas as pl
from jax.experimental.pallas import tpu as pltpu
from jax.sharding import Mesh
from jax.sharding import PartitionSpec as P

HQ = 32
HEAD = 128
MAXP = 4
EPSILON = 1e-06
ROPE_BASE = 1000000.0
DP = ("yh", "x", "z")
TP = ("yl", "core")
ALL = DP + TP
SIZES = {"yh": 2, "x": 4, "z": 4, "yl": 2, "core": 2}
PAIRS = [(i, j) for i in range(MAXP) for j in range(i, MAXP)]
FIRST = 80
CHUNK = 768
TOKENS_STEP = 512
AROUND = (0, 3, 1, 2)
bf16 = jnp.bfloat16
f32 = jnp.float32


def shift(value, axis, by):
    n = SIZES[axis]
    return lax.ppermute(value, axis, [(i, (i + by) % n) for i in range(n)])


def after(values, *deps):
    return lax.optimization_barrier((tuple(values), tuple(deps)))[0]


def ring_halves(block, axis, *deps):
    (block,) = after((block,), *deps)
    left, right = shift(block, axis, 1), shift(block, axis, -1)
    half = block.shape[0] // 2
    return block, left, right, shift(left[:half], axis, 1), shift(right[half:], axis, -1)


def ring(block, axis, *deps):
    (block,) = after((block,), *deps)
    return block, shift(block, axis, 1), shift(block, axis, -1), shift(block, axis, 2)


def two_rings(along_x, along_z, *deps, last=()):
    x0, z0 = after((along_x, along_z), *deps)
    (z_last,) = after((z0,), *last) if last else (z0,)
    x3, z3 = shift(x0, "x", 2), shift(z_last, "z", 2)
    x2, x1 = shift(x0, "x", -1), shift(x0, "x", 1)
    z2, z1 = shift(z0, "z", -1), shift(z0, "z", 1)
    return (x0, x1, x2, x3), (z0, z1, z2, z3)


def stack_kernel(moves, cuts, *refs):
    sources, outs = refs[: -len(cuts)], refs[-len(cuts) :]
    for i, at, n, to in moves:
        for out, (low, high) in zip(outs, cuts):
            out[to : to + n, :] = sources[i][at : at + n, low:high]


def stack(arrays, moves, cuts=None):
    rows, columns = sum(m[2] for m in moves), arrays[0].shape[1]
    cuts = cuts or [(0, columns)]
    return pl.pallas_call(
        functools.partial(stack_kernel, moves, cuts),
        in_specs=[pl.BlockSpec(memory_space=pltpu.VMEM)] * len(arrays),
        out_specs=[pl.BlockSpec(memory_space=pltpu.VMEM)] * len(cuts),
        out_shape=[jax.ShapeDtypeStruct((rows, c[1] - c[0]), arrays[0].dtype) for c in cuts],
        compiler_params=pltpu.CompilerParams(vmem_limit_bytes=24 * 1024 * 1024),
        cost_estimate=pl.CostEstimate(
            flops=0, bytes_accessed=4 * rows * columns, transcendentals=0
        ),
    )(*arrays)


def stack_ring(blocks, cut):
    n, columns = blocks[0].shape
    return stack(blocks, [(k, 0, n, k * n) for k in range(4)], [(0, cut), (cut, columns)])


def stack_slots(blocks):
    n = blocks[0].shape[0] // MAXP
    whole = 4 if len(blocks) == 4 else 3
    moves = [(k, p * n, n, (p * 4 + k) * n) for k in range(whole) for p in range(MAXP)]
    if whole == 3:
        moves += [(3 + p // 2, p % 2 * n, n, (p * 4 + 3) * n) for p in range(MAXP)]
    return stack(blocks, moves)[0]


def head_tables(gain, tokens, list_len):
    half = HEAD // 2
    positions = (jnp.arange(tokens, dtype=jnp.int32) % list_len).astype(f32)
    exponent = jnp.arange(half, dtype=f32) * (-2.0 / HEAD)
    angles = positions[:, None] * jnp.power(ROPE_BASE, exponent)[None, :]
    cosines, sines = jnp.cos(angles), jnp.sin(angles)
    same = jnp.concatenate([cosines, cosines], axis=1) * gain[None, :]
    crossed = jnp.concatenate([-sines, sines], axis=1) * jnp.roll(gain, half)[None, :]
    return same, crossed


def norm_rotate(values, same, crossed):
    mean = jnp.mean(values * values, axis=-1, keepdims=True)
    scaled = values * lax.rsqrt(mean + EPSILON)
    return (scaled * same + pltpu.roll(scaled, HEAD // 2, 1) * crossed).astype(bf16)


def teacher_kernel(heads, with_keys, list_len, *refs):
    place, states, q_same, q_cross = refs[:4]
    rest = refs[4:]
    if with_keys:
        k_same, k_cross = rest[:2]
        rest = rest[2:]
    else:
        scale_in, k_in, v_in = rest[:3]
        rest = rest[3:]
    member, tally = rest[:2]
    pieces = rest[2:10]
    rest = rest[10:]
    if with_keys:
        gram, scale_out, k_out, v_out, weights, sems = rest
    else:
        gram, weights, sems = rest

    @pl.when(pl.program_id(0) == 0)
    def _():
        yh, xx, zz = place[0], place[1], place[2]
        copies = []
        for part in range(2):
            base = part * FIRST
            for far in range(4):
                for near in range(4):
                    for h in range(2):
                        source = part * 4 + far
                        row = (near * 2 + h) * FIRST
                        rel_x, rel_z = (far, near) if part == 0 else (near, far)
                        x_at = lax.rem(xx + AROUND[rel_x], 4)
                        z_at = lax.rem(zz + AROUND[rel_z], 4)
                        y_at = lax.rem(yh + h, 2)
                        to = ((y_at * 4 + x_at) * 4 + z_at) * (2 * FIRST) + base
                        copies.append(
                            pltpu.make_async_copy(
                                pieces[source].at[pl.ds(row, FIRST), :],
                                weights.at[pl.ds(pl.multiple_of(to, 16), FIRST), :],
                                sems.at[len(copies)],
                            )
                        )
        for copy in copies:
            copy.start()
        for copy in copies:
            copy.wait()

    groups, _, width = states.shape
    total, squares = None, None
    for k in range(groups):
        piece = states[k]
        term = jnp.dot(
            piece, weights[k * width : (k + 1) * width, :], preferred_element_type=f32
        )
        total = term if total is None else total + term
        if with_keys:
            wide = piece.astype(f32)
            more = jnp.sum(wide * wide, axis=1, keepdims=True)
            squares = more if squares is None else squares + more
    if with_keys:
        scale = lax.rsqrt(squares / (groups * width) + EPSILON)
        scale_out[...] = scale
    else:
        scale = scale_in[...]
    total = total * scale
    if with_keys:
        keys = norm_rotate(total[:, :HEAD], k_same[...], k_cross[...])
        values = total[:, HEAD : 2 * HEAD].astype(bf16)
        k_out[...] = keys
        v_out[...] = values
        first = 2 * HEAD
    else:
        keys, values, first = k_in[...], v_in[...], 0
    tokens = total.shape[0]
    block = 128
    row = lax.broadcasted_iota(jnp.int32, (block, block), 0)
    col = lax.broadcasted_iota(jnp.int32, (block, block), 1)
    allowed = (col <= row) & (col // list_len == row // list_len)
    hide = jnp.where(allowed, 0.0, -1e30)
    ones = jnp.ones((block, HEAD), bf16)
    queries = [
        norm_rotate(total[:, first + h * HEAD : first + (h + 1) * HEAD], q_same[...], q_cross[...])
        for h in range(heads)
    ]
    mixed = []
    for s in range(tokens // block):
        part = slice(s * block, (s + 1) * block)
        stacked = jnp.concatenate([q[part] for q in queries], axis=0)
        scores = lax.dot_general(
            stacked, keys[part], (((1,), (1,)), ((), ())), preferred_element_type=f32
        )
        scores = scores.reshape(heads, block, block) * (1.0 / math.sqrt(HEAD)) + hide[None]
        shifted = jnp.exp(scores - jnp.max(scores, axis=-1, keepdims=True)).astype(bf16)
        summed = jnp.dot(
            shifted.reshape(heads * block, block),
            jnp.concatenate([values[part], ones], axis=1),
            preferred_element_type=f32,
        )
        result = (summed[:, :HEAD] / summed[:, HEAD:]).astype(bf16)
        mixed.append(
            jnp.concatenate([result[h * block : (h + 1) * block] for h in range(heads)], axis=1)
        )
    attended = jnp.concatenate(mixed, axis=0)
    pooled = jnp.dot(member[...], attended, preferred_element_type=f32)
    pooled = (pooled / tally[...]).astype(bf16)
    gram[0] = lax.dot_general(
        pooled, pooled, (((1,), (1,)), ((), ())), preferred_element_type=f32
    )


def teacher_chunk(place, states, q_tables, extra, member, tally, parts, heads, with_keys, list_len, span=None):
    groups, tokens, width = states.shape
    step = TOKENS_STEP
    first, steps = span or (0, tokens // step)
    tokens = steps * step
    lists = step // list_len
    rows = lists * MAXP
    columns = parts[0].shape[1]
    pieces = list(parts)
    block = lambda n, m: pl.BlockSpec((n, m), lambda g: (g, 0))
    later = lambda n, m: pl.BlockSpec((n, m), lambda g: (g + first, 0))
    fixed = lambda n, m: pl.BlockSpec((n, m), lambda g: (0, 0))
    extra_specs = [fixed(step, HEAD)] * 2
    if not with_keys:
        extra_specs = [block(step, 1)] + [block(step, HEAD)] * 2
    outs = [jax.ShapeDtypeStruct((tokens // step, rows, rows), f32)]
    out_specs = [pl.BlockSpec((1, rows, rows), lambda g: (g, 0, 0))]
    if with_keys:
        outs += [jax.ShapeDtypeStruct((tokens, 1), f32)]
        outs += [jax.ShapeDtypeStruct((tokens, HEAD), bf16)] * 2
        out_specs += [block(step, 1)] + [block(step, HEAD)] * 2
    depth = groups * width
    return pl.pallas_call(
        functools.partial(teacher_kernel, heads, with_keys, list_len),
        grid=(tokens // step,),
        in_specs=[
            pl.BlockSpec(memory_space=pltpu.SMEM),
            pl.BlockSpec((groups, step, width), lambda g: (0, g + first, 0)),
        ]
        + [fixed(step, HEAD)] * 2
        + extra_specs
        + [later(rows, step), later(rows, 1)]
        + [pl.BlockSpec(memory_space=pltpu.HBM)] * len(pieces),
        out_specs=out_specs,
        out_shape=outs,
        scratch_shapes=[
            pltpu.VMEM((depth, columns), bf16),
            pltpu.SemaphoreType.DMA((64,)),
        ],
        compiler_params=pltpu.CompilerParams(
            dimension_semantics=("arbitrary",), vmem_limit_bytes=58 * 1024 * 1024
        ),
        cost_estimate=pl.CostEstimate(
            flops=2 * tokens * depth * columns,
            bytes_accessed=2 * depth * (tokens + columns),
            transcendentals=tokens * 128 * heads,
        ),
    )(place, states, *q_tables, *extra, member, tally, *pieces)


def rms_scale(values, weights):
    return values * lax.rsqrt(jnp.mean(values * values, axis=-1, keepdims=True) + EPSILON) * weights


def forward_kernel(count, *refs):
    z, rows, (gain, w_gate, w_up), rest = refs[0], refs[1 : 1 + count], refs[1 + count : 4 + count], refs[4 + count :]
    values = rows[0][...]
    if count == 2:
        early = pl.program_id(0) < pl.num_programs(0) // 2
        values = jnp.where(early, values, rows[1][...])
    values = values.astype(f32)
    active, scaled = rest[0], rest[-1]
    scaled[...] = rms_scale(values, gain[...]).T.astype(bf16)
    gate_pre = jnp.dot(w_gate[...], scaled[...], preferred_element_type=f32)
    up_pre = jnp.dot(w_up[...], scaled[...], preferred_element_type=f32)
    sigma = jax.nn.sigmoid(gate_pre)
    gated = gate_pre * sigma
    active[...] = (gated * up_pre).astype(bf16)
    if count == 2:
        gate_slope, up_slope, picked = rest[1:4]
        gate_slope[...] = (up_pre * sigma * (1.0 + gate_pre * (1.0 - sigma))).astype(bf16)
        up_slope[...] = gated.astype(bf16)
        pick_rows(picked, scaled, z[0], 8)


def pick_rows(picked, source, z, groups):
    own = picked.shape[0] // groups
    for k in range(groups):
        start = pl.multiple_of((k * 4 + z) * own, 16)
        picked[k * own : (k + 1) * own, :] = source[pl.ds(start, own), :]


def forward(z, rows, gain, w_gate, w_up):
    count = len(rows)
    size, width = rows[0].shape
    units = w_gate.shape[0]
    tile = 256
    middle = size // tile
    total = count * size
    whole = lambda a: pl.BlockSpec(a.shape, lambda g: (0, 0), pipeline_mode=pl.Buffered(1))
    across = lambda n: pl.BlockSpec((n, tile), lambda g: (0, g))
    outs = [units] if count == 1 else [units, units, units, width // 4]
    row_specs = [
        pl.BlockSpec((tile, width), lambda g: (jnp.minimum(g, middle - 1), 0)),
        pl.BlockSpec((tile, width), lambda g: (jnp.maximum(g - middle, 0), 0)),
    ]
    return pl.pallas_call(
        functools.partial(forward_kernel, count),
        grid=(count * middle,),
        in_specs=[pl.BlockSpec(memory_space=pltpu.SMEM)]
        + row_specs[:count]
        + [whole(gain), whole(w_gate), whole(w_up)],
        out_specs=[across(n) for n in outs],
        out_shape=[jax.ShapeDtypeStruct((n, total), bf16) for n in outs],
        scratch_shapes=[pltpu.VMEM((width, tile), bf16)],
        compiler_params=pltpu.CompilerParams(
            dimension_semantics=("arbitrary",), vmem_limit_bytes=(58 if count == 2 else 36) * 1024 * 1024
        ),
        cost_estimate=pl.CostEstimate(
            flops=4 * total * width * units,
            bytes_accessed=2 * total * width + 4 * width * units + 6 * total * units,
            transcendentals=total * units,
        ),
    )(z, *rows, gain, w_gate, w_up)


def pack_kernel(gram_a, gram_b, base, dispatch, out):
    steps, rows, _ = gram_a.shape
    row = lax.broadcasted_iota(jnp.int32, (rows, rows), 0)
    col = lax.broadcasted_iota(jnp.int32, (rows, rows), 1)
    lane = lax.broadcasted_iota(jnp.int32, (rows, 128), 1)
    same = row // MAXP == col // MAXP
    blocks = []
    for s in range(steps):
        gram = gram_a[s] + gram_b[s]
        block = base[s * rows : (s + 1) * rows, :]
        for k, (i, j) in enumerate(PAIRS):
            wanted = same & (row % MAXP == i) & (col % MAXP == j)
            value = jnp.sum(jnp.where(wanted, gram, 0.0), axis=1, keepdims=True)
            block = block + jnp.where(lane == k, value, 0.0)
        blocks.append(block)
    sent = jnp.dot(
        dispatch[...],
        jnp.concatenate(blocks, axis=0),
        precision=lax.Precision.HIGHEST,
        preferred_element_type=f32,
    )
    total = sent[:128]
    for q in range(1, 8):
        total = total + pltpu.roll(sent[q * 128 : (q + 1) * 128], 16 * q, 1)
    out[...] = total


def pack(gram_a, gram_b, base, dispatch):
    return pl.pallas_call(
        pack_kernel,
        in_specs=[pl.BlockSpec(memory_space=pltpu.VMEM)] * 4,
        out_specs=pl.BlockSpec(memory_space=pltpu.VMEM),
        out_shape=jax.ShapeDtypeStruct((128, 128), f32),
        compiler_params=pltpu.CompilerParams(vmem_limit_bytes=16 * 1024 * 1024),
        cost_estimate=pl.CostEstimate(
            flops=2 * 6 * 1024 * 128 * 128, bytes_accessed=1 << 20, transcendentals=0
        ),
    )(gram_a, gram_b, base, dispatch)


def hidden_kernel(rows_a, rows_b, ffn_a, ffn_b, turned, grams):
    @pl.when(pl.program_id(0) == 0)
    def _():
        grams[...] = jnp.zeros_like(grams)

    for c, (rows, ffn) in enumerate(((rows_a, ffn_a), (rows_b, ffn_b))):
        hidden = (rows[...].astype(f32) + ffn[...].astype(f32)).T
        size = hidden.shape[1] // MAXP
        turned[:, c * MAXP * size : (c + 1) * MAXP * size] = hidden.astype(bf16)
        cut = [hidden[:, i * size : (i + 1) * size] for i in range(MAXP)]
        for k, (i, j) in enumerate(PAIRS):
            grams[k : k + 1, c * size : (c + 1) * size] += jnp.sum(
                cut[i] * cut[j], axis=0, keepdims=True
            )


def hidden_parts(rows_a, rows_b, ffn_a, ffn_b):
    rows, width = rows_a.shape
    tile = 256
    spec = pl.BlockSpec((rows, tile), lambda g: (0, g))
    return pl.pallas_call(
        hidden_kernel,
        grid=(width // tile,),
        in_specs=[spec] * 4,
        out_specs=[
            pl.BlockSpec((tile, 2 * rows), lambda g: (g, 0)),
            pl.BlockSpec((16, 2 * rows // MAXP), lambda g: (0, 0)),
        ],
        out_shape=[
            jax.ShapeDtypeStruct((width, 2 * rows), bf16),
            jax.ShapeDtypeStruct((16, 2 * rows // MAXP), f32),
        ],
        compiler_params=pltpu.CompilerParams(
            dimension_semantics=("arbitrary",), vmem_limit_bytes=24 * 1024 * 1024
        ),
        cost_estimate=pl.CostEstimate(
            flops=24 * rows * width, bytes_accessed=12 * rows * width, transcendentals=0
        ),
    )(rows_a, rows_b, ffn_a, ffn_b)


def cosines(at, size):
    scales = [jnp.sqrt(at[i, i] / size + EPSILON) for i in range(MAXP)]
    return {(i, j): at[i, j] / (size * scales[i] * scales[j]) for i, j in PAIRS}, scales


def back_kernel(width, z, target, grams, turned, active, back, down, losses, factors, picked, held, sem):
    slots = target.shape[1]
    fetch = pltpu.make_async_copy(active, held, sem)

    @pl.when(pl.program_id(0) == 0)
    def _():
        fetch.start()

    @pl.when(pl.program_id(0) == 0)
    def _():
        row = lambda ref, k: ref[k : k + 1, :]
        wanted, _ = cosines({p: row(target, k) for k, p in enumerate(PAIRS)}, HQ * HEAD)
        have, scales = cosines({p: row(grams, k) for k, p in enumerate(PAIRS)}, width)
        count = row(target, len(PAIRS))
        alive = [jnp.where(count > i + 0.5, 1.0, 0.0) for i in range(MAXP)]
        bound = jnp.maximum(count, 1.0)
        over = 1.0 / (bound * bound)
        slope = {}
        loss = None
        for i, j in PAIRS:
            both = alive[i] * alive[j]
            differ = have[i, j] - wanted[i, j]
            slope[i, j] = slope[j, i] = 2.0 * both * differ * over
            term = (1.0 if i == j else 2.0) * both * differ * differ
            loss = term if loss is None else loss + term
        losses[...] = jnp.broadcast_to(loss * over, losses.shape)
        for i in range(MAXP):
            pull = sum(slope[i, j] * have[min(i, j), max(i, j)] for j in range(MAXP))
            for j in range(MAXP):
                term = slope[i, j] / (scales[i] * scales[j])
                if i == j:
                    term = term - pull / (scales[i] * scales[i])
                factors[i * MAXP + j : i * MAXP + j + 1, :] = 2.0 * term

    half = slots // 2
    for c in range(2):
        at = lambda i: slice((c * MAXP + i) * half, (c * MAXP + i + 1) * half)
        cut = [turned[:, at(i)].astype(f32) for i in range(MAXP)]
        for i in range(MAXP):
            mixed = None
            for j in range(MAXP):
                k = i * MAXP + j
                term = factors[k : k + 1, c * half : (c + 1) * half] * cut[j]
                mixed = term if mixed is None else mixed + term
            back[:, at(i)] = mixed.astype(bf16)
    step = pl.program_id(0)
    own = down.shape[1]
    group = back.shape[0] // 2
    for k in range(2):
        start = pl.multiple_of(k * group + z[0] * own, 16)
        to = pl.multiple_of((step * 2 + k) * own, 16)
        picked[pl.ds(to, own), :] = back[pl.ds(start, own), :]

    @pl.when(step == pl.num_programs(0) - 1)
    def _():
        fetch.wait()
        product = lax.dot_general(
            picked[...], held[...], (((1,), (1,)), ((), ())), preferred_element_type=f32
        ).astype(bf16)
        for k in range(down.shape[0]):
            down[k] = product[k * own : (k + 1) * own]


def pull_back(z, target, grams, turned, active):
    width, rows = turned.shape
    units = active.shape[0]
    own = width // 32
    tile = width // 4
    fixed = pl.BlockSpec(target.shape, lambda g: (0, 0))
    moving = lambda n: pl.BlockSpec((n, rows), lambda g: (g, 0))
    return pl.pallas_call(
        functools.partial(back_kernel, width),
        grid=(4,),
        in_specs=[
            pl.BlockSpec(memory_space=pltpu.SMEM),
            fixed,
            fixed,
            moving(tile),
            pl.BlockSpec(memory_space=pltpu.HBM),
        ],
        out_specs=[
            moving(tile),
            pl.BlockSpec((8, own, units), lambda g: (0, 0, 0)),
            pl.BlockSpec((8, target.shape[1]), lambda g: (0, 0)),
        ],
        out_shape=[
            jax.ShapeDtypeStruct((width, rows), bf16),
            jax.ShapeDtypeStruct((8, own, units), bf16),
            jax.ShapeDtypeStruct((8, target.shape[1]), f32),
        ],
        scratch_shapes=[
            pltpu.VMEM(target.shape, f32),
            pltpu.VMEM((8 * own, rows), bf16),
            pltpu.VMEM((units, rows), bf16),
            pltpu.SemaphoreType.DMA,
        ],
        compiler_params=pltpu.CompilerParams(
            dimension_semantics=("arbitrary",), vmem_limit_bytes=32 * 1024 * 1024
        ),
        cost_estimate=pl.CostEstimate(
            flops=8 * rows * width + 16 * own * rows * units, bytes_accessed=5 * rows * width, transcendentals=0
        ),
    )(z, target, grams, turned, active)


def inner_kernel(w_down, back, gate_slope, up_slope, gate_in, up_in):
    total = jnp.dot(w_down[...], back[...], preferred_element_type=f32)
    gate_in[...] = (total * gate_slope[...].astype(f32)).astype(bf16)
    up_in[...] = (total * up_slope[...].astype(f32)).astype(bf16)


def inner_grads(w_down, back, gate_slope, up_slope):
    units, width = w_down.shape
    rows = back.shape[1]
    tile = 256
    across = lambda n: pl.BlockSpec((n, tile), lambda g: (0, g))
    return pl.pallas_call(
        inner_kernel,
        grid=(rows // tile,),
        in_specs=[
            pl.BlockSpec(w_down.shape, lambda g: (0, 0), pipeline_mode=pl.Buffered(1)),
            across(width),
            across(units),
            across(units),
        ],
        out_specs=[across(units)] * 2,
        out_shape=[jax.ShapeDtypeStruct((units, rows), bf16)] * 2,
        compiler_params=pltpu.CompilerParams(
            dimension_semantics=("arbitrary",), vmem_limit_bytes=58 * 1024 * 1024
        ),
        cost_estimate=pl.CostEstimate(
            flops=2 * rows * width * units,
            bytes_accessed=2 * (rows * width + units * width + 4 * rows * units),
            transcendentals=0,
        ),
    )(w_down, back, gate_slope, up_slope)


def grad_kernel(picked, inner, *refs):
    out = refs[-1]
    product = lax.dot_general(
        picked[...], inner[...], (((1,), (1,)), ((), ())), preferred_element_type=f32
    ).astype(bf16)
    own = picked.shape[0] // out.shape[0]
    for k in range(out.shape[0]):
        out[k, :own] = product[k * own : (k + 1) * own]
        if len(refs) == 2:
            out[k, own:] = refs[0][k]


def weight_grad(picked, inner, *more):
    features, rows = picked.shape
    units = inner.shape[0]
    size = features // 8 + sum(a.shape[1] for a in more)
    return pl.pallas_call(
        grad_kernel,
        in_specs=[pl.BlockSpec(memory_space=pltpu.VMEM)] * (2 + len(more)),
        out_specs=pl.BlockSpec(memory_space=pltpu.VMEM),
        out_shape=jax.ShapeDtypeStruct((8, size, units), bf16),
        compiler_params=pltpu.CompilerParams(vmem_limit_bytes=32 * 1024 * 1024),
        cost_estimate=pl.CostEstimate(
            flops=2 * features * rows * units,
            bytes_accessed=2 * (features * rows + units * rows + features * units),
            transcendentals=0,
        ),
    )(picked, inner, *more)


def send_x(blocks, x):
    own = lax.dynamic_index_in_dim(blocks, x, 1, keepdims=False)
    outs = [lax.dynamic_index_in_dim(blocks, lax.rem(x + by, 4), 1, keepdims=False) for by in range(1, 4)]
    return (own, *(shift(out, "x", by + 1) for by, out in enumerate(outs)))


def add_up(terms):
    total = terms[0].astype(f32)
    for term in terms[1:]:
        total = total + term.astype(f32)
    return total


def scatter_y(blocks, yh, *deps):
    mine = lax.dynamic_index_in_dim(blocks, yh, 0, keepdims=False)
    out = lax.dynamic_index_in_dim(blocks, 1 - yh, 0, keepdims=False)
    came = shift(out, "yh", 1)
    if deps:
        (came,) = after((came,), *deps)
    return mine.astype(f32) + came.astype(f32)


def shards(
    teacher_states,
    teacher_gain,
    w_query,
    key_weight,
    value_weight,
    query_gain,
    key_gain,
    segments,
    passage_counts,
    swap_order,
    list_owner,
    student_rows,
    student_gain,
    w_gate,
    w_up,
    w_down,
):
    yh, x, z, yl, core = (lax.axis_index(a) for a in ALL)
    dp = (yh * 4 + x) * 4 + z
    lists, list_len = segments.shape
    slots = student_rows.shape[0]
    width = student_rows.shape[2]

    halves = jnp.swapaxes(student_rows.reshape(2, slots // 2, MAXP, width), 1, 2)
    own_rows = halves.reshape(slots * MAXP, width)
    half = own_rows.shape[0] // 2
    rows_half = lax.dynamic_slice_in_dim(own_rows, core * half, half, 0)
    rows_ring = ring_halves(rows_half, "z")

    depth = w_query.shape[0]
    row_gain = lax.dynamic_slice_in_dim(teacher_gain, dp * depth, depth, 0).astype(f32)[:, None]
    weights = jnp.concatenate([key_weight, value_weight, w_query], axis=1)
    weights = (weights.astype(f32) * row_gain).astype(bf16)
    across_y = shift(weights, "yh", 1)
    states = lax.all_gather(teacher_states, TP, axis=0, tiled=False)
    one = jnp.concatenate([weights[:FIRST], across_y[:FIRST]], axis=0)
    two = jnp.concatenate([weights[FIRST:], across_y[FIRST:]], axis=0)

    gain = student_gain.astype(f32)[None, :]
    z_at = z[None].astype(jnp.int32)
    (active_own,) = forward(z_at, (own_rows,), gain, w_gate.T, w_up.T)

    partial = lax.dot_general(
        active_own, w_down, (((0,), (0,)), ((), ())), preferred_element_type=f32
    ).astype(bf16)
    kept = lax.dynamic_slice_in_dim(partial, core * half, half, 0).astype(f32)
    given = lax.dynamic_slice_in_dim(partial, (1 - core) * half, half, 0)
    pair_sum = (kept + shift(given, "core", 1).astype(f32)).astype(bf16)
    two_ring, one_ring = two_rings(two, one, *rows_ring[3:], pair_sum)

    spot = jnp.arange(MAXP, dtype=jnp.int32)
    live = spot[None, :] < passage_counts[:, None]
    member = (segments[:, None, :] == swap_order[:, :, None]) & live[:, :, None]
    tally = jnp.maximum(jnp.sum(member.astype(f32), axis=2), 1.0).reshape(lists * MAXP, 1)
    group = TOKENS_STEP // list_len
    same_list = jnp.eye(group, dtype=bool)
    spread_member = (
        member.reshape(lists // group, group, MAXP, 1, list_len)
        & same_list[None, :, None, :, None]
    )
    spread_member = spread_member.reshape(lists * MAXP, TOKENS_STEP).astype(bf16)

    line_z = stack_ring(one_ring, CHUNK)
    line_x = stack_ring(two_ring, CHUNK)
    rows_mine = stack_slots(after(rows_ring, line_z[1], line_x[1], spread_member, tally))
    rows_other = shift(rows_mine, "core", 1)

    def spread(k, *before, last=()):
        rings = two_rings(line_z[k], line_x[k], *before, last=last)
        return (*rings[0], *rings[1])

    ffn_half = lax.psum(pair_sum, "yl")
    parts_a = spread(0, line_x[0], line_z[0])

    active, gate_slope, up_slope, normed_pick = forward(
        z_at, (rows_mine, rows_other), gain, w_gate.T, w_up.T
    )

    owner = list_owner[:, 0]
    index = jnp.arange(lists, dtype=jnp.int32)
    earlier = jnp.sum(
        ((owner[None, :] == owner[:, None]) & (index[None, :] < index[:, None])).astype(jnp.int32),
        axis=1,
    )
    slot_of = owner * 2 + earlier
    select = (jnp.arange(slots, dtype=jnp.int32)[:, None] == slot_of[None, :]).astype(f32)
    per = slots // 2

    place = jnp.stack([yh, x, z]).astype(jnp.int32)
    q_tables = head_tables(query_gain, TOKENS_STEP, list_len)
    k_tables = head_tables(key_gain, TOKENS_STEP, list_len)
    gram_a, scale, keys, values = teacher_chunk(
        place, states, q_tables, k_tables, spread_member, tally, parts_a, 4, True, list_len
    )
    parts_b = spread(1, *parts_a, active, last=(gram_a,))
    ffn_ring = ring(ffn_half, "z", *parts_b, gram_a)
    (gram_b,) = teacher_chunk(
        place, states, q_tables, (scale, keys, values), spread_member, tally, parts_b, 4, False, list_len
    )
    line = jnp.arange(1024, dtype=jnp.int32)
    rel, e, d8, z_to = line // 256, line // 128 % 2, line // 16 % 8, line // 4 % 4
    order = jnp.where(rel == 0, 0, jnp.where(rel == 1, 3, rel - 1))
    slot_to = (d8 * 4 + (z_to + order) % 4) * 2 + e
    dispatch = (slot_to[:, None] == jnp.repeat(slot_of, MAXP)[None, :]).astype(f32)
    counted = (jnp.arange(128)[None, None, :] == len(PAIRS)) & (spot[None, :, None] == 0)
    base = jnp.where(counted, 0.25 * passage_counts.astype(f32)[:, None, None], 0.0)
    send = pack(gram_a, gram_b, base.reshape(lists * MAXP, 128), dispatch)
    ffn_mine = stack_slots(after(ffn_ring, send))
    ffn_other = shift(ffn_mine, "core", 1)
    turned, grams = hidden_parts(rows_mine, rows_other, ffn_mine, ffn_other)

    got = lax.all_to_all(send, ALL, split_axis=0, concat_axis=0, tiled=True)
    got = jnp.sum(got.reshape(32, 4, 128), axis=1)
    got = got.reshape(2, 16, 4, 2, 16).transpose(4, 0, 2, 1, 3).reshape(16, 2, 4 * per)
    got = jnp.where(core == 0, got, got[:, ::-1]).reshape(16, 8 * per)

    back, grad_down, losses = pull_back(z_at, got, grams, turned, active)
    cut = lambda grad: grad.reshape(2, 4, *grad.shape[1:])
    slot_losses = losses[0].reshape(2, 4, 4, 4, 2)
    slot_losses = lax.dynamic_index_in_dim(slot_losses, z, 3, keepdims=False)
    slot_losses = jnp.where(core == 0, slot_losses, slot_losses[::-1])
    slot_losses = slot_losses.transpose(0, 2, 1, 3).reshape(8, 8)
    owners = (yh * 4 + x) * 4 + (z + jnp.array(AROUND)) % 4
    lanes = (owners[:, None] * 2 + jnp.arange(2)[None, :]).reshape(8)
    lane = jnp.arange(w_gate.shape[1], dtype=jnp.int32)
    spots = (lanes[:, None] == lane[None, :]).astype(f32)
    laid = jnp.sum(slot_losses[:, :, None] * spots[None], axis=1)
    terms, left = [], laid
    for _ in range(3):
        terms.append(left.astype(bf16))
        left = left - terms[-1].astype(f32)
    zeros = jnp.zeros((8, 13, lane.shape[0]), bf16)
    loss_rows = jnp.concatenate([jnp.stack(terms, axis=1), zeros], axis=1)
    down_terms = send_x(cut(grad_down), x)
    gate_in, up_in = inner_grads(w_down, back, gate_slope, up_slope)
    (up_in,) = after((up_in,), down_terms[3])
    grad_up = weight_grad(normed_pick, up_in, loss_rows)
    up_terms = send_x(cut(grad_up), x)
    (gate_in,) = after((gate_in,), grad_up)
    grad_gate = weight_grad(normed_pick, gate_in)
    gate_y = scatter_y(cut(grad_gate), yh).astype(bf16)
    down_sum = scatter_y(add_up(down_terms).astype(bf16), yh, gate_y)
    up_sum = scatter_y(add_up(up_terms).astype(bf16), yh, gate_y)
    gate_sum = add_up(send_x(gate_y[None], x))[0]

    returned = jnp.sum(up_sum[-16:, :slots], axis=0)
    list_loss = jnp.sum(select * returned[:, None], axis=0)
    return (list_loss, gate_sum, up_sum[:-16], down_sum.T)


def solution(mesh):
    fine = Mesh(mesh.devices.reshape(tuple(SIZES.values())), tuple(SIZES))
    placed = (
        P(DP, TP),
        P(),
        P(DP, TP),
        P(DP, TP),
        P(DP, TP),
        P(),
        P(),
        P(DP, None),
        P(DP),
        P(DP, None),
        P(DP, None),
        P(DP, None, None),
        P(),
        P(None, TP),
        P(None, TP),
        P(TP, None),
    )
    return jax.shard_map(
        shards,
        mesh=fine,
        in_specs=placed,
        out_specs=(P(DP), P(DP, TP), P(DP, TP), P(TP, DP)),
        check_vma=False,
    )
```

```python
import functools
import math

import jax
import jax.numpy as jnp
from jax import lax
from jax.experimental import pallas as pl
from jax.experimental.pallas import tpu as pltpu
from jax.sharding import Mesh
from jax.sharding import PartitionSpec as P

HQ = 32
HEAD = 128
MAXP = 4
EPSILON = 1e-06
ROPE_BASE = 1000000.0
DP = ("yh", "x", "z")
TP = ("yl", "core")
ALL = DP + TP
SIZES = {"yh": 2, "x": 4, "z": 4, "yl": 2, "core": 2}
PAIRS = [(i, j) for i in range(MAXP) for j in range(i, MAXP)]
FIRST = 80
CHUNK = 768
TOKENS_STEP = 512
AROUND = (0, 3, 1, 2)
bf16 = jnp.bfloat16
f32 = jnp.float32


def shift(value, axis, by):
    n = SIZES[axis]
    return lax.ppermute(value, axis, [(i, (i + by) % n) for i in range(n)])


def after(values, *deps):
    return lax.optimization_barrier((tuple(values), tuple(deps)))[0]


def ring_halves(block, axis, *deps):
    (block,) = after((block,), *deps)
    left, right = shift(block, axis, 1), shift(block, axis, -1)
    half = block.shape[0] // 2
    return block, left, right, shift(left[:half], axis, 1), shift(right[half:], axis, -1)


def ring(block, axis, *deps):
    (block,) = after((block,), *deps)
    return block, shift(block, axis, 1), shift(block, axis, -1), shift(block, axis, 2)


def two_rings(along_x, along_z, *deps, last=()):
    x0, z0 = after((along_x, along_z), *deps)
    (z_last,) = after((z0,), *last) if last else (z0,)
    x3, z3 = shift(x0, "x", 2), shift(z_last, "z", 2)
    x2, x1 = shift(x0, "x", -1), shift(x0, "x", 1)
    z2, z1 = shift(z0, "z", -1), shift(z0, "z", 1)
    return (x0, x1, x2, x3), (z0, z1, z2, z3)


def stack_kernel(moves, cuts, *refs):
    sources, outs = refs[: -len(cuts)], refs[-len(cuts) :]
    for i, at, n, to in moves:
        for out, (low, high) in zip(outs, cuts):
            out[to : to + n, :] = sources[i][at : at + n, low:high]


def stack(arrays, moves, cuts=None):
    rows, columns = sum(m[2] for m in moves), arrays[0].shape[1]
    cuts = cuts or [(0, columns)]
    return pl.pallas_call(
        functools.partial(stack_kernel, moves, cuts),
        in_specs=[pl.BlockSpec(memory_space=pltpu.VMEM)] * len(arrays),
        out_specs=[pl.BlockSpec(memory_space=pltpu.VMEM)] * len(cuts),
        out_shape=[jax.ShapeDtypeStruct((rows, c[1] - c[0]), arrays[0].dtype) for c in cuts],
        compiler_params=pltpu.CompilerParams(vmem_limit_bytes=24 * 1024 * 1024),
        cost_estimate=pl.CostEstimate(
            flops=0, bytes_accessed=4 * rows * columns, transcendentals=0
        ),
    )(*arrays)


def stack_ring(blocks, cut):
    n, columns = blocks[0].shape
    return stack(blocks, [(k, 0, n, k * n) for k in range(4)], [(0, cut), (cut, columns)])


def stack_slots(blocks):
    n = blocks[0].shape[0] // MAXP
    whole = 4 if len(blocks) == 4 else 3
    moves = [(k, p * n, n, (p * 4 + k) * n) for k in range(whole) for p in range(MAXP)]
    if whole == 3:
        moves += [(3 + p // 2, p % 2 * n, n, (p * 4 + 3) * n) for p in range(MAXP)]
    return stack(blocks, moves)[0]


def head_tables(gain, tokens, list_len):
    half = HEAD // 2
    positions = (jnp.arange(tokens, dtype=jnp.int32) % list_len).astype(f32)
    exponent = jnp.arange(half, dtype=f32) * (-2.0 / HEAD)
    angles = positions[:, None] * jnp.power(ROPE_BASE, exponent)[None, :]
    cosines, sines = jnp.cos(angles), jnp.sin(angles)
    same = jnp.concatenate([cosines, cosines], axis=1) * gain[None, :]
    crossed = jnp.concatenate([-sines, sines], axis=1) * jnp.roll(gain, half)[None, :]
    return same, crossed


def norm_rotate(values, same, crossed):
    mean = jnp.mean(values * values, axis=-1, keepdims=True)
    scaled = values * lax.rsqrt(mean + EPSILON)
    return (scaled * same + pltpu.roll(scaled, HEAD // 2, 1) * crossed).astype(bf16)


def teacher_kernel(heads, with_keys, list_len, *refs):
    place, states, q_same, q_cross = refs[:4]
    rest = refs[4:]
    if with_keys:
        k_same, k_cross = rest[:2]
        rest = rest[2:]
    else:
        scale_in, k_in, v_in = rest[:3]
        rest = rest[3:]
    member, tally = rest[:2]
    pieces = rest[2:10]
    rest = rest[10:]
    if with_keys:
        gram, scale_out, k_out, v_out, weights, sems = rest
    else:
        gram, weights, sems = rest

    @pl.when(pl.program_id(0) == 0)
    def _():
        yh, xx, zz = place[0], place[1], place[2]
        copies = []
        for part in range(2):
            base = part * FIRST
            for far in range(4):
                for near in range(4):
                    for h in range(2):
                        source = part * 4 + far
                        row = (near * 2 + h) * FIRST
                        rel_x, rel_z = (far, near) if part == 0 else (near, far)
                        x_at = lax.rem(xx + AROUND[rel_x], 4)
                        z_at = lax.rem(zz + AROUND[rel_z], 4)
                        y_at = lax.rem(yh + h, 2)
                        to = ((y_at * 4 + x_at) * 4 + z_at) * (2 * FIRST) + base
                        copies.append(
                            pltpu.make_async_copy(
                                pieces[source].at[pl.ds(row, FIRST), :],
                                weights.at[pl.ds(pl.multiple_of(to, 16), FIRST), :],
                                sems.at[len(copies)],
                            )
                        )
        for copy in copies:
            copy.start()
        for copy in copies:
            copy.wait()

    groups, _, width = states.shape
    total, squares = None, None
    for k in range(groups):
        piece = states[k]
        term = jnp.dot(
            piece, weights[k * width : (k + 1) * width, :], preferred_element_type=f32
        )
        total = term if total is None else total + term
        if with_keys:
            wide = piece.astype(f32)
            more = jnp.sum(wide * wide, axis=1, keepdims=True)
            squares = more if squares is None else squares + more
    if with_keys:
        scale = lax.rsqrt(squares / (groups * width) + EPSILON)
        scale_out[...] = scale
    else:
        scale = scale_in[...]
    total = total * scale
    if with_keys:
        keys = norm_rotate(total[:, :HEAD], k_same[...], k_cross[...])
        values = total[:, HEAD : 2 * HEAD].astype(bf16)
        k_out[...] = keys
        v_out[...] = values
        first = 2 * HEAD
    else:
        keys, values, first = k_in[...], v_in[...], 0
    tokens = total.shape[0]
    block = 128
    row = lax.broadcasted_iota(jnp.int32, (block, block), 0)
    col = lax.broadcasted_iota(jnp.int32, (block, block), 1)
    allowed = (col <= row) & (col // list_len == row // list_len)
    hide = jnp.where(allowed, 0.0, -1e30)
    ones = jnp.ones((block, HEAD), bf16)
    queries = [
        norm_rotate(total[:, first + h * HEAD : first + (h + 1) * HEAD], q_same[...], q_cross[...])
        for h in range(heads)
    ]
    mixed = []
    for s in range(tokens // block):
        part = slice(s * block, (s + 1) * block)
        stacked = jnp.concatenate([q[part] for q in queries], axis=0)
        scores = lax.dot_general(
            stacked, keys[part], (((1,), (1,)), ((), ())), preferred_element_type=f32
        )
        scores = scores.reshape(heads, block, block) * (1.0 / math.sqrt(HEAD)) + hide[None]
        shifted = jnp.exp(scores - jnp.max(scores, axis=-1, keepdims=True)).astype(bf16)
        summed = jnp.dot(
            shifted.reshape(heads * block, block),
            jnp.concatenate([values[part], ones], axis=1),
            preferred_element_type=f32,
        )
        result = (summed[:, :HEAD] / summed[:, HEAD:]).astype(bf16)
        mixed.append(
            jnp.concatenate([result[h * block : (h + 1) * block] for h in range(heads)], axis=1)
        )
    attended = jnp.concatenate(mixed, axis=0)
    pooled = jnp.dot(member[...], attended, preferred_element_type=f32)
    pooled = (pooled / tally[...]).astype(bf16)
    gram[0] = lax.dot_general(
        pooled, pooled, (((1,), (1,)), ((), ())), preferred_element_type=f32
    )


def teacher_chunk(place, states, q_tables, extra, member, tally, parts, heads, with_keys, list_len, span=None):
    groups, tokens, width = states.shape
    step = TOKENS_STEP
    first, steps = span or (0, tokens // step)
    tokens = steps * step
    lists = step // list_len
    rows = lists * MAXP
    columns = parts[0].shape[1]
    pieces = list(parts)
    block = lambda n, m: pl.BlockSpec((n, m), lambda g: (g, 0))
    later = lambda n, m: pl.BlockSpec((n, m), lambda g: (g + first, 0))
    fixed = lambda n, m: pl.BlockSpec((n, m), lambda g: (0, 0))
    extra_specs = [fixed(step, HEAD)] * 2
    if not with_keys:
        extra_specs = [block(step, 1)] + [block(step, HEAD)] * 2
    outs = [jax.ShapeDtypeStruct((tokens // step, rows, rows), f32)]
    out_specs = [pl.BlockSpec((1, rows, rows), lambda g: (g, 0, 0))]
    if with_keys:
        outs += [jax.ShapeDtypeStruct((tokens, 1), f32)]
        outs += [jax.ShapeDtypeStruct((tokens, HEAD), bf16)] * 2
        out_specs += [block(step, 1)] + [block(step, HEAD)] * 2
    depth = groups * width
    return pl.pallas_call(
        functools.partial(teacher_kernel, heads, with_keys, list_len),
        grid=(tokens // step,),
        in_specs=[
            pl.BlockSpec(memory_space=pltpu.SMEM),
            pl.BlockSpec((groups, step, width), lambda g: (0, g + first, 0)),
        ]
        + [fixed(step, HEAD)] * 2
        + extra_specs
        + [later(rows, step), later(rows, 1)]
        + [pl.BlockSpec(memory_space=pltpu.HBM)] * len(pieces),
        out_specs=out_specs,
        out_shape=outs,
        scratch_shapes=[
            pltpu.VMEM((depth, columns), bf16),
            pltpu.SemaphoreType.DMA((64,)),
        ],
        compiler_params=pltpu.CompilerParams(
            dimension_semantics=("arbitrary",), vmem_limit_bytes=58 * 1024 * 1024
        ),
        cost_estimate=pl.CostEstimate(
            flops=2 * tokens * depth * columns,
            bytes_accessed=2 * depth * (tokens + columns),
            transcendentals=tokens * 128 * heads,
        ),
    )(place, states, *q_tables, *extra, member, tally, *pieces)


def rms_scale(values, weights):
    return values * lax.rsqrt(jnp.mean(values * values, axis=-1, keepdims=True) + EPSILON) * weights


def forward_kernel(count, *refs):
    z, rows, (gain, w_gate, w_up), rest = refs[0], refs[1 : 1 + count], refs[1 + count : 4 + count], refs[4 + count :]
    values = rows[0][...]
    if count == 2:
        early = pl.program_id(0) < pl.num_programs(0) // 2
        values = jnp.where(early, values, rows[1][...])
    values = values.astype(f32)
    active, scaled = rest[0], rest[-1]
    scaled[...] = rms_scale(values, gain[...]).T.astype(bf16)
    gate_pre = jnp.dot(w_gate[...], scaled[...], preferred_element_type=f32)
    up_pre = jnp.dot(w_up[...], scaled[...], preferred_element_type=f32)
    sigma = jax.nn.sigmoid(gate_pre)
    gated = gate_pre * sigma
    active[...] = (gated * up_pre).astype(bf16)
    if count == 2:
        gate_slope, up_slope, picked = rest[1:4]
        gate_slope[...] = (up_pre * sigma * (1.0 + gate_pre * (1.0 - sigma))).astype(bf16)
        up_slope[...] = gated.astype(bf16)
        pick_rows(picked, scaled, z[0], 8)


def pick_rows(picked, source, z, groups):
    own = picked.shape[0] // groups
    for k in range(groups):
        start = pl.multiple_of((k * 4 + z) * own, 16)
        picked[k * own : (k + 1) * own, :] = source[pl.ds(start, own), :]


def forward(z, rows, gain, w_gate, w_up):
    count = len(rows)
    size, width = rows[0].shape
    units = w_gate.shape[0]
    tile = 256
    middle = size // tile
    total = count * size
    whole = lambda a: pl.BlockSpec(a.shape, lambda g: (0, 0), pipeline_mode=pl.Buffered(1))
    across = lambda n: pl.BlockSpec((n, tile), lambda g: (0, g))
    outs = [units] if count == 1 else [units, units, units, width // 4]
    row_specs = [
        pl.BlockSpec((tile, width), lambda g: (jnp.minimum(g, middle - 1), 0)),
        pl.BlockSpec((tile, width), lambda g: (jnp.maximum(g - middle, 0), 0)),
    ]
    return pl.pallas_call(
        functools.partial(forward_kernel, count),
        grid=(count * middle,),
        in_specs=[pl.BlockSpec(memory_space=pltpu.SMEM)]
        + row_specs[:count]
        + [whole(gain), whole(w_gate), whole(w_up)],
        out_specs=[across(n) for n in outs],
        out_shape=[jax.ShapeDtypeStruct((n, total), bf16) for n in outs],
        scratch_shapes=[pltpu.VMEM((width, tile), bf16)],
        compiler_params=pltpu.CompilerParams(
            dimension_semantics=("arbitrary",), vmem_limit_bytes=(58 if count == 2 else 36) * 1024 * 1024
        ),
        cost_estimate=pl.CostEstimate(
            flops=4 * total * width * units,
            bytes_accessed=2 * total * width + 4 * width * units + 6 * total * units,
            transcendentals=total * units,
        ),
    )(z, *rows, gain, w_gate, w_up)


def pack_kernel(gram_a, gram_b, base, dispatch, out):
    steps, rows, _ = gram_a.shape
    row = lax.broadcasted_iota(jnp.int32, (rows, rows), 0)
    col = lax.broadcasted_iota(jnp.int32, (rows, rows), 1)
    lane = lax.broadcasted_iota(jnp.int32, (rows, 128), 1)
    same = row // MAXP == col // MAXP
    blocks = []
    for s in range(steps):
        gram = gram_a[s] + gram_b[s]
        block = base[s * rows : (s + 1) * rows, :]
        for k, (i, j) in enumerate(PAIRS):
            wanted = same & (row % MAXP == i) & (col % MAXP == j)
            value = jnp.sum(jnp.where(wanted, gram, 0.0), axis=1, keepdims=True)
            block = block + jnp.where(lane == k, value, 0.0)
        blocks.append(block)
    sent = jnp.dot(
        dispatch[...],
        jnp.concatenate(blocks, axis=0),
        precision=lax.Precision.HIGHEST,
        preferred_element_type=f32,
    )
    total = sent[:128]
    for q in range(1, 8):
        total = total + pltpu.roll(sent[q * 128 : (q + 1) * 128], 16 * q, 1)
    out[...] = total


def pack(gram_a, gram_b, base, dispatch):
    return pl.pallas_call(
        pack_kernel,
        in_specs=[pl.BlockSpec(memory_space=pltpu.VMEM)] * 4,
        out_specs=pl.BlockSpec(memory_space=pltpu.VMEM),
        out_shape=jax.ShapeDtypeStruct((128, 128), f32),
        compiler_params=pltpu.CompilerParams(vmem_limit_bytes=16 * 1024 * 1024),
        cost_estimate=pl.CostEstimate(
            flops=2 * 6 * 1024 * 128 * 128, bytes_accessed=1 << 20, transcendentals=0
        ),
    )(gram_a, gram_b, base, dispatch)


def hidden_kernel(rows_a, rows_b, ffn_a, ffn_b, turned, grams):
    @pl.when(pl.program_id(0) == 0)
    def _():
        grams[...] = jnp.zeros_like(grams)

    for c, (rows, ffn) in enumerate(((rows_a, ffn_a), (rows_b, ffn_b))):
        hidden = (rows[...].astype(f32) + ffn[...].astype(f32)).T
        size = hidden.shape[1] // MAXP
        turned[:, c * MAXP * size : (c + 1) * MAXP * size] = hidden.astype(bf16)
        cut = [hidden[:, i * size : (i + 1) * size] for i in range(MAXP)]
        for k, (i, j) in enumerate(PAIRS):
            grams[k : k + 1, c * size : (c + 1) * size] += jnp.sum(
                cut[i] * cut[j], axis=0, keepdims=True
            )


def hidden_parts(rows_a, rows_b, ffn_a, ffn_b):
    rows, width = rows_a.shape
    tile = 256
    spec = pl.BlockSpec((rows, tile), lambda g: (0, g))
    return pl.pallas_call(
        hidden_kernel,
        grid=(width // tile,),
        in_specs=[spec] * 4,
        out_specs=[
            pl.BlockSpec((tile, 2 * rows), lambda g: (g, 0)),
            pl.BlockSpec((16, 2 * rows // MAXP), lambda g: (0, 0)),
        ],
        out_shape=[
            jax.ShapeDtypeStruct((width, 2 * rows), bf16),
            jax.ShapeDtypeStruct((16, 2 * rows // MAXP), f32),
        ],
        compiler_params=pltpu.CompilerParams(
            dimension_semantics=("arbitrary",), vmem_limit_bytes=24 * 1024 * 1024
        ),
        cost_estimate=pl.CostEstimate(
            flops=24 * rows * width, bytes_accessed=12 * rows * width, transcendentals=0
        ),
    )(rows_a, rows_b, ffn_a, ffn_b)


def cosines(at, size):
    scales = [jnp.sqrt(at[i, i] / size + EPSILON) for i in range(MAXP)]
    return {(i, j): at[i, j] / (size * scales[i] * scales[j]) for i, j in PAIRS}, scales


def back_kernel(width, z, target, grams, turned, active, back, down, losses, factors, picked, held, sem):
    slots = target.shape[1]
    fetch = pltpu.make_async_copy(active, held, sem)

    @pl.when(pl.program_id(0) == 0)
    def _():
        fetch.start()

    @pl.when(pl.program_id(0) == 0)
    def _():
        row = lambda ref, k: ref[k : k + 1, :]
        wanted, _ = cosines({p: row(target, k) for k, p in enumerate(PAIRS)}, HQ * HEAD)
        have, scales = cosines({p: row(grams, k) for k, p in enumerate(PAIRS)}, width)
        count = row(target, len(PAIRS))
        alive = [jnp.where(count > i + 0.5, 1.0, 0.0) for i in range(MAXP)]
        bound = jnp.maximum(count, 1.0)
        over = 1.0 / (bound * bound)
        slope = {}
        loss = None
        for i, j in PAIRS:
            both = alive[i] * alive[j]
            differ = have[i, j] - wanted[i, j]
            slope[i, j] = slope[j, i] = 2.0 * both * differ * over
            term = (1.0 if i == j else 2.0) * both * differ * differ
            loss = term if loss is None else loss + term
        losses[...] = jnp.broadcast_to(loss * over, losses.shape)
        for i in range(MAXP):
            pull = sum(slope[i, j] * have[min(i, j), max(i, j)] for j in range(MAXP))
            for j in range(MAXP):
                term = slope[i, j] / (scales[i] * scales[j])
                if i == j:
                    term = term - pull / (scales[i] * scales[i])
                factors[i * MAXP + j : i * MAXP + j + 1, :] = 2.0 * term

    half = slots // 2
    for c in range(2):
        at = lambda i: slice((c * MAXP + i) * half, (c * MAXP + i + 1) * half)
        cut = [turned[:, at(i)].astype(f32) for i in range(MAXP)]
        for i in range(MAXP):
            mixed = None
            for j in range(MAXP):
                k = i * MAXP + j
                term = factors[k : k + 1, c * half : (c + 1) * half] * cut[j]
                mixed = term if mixed is None else mixed + term
            back[:, at(i)] = mixed.astype(bf16)
    step = pl.program_id(0)
    own = down.shape[1]
    group = back.shape[0] // 2
    for k in range(2):
        start = pl.multiple_of(k * group + z[0] * own, 16)
        to = pl.multiple_of((step * 2 + k) * own, 16)
        picked[pl.ds(to, own), :] = back[pl.ds(start, own), :]

    @pl.when(step == pl.num_programs(0) - 1)
    def _():
        fetch.wait()
        product = lax.dot_general(
            picked[...], held[...], (((1,), (1,)), ((), ())), preferred_element_type=f32
        ).astype(bf16)
        for k in range(down.shape[0]):
            down[k] = product[k * own : (k + 1) * own]


def pull_back(z, target, grams, turned, active):
    width, rows = turned.shape
    units = active.shape[0]
    own = width // 32
    tile = width // 4
    fixed = pl.BlockSpec(target.shape, lambda g: (0, 0))
    moving = lambda n: pl.BlockSpec((n, rows), lambda g: (g, 0))
    return pl.pallas_call(
        functools.partial(back_kernel, width),
        grid=(4,),
        in_specs=[
            pl.BlockSpec(memory_space=pltpu.SMEM),
            fixed,
            fixed,
            moving(tile),
            pl.BlockSpec(memory_space=pltpu.HBM),
        ],
        out_specs=[
            moving(tile),
            pl.BlockSpec((8, own, units), lambda g: (0, 0, 0)),
            pl.BlockSpec((8, target.shape[1]), lambda g: (0, 0)),
        ],
        out_shape=[
            jax.ShapeDtypeStruct((width, rows), bf16),
            jax.ShapeDtypeStruct((8, own, units), bf16),
            jax.ShapeDtypeStruct((8, target.shape[1]), f32),
        ],
        scratch_shapes=[
            pltpu.VMEM(target.shape, f32),
            pltpu.VMEM((8 * own, rows), bf16),
            pltpu.VMEM((units, rows), bf16),
            pltpu.SemaphoreType.DMA,
        ],
        compiler_params=pltpu.CompilerParams(
            dimension_semantics=("arbitrary",), vmem_limit_bytes=32 * 1024 * 1024
        ),
        cost_estimate=pl.CostEstimate(
            flops=8 * rows * width + 16 * own * rows * units, bytes_accessed=5 * rows * width, transcendentals=0
        ),
    )(z, target, grams, turned, active)


def inner_kernel(w_down, back, gate_slope, up_slope, gate_in, up_in):
    total = jnp.dot(w_down[...], back[...], preferred_element_type=f32)
    gate_in[...] = (total * gate_slope[...].astype(f32)).astype(bf16)
    up_in[...] = (total * up_slope[...].astype(f32)).astype(bf16)


def inner_grads(w_down, back, gate_slope, up_slope):
    units, width = w_down.shape
    rows = back.shape[1]
    tile = 256
    across = lambda n: pl.BlockSpec((n, tile), lambda g: (0, g))
    return pl.pallas_call(
        inner_kernel,
        grid=(rows // tile,),
        in_specs=[
            pl.BlockSpec(w_down.shape, lambda g: (0, 0), pipeline_mode=pl.Buffered(1)),
            across(width),
            across(units),
            across(units),
        ],
        out_specs=[across(units)] * 2,
        out_shape=[jax.ShapeDtypeStruct((units, rows), bf16)] * 2,
        compiler_params=pltpu.CompilerParams(
            dimension_semantics=("arbitrary",), vmem_limit_bytes=58 * 1024 * 1024
        ),
        cost_estimate=pl.CostEstimate(
            flops=2 * rows * width * units,
            bytes_accessed=2 * (rows * width + units * width + 4 * rows * units),
            transcendentals=0,
        ),
    )(w_down, back, gate_slope, up_slope)


def grad_kernel(picked, inner, *refs):
    out = refs[-1]
    product = lax.dot_general(
        picked[...], inner[...], (((1,), (1,)), ((), ())), preferred_element_type=f32
    ).astype(bf16)
    own = picked.shape[0] // out.shape[0]
    for k in range(out.shape[0]):
        out[k, :own] = product[k * own : (k + 1) * own]
        if len(refs) == 2:
            out[k, own:] = refs[0][k]


def weight_grad(picked, inner, *more):
    features, rows = picked.shape
    units = inner.shape[0]
    size = features // 8 + sum(a.shape[1] for a in more)
    return pl.pallas_call(
        grad_kernel,
        in_specs=[pl.BlockSpec(memory_space=pltpu.VMEM)] * (2 + len(more)),
        out_specs=pl.BlockSpec(memory_space=pltpu.VMEM),
        out_shape=jax.ShapeDtypeStruct((8, size, units), bf16),
        compiler_params=pltpu.CompilerParams(vmem_limit_bytes=32 * 1024 * 1024),
        cost_estimate=pl.CostEstimate(
            flops=2 * features * rows * units,
            bytes_accessed=2 * (features * rows + units * rows + features * units),
            transcendentals=0,
        ),
    )(picked, inner, *more)


def send_x(blocks, x):
    own = lax.dynamic_index_in_dim(blocks, x, 1, keepdims=False)
    outs = [lax.dynamic_index_in_dim(blocks, lax.rem(x + by, 4), 1, keepdims=False) for by in range(1, 4)]
    return (own, *(shift(out, "x", by + 1) for by, out in enumerate(outs)))


def add_up(terms):
    total = terms[0].astype(f32)
    for term in terms[1:]:
        total = total + term.astype(f32)
    return total


def scatter_y(blocks, yh, *deps):
    mine = lax.dynamic_index_in_dim(blocks, yh, 0, keepdims=False)
    out = lax.dynamic_index_in_dim(blocks, 1 - yh, 0, keepdims=False)
    came = shift(out, "yh", 1)
    if deps:
        (came,) = after((came,), *deps)
    return mine.astype(f32) + came.astype(f32)


def shards(
    teacher_states,
    teacher_gain,
    w_query,
    key_weight,
    value_weight,
    query_gain,
    key_gain,
    segments,
    passage_counts,
    swap_order,
    list_owner,
    student_rows,
    student_gain,
    w_gate,
    w_up,
    w_down,
):
    yh, x, z, yl, core = (lax.axis_index(a) for a in ALL)
    dp = (yh * 4 + x) * 4 + z
    lists, list_len = segments.shape
    slots = student_rows.shape[0]
    width = student_rows.shape[2]

    halves = jnp.swapaxes(student_rows.reshape(2, slots // 2, MAXP, width), 1, 2)
    own_rows = halves.reshape(slots * MAXP, width)
    half = own_rows.shape[0] // 2
    rows_half = lax.dynamic_slice_in_dim(own_rows, core * half, half, 0)
    rows_ring = ring_halves(rows_half, "z")

    depth = w_query.shape[0]
    row_gain = lax.dynamic_slice_in_dim(teacher_gain, dp * depth, depth, 0).astype(f32)[:, None]
    weights = jnp.concatenate([key_weight, value_weight, w_query], axis=1)
    weights = (weights.astype(f32) * row_gain).astype(bf16)
    across_y = shift(weights, "yh", 1)
    states = lax.all_gather(teacher_states, TP, axis=0, tiled=False)
    one = jnp.concatenate([weights[:FIRST], across_y[:FIRST]], axis=0)
    two = jnp.concatenate([weights[FIRST:], across_y[FIRST:]], axis=0)

    gain = student_gain.astype(f32)[None, :]
    z_at = z[None].astype(jnp.int32)
    (active_own,) = forward(z_at, (own_rows,), gain, w_gate.T, w_up.T)

    partial = lax.dot_general(
        active_own, w_down, (((0,), (0,)), ((), ())), preferred_element_type=f32
    ).astype(bf16)
    kept = lax.dynamic_slice_in_dim(partial, core * half, half, 0).astype(f32)
    given = lax.dynamic_slice_in_dim(partial, (1 - core) * half, half, 0)
    pair_sum = (kept + shift(given, "core", 1).astype(f32)).astype(bf16)
    two_ring, one_ring = two_rings(two, one, *rows_ring[3:], pair_sum)

    spot = jnp.arange(MAXP, dtype=jnp.int32)
    live = spot[None, :] < passage_counts[:, None]
    member = (segments[:, None, :] == swap_order[:, :, None]) & live[:, :, None]
    tally = jnp.maximum(jnp.sum(member.astype(f32), axis=2), 1.0).reshape(lists * MAXP, 1)
    group = TOKENS_STEP // list_len
    same_list = jnp.eye(group, dtype=bool)
    spread_member = (
        member.reshape(lists // group, group, MAXP, 1, list_len)
        & same_list[None, :, None, :, None]
    )
    spread_member = spread_member.reshape(lists * MAXP, TOKENS_STEP).astype(bf16)

    line_z = stack_ring(one_ring, CHUNK)
    line_x = stack_ring(two_ring, CHUNK)
    rows_mine = stack_slots(after(rows_ring, line_z[1], line_x[1], spread_member, tally))
    rows_other = shift(rows_mine, "core", 1)

    def spread(k, *before, last=()):
        rings = two_rings(line_z[k], line_x[k], *before, last=last)
        return (*rings[0], *rings[1])

    ffn_half = lax.psum(pair_sum, "yl")
    parts_a = spread(0, line_x[0], line_z[0], rows_other)

    active, gate_slope, up_slope, normed_pick = forward(
        z_at, (rows_mine, rows_other), gain, w_gate.T, w_up.T
    )

    owner = list_owner[:, 0]
    index = jnp.arange(lists, dtype=jnp.int32)
    earlier = jnp.sum(
        ((owner[None, :] == owner[:, None]) & (index[None, :] < index[:, None])).astype(jnp.int32),
        axis=1,
    )
    slot_of = owner * 2 + earlier
    select = (jnp.arange(slots, dtype=jnp.int32)[:, None] == slot_of[None, :]).astype(f32)
    per = slots // 2

    place = jnp.stack([yh, x, z]).astype(jnp.int32)
    q_tables = head_tables(query_gain, TOKENS_STEP, list_len)
    k_tables = head_tables(key_gain, TOKENS_STEP, list_len)
    gram_a, scale, keys, values = teacher_chunk(
        place, states, q_tables, k_tables, spread_member, tally, parts_a, 4, True, list_len
    )
    parts_b = spread(1, *parts_a, active, last=(gram_a,))
    ffn_ring = ring(ffn_half, "z", *parts_b, gram_a)
    (gram_b,) = teacher_chunk(
        place, states, q_tables, (scale, keys, values), spread_member, tally, parts_b, 4, False, list_len
    )
    line = jnp.arange(1024, dtype=jnp.int32)
    rel, e, d8, z_to = line // 256, line // 128 % 2, line // 16 % 8, line // 4 % 4
    order = jnp.where(rel == 0, 0, jnp.where(rel == 1, 3, rel - 1))
    slot_to = (d8 * 4 + (z_to + order) % 4) * 2 + e
    dispatch = (slot_to[:, None] == jnp.repeat(slot_of, MAXP)[None, :]).astype(f32)
    counted = (jnp.arange(128)[None, None, :] == len(PAIRS)) & (spot[None, :, None] == 0)
    base = jnp.where(counted, 0.25 * passage_counts.astype(f32)[:, None, None], 0.0)
    send = pack(gram_a, gram_b, base.reshape(lists * MAXP, 128), dispatch)
    ffn_mine = stack_slots(after(ffn_ring, send))
    ffn_other = shift(ffn_mine, "core", 1)
    turned, grams = hidden_parts(rows_mine, rows_other, ffn_mine, ffn_other)

    got = lax.all_to_all(send, ALL, split_axis=0, concat_axis=0, tiled=True)
    got = jnp.sum(got.reshape(32, 4, 128), axis=1)
    got = got.reshape(2, 16, 4, 2, 16).transpose(4, 0, 2, 1, 3).reshape(16, 2, 4 * per)
    got = jnp.where(core == 0, got, got[:, ::-1]).reshape(16, 8 * per)

    back, grad_down, losses = pull_back(z_at, got, grams, turned, active)
    cut = lambda grad: grad.reshape(2, 4, *grad.shape[1:])
    slot_losses = losses[0].reshape(2, 4, 4, 4, 2)
    slot_losses = lax.dynamic_index_in_dim(slot_losses, z, 3, keepdims=False)
    slot_losses = jnp.where(core == 0, slot_losses, slot_losses[::-1])
    slot_losses = slot_losses.transpose(0, 2, 1, 3).reshape(8, 8)
    owners = (yh * 4 + x) * 4 + (z + jnp.array(AROUND)) % 4
    lanes = (owners[:, None] * 2 + jnp.arange(2)[None, :]).reshape(8)
    lane = jnp.arange(w_gate.shape[1], dtype=jnp.int32)
    spots = (lanes[:, None] == lane[None, :]).astype(f32)
    laid = jnp.sum(slot_losses[:, :, None] * spots[None], axis=1)
    terms, left = [], laid
    for _ in range(3):
        terms.append(left.astype(bf16))
        left = left - terms[-1].astype(f32)
    zeros = jnp.zeros((8, 13, lane.shape[0]), bf16)
    loss_rows = jnp.concatenate([jnp.stack(terms, axis=1), zeros], axis=1)
    down_terms = send_x(cut(grad_down), x)
    gate_in, up_in = inner_grads(w_down, back, gate_slope, up_slope)
    (up_in,) = after((up_in,), down_terms[3])
    grad_up = weight_grad(normed_pick, up_in, loss_rows)
    up_terms = send_x(cut(grad_up), x)
    (gate_in,) = after((gate_in,), grad_up)
    grad_gate = weight_grad(normed_pick, gate_in)
    gate_y = scatter_y(cut(grad_gate), yh).astype(bf16)
    down_sum = scatter_y(add_up(down_terms).astype(bf16), yh, gate_y)
    up_sum = scatter_y(add_up(up_terms).astype(bf16), yh, gate_y)
    gate_sum = add_up(send_x(gate_y[None], x))[0]

    returned = jnp.sum(up_sum[-16:, :slots], axis=0)
    list_loss = jnp.sum(select * returned[:, None], axis=0)
    return (list_loss, gate_sum, up_sum[:-16], down_sum.T)


def solution(mesh):
    fine = Mesh(mesh.devices.reshape(tuple(SIZES.values())), tuple(SIZES))
    placed = (
        P(DP, TP),
        P(),
        P(DP, TP),
        P(DP, TP),
        P(DP, TP),
        P(),
        P(),
        P(DP, None),
        P(DP),
        P(DP, None),
        P(DP, None),
        P(DP, None, None),
        P(),
        P(None, TP),
        P(None, TP),
        P(TP, None),
    )
    return jax.shard_map(
        shards,
        mesh=fine,
        in_specs=placed,
        out_specs=(P(DP), P(DP, TP), P(DP, TP), P(TP, DP)),
        check_vma=False,
    )
```
